512 devices in a mesh: beam: 64 (over z, x), trans: 8 (over y, core).
Axes of the slice: x: 4, y: 4, z: 16, core: 2. Of those that a mesh axis runs over, the one named last changes fastest.
Arguments:
- packets: float32 [2, 64, 4096, 128], P(None, 'trans', 'beam'), may hold values from -60 to 60
- kinetic_x: float32 [64, 64], replicated, as said below
- kinetic_y: float32 [64, 64], replicated, as said below
- element_kinetic: float32 [65, 65], replicated, as said below
- potential: float32 [64, 4096, 128], P('trans', 'beam'), may hold values from -0.4 to 0.4, as said below
Outputs:
- basis: float32 [10, 64, 4096, 128], P(None, 'trans', 'beam')
- rfactor: float32 [2, 10, 10], replicated
The draws below stay inside these ranges and needn't reach their ends.
Inputs may be any that keep to these rules, and one draw needn't show every extreme that they name: kinetic_x is symmetric. kinetic_y is symmetric. element_kinetic is symmetric. `potential`: the absorbing part (the last 64 entries of each row) is not negative.
All inputs are finite; a program needn't handle non-finite values.
Results may differ from the reference program's by a relative error of at most 0.00075.
Values sent between devices are 32-bit elements; how exact they have to be, the bound alone decides.
No kernel may reach another device: no remote copies, remote signals or barrier semaphores. Data moves between devices by JAX's collectives and lax.ppermute only.
A program may use at most 64 MiB of HBM per device.

```python
import jax
import jax.numpy as jnp
from jax import lax

X = 64
Y = 64
ELEM = 64
POWERS = 4
PACKETS = 2
NCOL = 10
Z = 4096


def symmetric_matrix(key, order, scale):
    raw = jax.random.normal(key, (order, order), jnp.float32)
    return (raw + raw.T) * (scale * 0.70710678)


def draw_packets(key, part):
    beam_pos = jnp.arange(Z, dtype=jnp.float32) / float(max(Z - 1, 1))
    values = jnp.clip(jax.random.normal(key, (PACKETS, X, Z, 2 * Y), jnp.float32), -6.0, 6.0)
    envelope = jnp.power(3.0, beam_pos)
    return values * envelope[None, None, :, None]


def draw_kinetic_x(key, part):
    return symmetric_matrix(jax.random.fold_in(key, 11), X, 0.025)


def draw_kinetic_y(key, part):
    return symmetric_matrix(jax.random.fold_in(key, 12), Y, 0.025)


def draw_element_kinetic(key, part):
    return symmetric_matrix(jax.random.fold_in(key, 13), ELEM + 1, 0.02)


def draw_potential(key, part):
    key_real = jax.random.fold_in(key, 21)
    key_abs = jax.random.fold_in(key, 22)
    real_part = jax.random.uniform(key_real, (X, Z, Y), jnp.float32, -0.4, 0.4)
    abs_part = jax.random.uniform(key_abs, (X, Z, Y), jnp.float32, 0.0, 0.3)
    return jnp.concatenate([real_part, abs_part], axis=-1)


def setup_inputs(seed: int = 0) -> dict:
    keys = jax.random.split(jax.random.key(seed), 6)
    return {
        "packets": draw_packets(jax.random.fold_in(keys[5], 71), 0),
        "kinetic_x": draw_kinetic_x(jax.random.fold_in(keys[5], 71), 0),
        "kinetic_y": draw_kinetic_y(jax.random.fold_in(keys[5], 71), 0),
        "element_kinetic": draw_element_kinetic(jax.random.fold_in(keys[5], 71), 0),
        "potential": draw_potential(jax.random.fold_in(keys[5], 71), 0),
    }


def rotate_half(vectors):
    half_width = vectors.shape[-1] // 2
    return jnp.concatenate([-vectors[..., half_width:], vectors[..., :half_width]], axis=-1)

def apply_ham(vectors, kinetic_x, kinetic_y, element_kinetic, potential):
    precise = lax.Precision.HIGHEST
    npack, rows_x, rows_z, width = vectors.shape
    half_width = width // 2
    along_x = jnp.einsum('ab,pbzc->pazc', kinetic_x, vectors, precision=precise)
    doubled = jnp.kron(jnp.eye(2, dtype=kinetic_y.dtype), kinetic_y)
    along_y = jnp.einsum('pxzv,wv->pxzw', vectors, doubled, precision=precise)
    elem_len = element_kinetic.shape[0] - 1
    elements = rows_z // elem_len
    interior = vectors.reshape(npack, rows_x, elements, elem_len, width)
    following = jnp.concatenate([interior[:, :, 1:, 0:1], jnp.zeros((npack, rows_x, 1, 1, width), jnp.float32)], axis=2)
    blocks = jnp.concatenate([interior, following], axis=3)
    result = jnp.einsum('ij,pxejc->pxeic', element_kinetic, blocks, precision=precise)
    carried = jnp.concatenate([jnp.zeros((npack, rows_x, 1, width), jnp.float32), result[:, :, :-1, elem_len]], axis=2)
    along_z = result[:, :, :, :elem_len].at[:, :, :, 0].add(carried).reshape(vectors.shape)
    real_part = vectors[..., :half_width]
    imag_part = vectors[..., half_width:]
    pot_real = potential[..., :half_width][None]
    pot_abs = potential[..., half_width:][None]
    optical = jnp.concatenate([pot_real * real_part + pot_abs * imag_part, pot_real * imag_part - pot_abs * real_part], axis=-1)
    return along_x + along_y + along_z + optical

def gram_matrix(columns, turned):
    precise = lax.Precision.HIGHEST
    ncols = columns.shape[0]
    flat = columns.reshape(ncols, -1)
    flat_turned = turned.reshape(ncols, -1)
    gram_re = jnp.dot(flat, flat.T, precision=precise)
    gram_im = -jnp.dot(flat, flat_turned.T, precision=precise)
    return (gram_re, gram_im)

def cholesky_upper(gram_re, gram_im):
    precise = lax.Precision.HIGHEST
    ncols = gram_re.shape[0]
    upper_re = jnp.zeros((ncols, ncols), jnp.float32)
    upper_im = jnp.zeros((ncols, ncols), jnp.float32)
    places = jnp.arange(ncols)
    for j in range(ncols):
        above_re = upper_re[:j, j]
        above_im = upper_im[:j, j]
        row_re = gram_re[j] - jnp.dot(above_re, upper_re[:j], precision=precise) - jnp.dot(above_im, upper_im[:j], precision=precise)
        row_im = gram_im[j] - jnp.dot(above_re, upper_im[:j], precision=precise) + jnp.dot(above_im, upper_re[:j], precision=precise)
        pivot = jnp.sqrt(row_re[j])
        upper_re = upper_re.at[j].set(jnp.where(places > j, row_re / pivot, jnp.where(places == j, pivot, 0.0)))
        upper_im = upper_im.at[j].set(jnp.where(places > j, row_im / pivot, 0.0))
    return (upper_re, upper_im)

def upper_inverse(upper_re, upper_im):
    precise = lax.Precision.HIGHEST
    ncols = upper_re.shape[0]
    inv_re = jnp.zeros((ncols, ncols), jnp.float32)
    inv_im = jnp.zeros((ncols, ncols), jnp.float32)
    places = jnp.arange(ncols)
    for j in range(ncols):
        col_re = jnp.where(places == j, 1.0, 0.0).astype(jnp.float32)
        col_im = jnp.zeros((ncols,), jnp.float32)
        if j > 0:
            col_re = col_re - jnp.dot(inv_re[:, :j], upper_re[:j, j], precision=precise) + jnp.dot(inv_im[:, :j], upper_im[:j, j], precision=precise)
            col_im = col_im - jnp.dot(inv_re[:, :j], upper_im[:j, j], precision=precise) - jnp.dot(inv_im[:, :j], upper_re[:j, j], precision=precise)
        inv_re = inv_re.at[:, j].set(col_re / upper_re[j, j])
        inv_im = inv_im.at[:, j].set(col_im / upper_re[j, j])
    return (inv_re, inv_im)

def solve_basis(columns, turned, upper_re, upper_im):
    precise = lax.Precision.HIGHEST
    inv_re, inv_im = upper_inverse(upper_re, upper_im)
    return jnp.tensordot(inv_re.T, columns, axes=1, precision=precise) + jnp.tensordot(inv_im.T, turned, axes=1, precision=precise)

def reference(packets, kinetic_x, kinetic_y, element_kinetic, potential):
    columns = [packets]
    earlier = packets
    current = apply_ham(packets, kinetic_x, kinetic_y, element_kinetic, potential)
    columns.append(current)
    for k in range(POWERS - 1):
        upcoming = 2.0 * apply_ham(current, kinetic_x, kinetic_y, element_kinetic, potential) - earlier
        earlier = current
        current = upcoming
        columns.append(current)
    stacked = jnp.stack(columns, axis=1)
    stacked = stacked.reshape((NCOL,) + packets.shape[1:])
    turned = rotate_half(stacked)
    cells = float(X * Y * Z)
    gram_re, gram_im = gram_matrix(stacked, turned)
    upper_re, upper_im = cholesky_upper(gram_re / cells, gram_im / cells)
    basis = solve_basis(stacked, turned, upper_re, upper_im)
    return (basis, jnp.stack([upper_re, upper_im]))
```

```python
import functools

import jax
import jax.numpy as jnp
from jax import lax
from jax.experimental import pallas as pl
from jax.experimental.pallas import tpu as pltpu
from jax.sharding import PartitionSpec as P

POWERS = 4
F32 = jnp.float32
BF16 = jnp.bfloat16
LIMIT = 48 * 1024 * 1024


def split(v):
    high = v.astype(BF16)
    return high, (v - high.astype(F32)).astype(BF16)


def passed(x, by):
    peers = lax.axis_size("beam")
    return lax.ppermute(x, "beam", [(i, i + by) for i in range(peers) if 0 <= i + by < peers])


def step_body(fix, with_prev, last, nx, nz, width, chip, scal, *refs):
    refs = list(refs)
    cur_ref = refs.pop(0)
    if fix:
        pin_ref, bin_ref = refs.pop(0), refs.pop(0)
    prev_ref = refs.pop(0) if with_prev else None
    pot_ref, kz_ref, kx_ref, wy_ref, rcol_ref, wvec_ref = refs[:6]
    refs = refs[6:]
    out_ref = refs.pop(0)
    if not last:
        first_ref, bridge_ref = refs.pop(0), refs.pop(0)
    if fix:
        rows_ref, col_ref = refs.pop(0), refs.pop(0)
    else:
        col_ref = cur_ref
    half = width // 2
    scale = 2.0 if with_prev else 1.0
    left = lax.broadcasted_iota(jnp.int32, (nz, width), 1) < half
    x_start = scal[0] if last else 0

    def fixed(x):
        at = pl.ds(pl.multiple_of(x * nz, nz), nz)
        u = cur_ref[at, :]
        if fix:
            u = u + rcol_ref[...] * pin_ref[pl.ds(x, 1), :]
            head = u[0:8] + jnp.where(
                lax.broadcasted_iota(jnp.int32, (8, width), 0) == 0, bin_ref[pl.ds(x, 1), :], 0.0
            )
            u = jnp.concatenate([head, u[8:]], axis=0)
            col_ref[at, :] = u
        return u

    def local_pair(x0):
        us = []
        for q in range(2):
            if last:
                us.append(col_ref[pl.ds(pl.multiple_of((x_start + x0 + q) * nz, nz), nz), :])
            else:
                us.append(fixed(x0 + q))
        parts = [split(u) for u in us]
        highs = jnp.concatenate([p[0] for p in parts], axis=1)
        lows = jnp.concatenate([p[1] for p in parts], axis=1)
        along_z = jnp.dot(
            kz_ref[...],
            jnp.concatenate([highs, lows, highs], axis=0),
            preferred_element_type=F32,
        )
        along_y = jnp.dot(
            jnp.concatenate([jnp.concatenate(p, axis=1) for p in parts], axis=0),
            wy_ref[...],
            preferred_element_type=F32,
        )
        for q in range(2):
            u = us[q]
            x = x0 + q
            at = pl.ds(pl.multiple_of((x_start + x) * nz, nz), nz)
            to = pl.ds(pl.multiple_of(x * nz, nz), nz)
            pv = pot_ref[at, :]
            pr = pltpu.roll(pv, half, 1)
            optical = jnp.where(left, pv, pr) * u + jnp.where(left, pr, -pv) * pltpu.roll(u, half, 1)
            ay = along_y[q * nz : (q + 1) * nz]
            new = (
                along_z[:, q * width : (q + 1) * width]
                + ay[:, :width]
                + ay[:, width:]
                + scale * optical
            )
            if with_prev:
                new = new - prev_ref[at, :]
            out_ref[to, :] = new

    if last:

        def fix_some(i, carry):
            for q in range(8):
                fixed(i * 8 + q)
            return carry

        lax.fori_loop(0, nx // 8, fix_some, 0)
    out_x = chip if last else nx
    pairs = 4

    def local_some(i, carry):
        for q in range(pairs):
            local_pair((i * pairs + q) * 2)
        return carry

    lax.fori_loop(0, out_x // (2 * pairs), local_some, 0)
    if fix:
        rows_ref[...] = col_ref[pl.ds(pl.multiple_of(scal[0] * nz, nz), chip * nz), :]

    def across_pair(z0, bridge):
        us = [col_ref[pl.ds(z0 + q, nx, stride=nz), :] for q in range(2)]
        parts = [split(u) for u in us]
        highs = jnp.concatenate([p[0] for p in parts], axis=1)
        lows = jnp.concatenate([p[1] for p in parts], axis=1)
        along_x = jnp.dot(
            kx_ref[...],
            jnp.concatenate([highs, lows, highs], axis=0),
            preferred_element_type=F32,
        )
        for q in range(2):
            at = pl.ds(z0 + q, out_x, stride=nz)
            new = out_ref[at, :] + along_x[:, q * width : (q + 1) * width]
            out_ref[at, :] = new
            if not last:
                bridge = bridge + wvec_ref[pl.ds(z0 + q, 1), :] * new
        return bridge

    def across_some(i, bridge):
        for q in range(pairs):
            bridge = across_pair((i * pairs + q) * 2, bridge)
        return bridge

    bridge = jnp.zeros((out_x, width), F32)
    bridge = lax.fori_loop(0, nz // (2 * pairs), across_some, bridge)
    if not last:
        bridge_ref[...] = bridge
        first_ref[...] = out_ref[pl.ds(0, nx, stride=nz), :]


def vm():
    return pl.BlockSpec(memory_space=pltpu.VMEM)


def in_vmem(*shape):
    return pltpu.VMEM(shape, F32)


def step(scal, cur, halo, prev, pot, kz, kx, wy, rcol, wvec, nx, nz, chip, last):
    fix, with_prev = halo is not None, prev is not None
    width = cur.shape[-1]
    ins = [cur] + (list(halo) if fix else []) + ([prev] if with_prev else [])
    ins += [pot, kz, kx, wy, rcol, wvec]
    outs = [in_vmem((chip if last else nx) * nz, width)]
    if not last:
        outs += [in_vmem(nx, width), in_vmem(nx, width)]
    if fix:
        outs += [in_vmem(chip * nz, width)]
    scratch = []
    if fix:
        if last:
            scratch = [pltpu.VMEM((nx * nz, width), F32)]
        else:
            outs += [in_vmem(nx * nz, width)]
    body = functools.partial(step_body, fix, with_prev, last, nx, nz, width, chip)
    return pl.pallas_call(
        body,
        out_shape=outs,
        in_specs=[pl.BlockSpec(memory_space=pltpu.SMEM)] + [vm()] * len(ins),
        out_specs=[vm()] * len(outs),
        scratch_shapes=scratch,
        compiler_params=pltpu.CompilerParams(vmem_limit_bytes=LIMIT),
        cost_estimate=pl.CostEstimate(flops=4 * 10**9, bytes_accessed=8 * 10**6, transcendentals=0),
        name="step",
    )(scal, *ins)


def finish_body(nz, rows, scal, last_ref, pin_ref, bin_ref, rcol_ref, *refs):
    cols = refs[: POWERS - 1]
    keep_ref, send_ref = refs[POWERS - 1 :]
    core = scal[1]
    size = rows * nz
    width = last_ref.shape[-1]
    top = lax.broadcasted_iota(jnp.int32, (8, width), 0) == 0
    for ref, where in ((keep_ref, core), (send_ref, 1 - core)):
        at = pl.ds(pl.multiple_of(where * size, size), size)
        for k in range(POWERS - 1):
            ref[k] = cols[k][at, :]
        for r in range(rows):
            x = where * rows + r
            u = last_ref[pl.ds(pl.multiple_of(x * nz, nz), nz), :]
            u = u + rcol_ref[...] * pin_ref[pl.ds(x, 1), :]
            head = u[0:8] + jnp.where(top, bin_ref[pl.ds(x, 1), :], 0.0)
            ref[POWERS - 1, r * nz : (r + 1) * nz, :] = jnp.concatenate([head, u[8:]], axis=0)


def gram_body(scal, packets_ref, keep_ref, recv_ref, cols_ref, gram_ref, acc_ref):
    core = scal[1]
    ncol, size, width = cols_ref.shape
    npow = ncol // 2
    half = width // 2
    cols_ref[0] = packets_ref[0]
    cols_ref[npow] = packets_ref[1]
    for k in range(npow - 1):
        cols_ref[core * npow + 1 + k] = keep_ref[k]
        cols_ref[(1 - core) * npow + 1 + k] = recv_ref[k]
    acc_ref[...] = jnp.zeros_like(acc_ref)
    sign = jnp.where(lax.broadcasted_iota(jnp.int32, (8, width), 1) < half, 1.0, -1.0)
    first, second = list(range(npow)), list(range(npow, ncol))
    groups = [
        [(a, b) for a in first for b in first if a <= b],
        [(a, b) for a in second for b in second if a <= b],
        [(a, b) for a in first for b in second[:3]],
        [(a, b) for a in first for b in second[3:]],
    ]
    for pairs in groups:
        used = sorted({c for pair in pairs for c in pair})
        turned = sorted({b for a, b in pairs if a != b})

        def chunk(i, sums, pairs=pairs, used=used, turned=turned):
            sums = list(sums)
            at = pl.ds(pl.multiple_of(i * 8, 8), 8)
            v = {c: cols_ref[c, at, :] for c in used}
            t = {c: pltpu.roll(v[c], half, 1) for c in turned}
            n = 0
            for a, b in pairs:
                sums[n] = sums[n] + v[a] * v[b]
                n += 1
                if a != b:
                    sums[n] = sums[n] + v[a] * t[b]
                    n += 1
            return tuple(sums)

        count = sum(1 if a == b else 2 for a, b in pairs)
        sums = lax.fori_loop(
            0, size // 8, chunk, tuple(jnp.zeros((8, width), F32) for _ in range(count)), unroll=2
        )
        n = 0
        for a, b in pairs:
            acc_ref[a * ncol + b : a * ncol + b + 1, :] = jnp.sum(sums[n], axis=0, keepdims=True)
            n += 1
            if a != b:
                acc_ref[b * ncol + a : b * ncol + a + 1, :] = jnp.sum(
                    sums[n] * sign, axis=0, keepdims=True
                )
                n += 1
    row = jnp.sum(acc_ref[...].T, axis=0, keepdims=True)
    gram_ref[...] = jnp.broadcast_to(row[None], gram_ref.shape)


def basis_body(cells, gram_ref, cols_ref, basis_ref, factor_ref, coef_ref):
    ncol, _, size, width = cols_ref.shape
    half = width // 2

    @pl.when(pl.program_id(0) == 0)
    def _():
        row = jnp.sum(gram_ref[...], axis=0) * (1.0 / cells)
        r = lax.broadcasted_iota(jnp.int32, (16, width), 0)
        c = lax.broadcasted_iota(jnp.int32, (16, width), 1)
        packed = jnp.zeros((16, width), F32)
        for j in range(ncol):
            moved = row if j == 0 else pltpu.roll(row, width - ncol * j, 1)
            packed = jnp.where(r == j, moved, packed)
        turned = jnp.concatenate([packed, jnp.zeros((width - 16, width), F32)], axis=0).T[:16]
        inside = (r < ncol) & (c < ncol)
        re = jnp.where(inside, jnp.where(r <= c, packed, turned), 0.0)
        im = jnp.where(inside & (r != c), jnp.where(r < c, turned, -packed), 0.0)
        re = jnp.where(c == r + 16, 1.0, re)
        up_re = jnp.zeros((16, width), F32)
        up_im = jnp.zeros((16, width), F32)
        for j in range(ncol):
            pivot = jnp.sqrt(re[j : j + 1, j : j + 1])
            inverse = 1.0 / pivot
            row_re = re[j : j + 1, :] * inverse
            row_im = im[j : j + 1, :] * inverse
            col_re = re[:, j : j + 1] * inverse
            col_im = im[:, j : j + 1] * inverse
            up_re = jnp.where(r == j, row_re, up_re)
            up_im = jnp.where(r == j, row_im, up_im)
            below = r > j
            re = re - jnp.where(below, col_re * row_re - col_im * row_im, 0.0)
            im = im - jnp.where(below, col_re * row_im + col_im * row_re, 0.0)
        keep = (c >= r) & (c < ncol)
        factor_ref[0] = jnp.where(keep, up_re, 0.0)
        factor_ref[1] = jnp.where(keep & (c > r), up_im, 0.0)
        sign = jnp.where(lax.broadcasted_iota(jnp.int32, (8, width), 1) < half, 1.0, -1.0)
        for k in range(ncol):
            for i in range(k + 1):
                coef_ref[0, k * ncol + i] = jnp.broadcast_to(up_re[k : k + 1, 16 + i : 17 + i], (8, width))
                coef_ref[1, k * ncol + i] = (
                    jnp.broadcast_to(up_im[k : k + 1, 16 + i : 17 + i], (8, width)) * sign
                )

    group = 4
    for start in range(0, size, 8 * group):
        slots = [slice(start + 8 * g, start + 8 * g + 8) for g in range(group)]
        v = [[cols_ref[i, 0, s, :] for s in slots] for i in range(ncol)]
        t = [[pltpu.roll(x, half, 1) for x in xs] for xs in v]
        for k in range(ncol):
            total = [None] * group
            for i in range(k + 1):
                re = coef_ref[0, k * ncol + i]
                im = coef_ref[1, k * ncol + i]
                for g in range(group):
                    term = re * v[i][g]
                    if i < k:
                        term = term + im * t[i][g]
                    total[g] = term if total[g] is None else total[g] + term
            for g in range(group):
                basis_ref[k, 0, slots[g], :] = total[g]


def shards(packets, kinetic_x, kinetic_y, element_kinetic, potential):
    npack, rows, nz, width = packets.shape
    trans = lax.axis_size("trans")
    nx = rows * trans
    ncol = npack * (POWERS + 1)
    me = lax.axis_index("trans")
    core = me % 2
    chip = 2 * rows
    scal = jnp.stack([(me // 2) * chip, core]).astype(jnp.int32)

    pot = lax.all_gather(potential, "trans", axis=0, tiled=True).reshape(nx * nz, width)
    sent = jnp.broadcast_to(packets[None], (trans // 2,) + packets.shape)
    sent = sent.reshape((trans, rows, nz, width))
    cur = lax.all_to_all(sent, "trans", 0, 0, tiled=True).reshape(nx * nz, width)

    corner = element_kinetic[nz, nz] * (lax.axis_index("beam") > 0).astype(F32)
    kz = element_kinetic[:nz, :nz].at[0, 0].add(corner)
    wrow = element_kinetic[nz, :nz]
    rcol = element_kinetic[:nz, nz]

    def parts_of(k):
        high = lax.reduce_precision(k, 8, 7)
        return high.astype(BF16), (k - high).astype(BF16)

    def left_weights(k):
        high, low = parts_of(k)
        return jnp.concatenate([high, high, low], axis=1)

    ky_high, ky_low = parts_of(jnp.kron(jnp.eye(2, dtype=F32), kinetic_y).T)
    wy = jnp.concatenate(
        [
            jnp.concatenate([ky_high, ky_low], axis=1),
            jnp.concatenate([ky_high, jnp.zeros_like(ky_low)], axis=1),
        ],
        axis=0,
    )
    kz1, kx1 = left_weights(kz), left_weights(kinetic_x)
    kz2, kx2, wy2 = kz1 * 2, kx1 * 2, wy * 2
    kx_last = lax.dynamic_slice_in_dim(kx2, scal[0], chip, 0)
    rcol1 = jnp.broadcast_to(rcol[:, None], (nz, width))
    rcol2 = rcol1 * 2.0
    wvec = jnp.broadcast_to(wrow[:, None], (nz, width))

    def halo(first, bridge, pin, bin_, scale):
        if pin is not None:
            bridge = bridge + (scale * jnp.dot(wrow, rcol, precision="highest")) * pin
            bridge = bridge + (scale * wrow[0]) * bin_
            first = first + (scale * rcol[0]) * pin + scale * bin_
        return passed(first, -1), passed(bridge, 1)

    whole = cur.reshape(nx, nz, width)
    halos = [halo(whole[:, 0], jnp.sum(whole * wvec, axis=1), None, None, 1.0)]
    columns = []
    prev = None
    local, first, bridge = step(
        scal, cur, None, None, pot, kz1, kx1, wy, rcol1, wvec, nx, nz, chip, False
    )
    prev = cur
    for k in range(1, POWERS):
        scale = 1.0 if k == 1 else 2.0
        pin, bin_ = halos[-1]
        fresh = halo(first, bridge, pin, bin_, scale)
        last = k == POWERS - 1
        got = step(
            scal,
            local,
            (pin, scale * bin_),
            prev,
            pot,
            kz2,
            kx_last if last else kx2,
            wy2,
            rcol1 if k == 1 else rcol2,
            wvec,
            nx,
            nz,
            chip,
            last,
        )
        if last:
            local, col_rows = got
        else:
            prev_next = got[4]
            local, first, bridge, col_rows = got[:4]
            prev = prev_next
        columns.append(col_rows)
        halos.append(fresh)
    pin, bin_ = halos[-1]
    pin = lax.dynamic_slice_in_dim(pin, scal[0], chip, 0)
    bin_ = lax.dynamic_slice_in_dim(2.0 * bin_, scal[0], chip, 0)
    size = rows * nz
    keep, send = pl.pallas_call(
        functools.partial(finish_body, nz, rows),
        out_shape=[in_vmem(POWERS, size, width)] * 2,
        in_specs=[pl.BlockSpec(memory_space=pltpu.SMEM)] + [vm()] * (4 + POWERS - 1),
        out_specs=[vm()] * 2,
        compiler_params=pltpu.CompilerParams(vmem_limit_bytes=LIMIT),
        name="finish",
    )(scal, local, pin, bin_, rcol2, *columns)
    recv = lax.ppermute(send, "trans", [(i, i ^ 1) for i in range(trans)])
    cols, gram = pl.pallas_call(
        gram_body,
        out_shape=[in_vmem(ncol, size, width), in_vmem(trans, 1, width)],
        in_specs=[pl.BlockSpec(memory_space=pltpu.SMEM)] + [vm()] * 3,
        out_specs=[vm()] * 2,
        scratch_shapes=[pltpu.VMEM((128, width), F32)],
        compiler_params=pltpu.CompilerParams(vmem_limit_bytes=LIMIT),
        name="gram",
    )(scal, packets.reshape(npack, size, width), keep, recv)
    beam = lax.axis_size("beam")
    gram = jnp.sum(lax.all_to_all(gram, "trans", 0, 0, tiled=True), axis=0, keepdims=True)
    gram = lax.all_to_all(jnp.broadcast_to(gram, (beam, 1, width)), "beam", 0, 0, tiled=True)
    cells = float(nx * (width // 2) * nz * beam)
    basis, factor = pl.pallas_call(
        functools.partial(basis_body, cells),
        grid=(rows,),
        out_shape=[
            jax.ShapeDtypeStruct((ncol, rows, nz, width), F32),
            jax.ShapeDtypeStruct((2, 16, width), F32),
        ],
        in_specs=[
            pl.BlockSpec((beam, 1, width), lambda i: (0, 0, 0)),
            pl.BlockSpec((ncol, 1, nz, width), lambda i: (0, i, 0, 0)),
        ],
        out_specs=[
            pl.BlockSpec((ncol, 1, nz, width), lambda i: (0, i, 0, 0)),
            pl.BlockSpec((2, 16, width), lambda i: (0, 0, 0)),
        ],
        scratch_shapes=[pltpu.VMEM((2, ncol * ncol, 8, width), F32)],
        compiler_params=pltpu.CompilerParams(vmem_limit_bytes=LIMIT),
        name="basis",
    )(gram, cols.reshape(ncol, rows, nz, width))
    return basis, factor[:, :ncol, :ncol]


def solution(mesh):
    in_specs = (P(None, "trans", "beam", None), P(), P(), P(), P("trans", "beam", None))
    out_specs = (P(None, "trans", "beam", None), P())
    return jax.shard_map(shards, mesh=mesh, in_specs=in_specs, out_specs=out_specs, check_vma=False)
```

```python
import functools

import jax
import jax.numpy as jnp
from jax import lax
from jax.experimental import pallas as pl
from jax.experimental.pallas import tpu as pltpu
from jax.sharding import PartitionSpec as P

POWERS = 4
F32 = jnp.float32
BF16 = jnp.bfloat16
LIMIT = 16 * 1024 * 1024


def split(v):
    high = v.astype(BF16)
    return high, (v - high.astype(F32)).astype(BF16)


def passed(x, by):
    peers = lax.axis_size("beam")
    return lax.ppermute(x, "beam", [(i, i + by) for i in range(peers) if 0 <= i + by < peers])


PAD = 8


def step_body(fix, with_prev, last, nx, nz, width, chip, strides, scal, *refs):
    refs = list(refs)
    cur_ref = refs.pop(0)
    if fix:
        pin_ref, bin_ref = refs.pop(0), refs.pop(0)
    prev_ref = refs.pop(0) if with_prev else None
    pot_ref, kz_ref, kx_ref, wy_ref, rcol_ref, wvec_ref = refs[:6]
    refs = refs[6:]
    out_ref = refs.pop(0)
    if not last:
        first_ref, bridge_ref = refs.pop(0), refs.pop(0)
    rows_ref = refs.pop(0) if fix else None
    col_ref = refs.pop(0)
    cur_stride, prev_stride = strides
    stride = nz + PAD
    half = width // 2
    scale = 2.0 if with_prev else 1.0
    left = lax.broadcasted_iota(jnp.int32, (nz, width), 1) < half
    top = lax.broadcasted_iota(jnp.int32, (8, width), 0) == 0
    x_start = scal[0] if last else 0
    out_x = chip if last else nx

    def rows_of(x, step):
        return pl.ds(pl.multiple_of(x * step, 8), nz)

    def fixed(x):
        u = cur_ref[rows_of(x, cur_stride), :]
        if fix:
            u = u + rcol_ref[...] * pin_ref[pl.ds(x, 1), :]
            head = u[0:8] + jnp.where(top, bin_ref[pl.ds(x, 1), :], 0.0)
            u = jnp.concatenate([head, u[8:]], axis=0)
        col_ref[rows_of(x, stride), :] = u
        return u

    def product(k_ref, us):
        parts = [split(u) for u in us]
        rows = []
        for p, q in (parts[0:2], parts[2:4]):
            rows += [jnp.concatenate([p[0], q[0]], axis=1), jnp.concatenate([p[1], q[1]], axis=1)]
        got = jnp.dot(k_ref[...], jnp.concatenate(rows, axis=0), preferred_element_type=F32)
        m = got.shape[0] // 4
        outs = []
        for i in range(2):
            both = got[2 * i * m : (2 * i + 1) * m] + got[(2 * i + 1) * m : (2 * i + 2) * m]
            outs += [both[:, :width], both[:, width:]]
        return outs, parts

    def local_four(x0):
        us = []
        for q in range(4):
            if last:
                us.append(col_ref[rows_of(x_start + x0 + q, stride), :])
            else:
                us.append(fixed(x0 + q))
        along_z, parts = product(kz_ref, us)
        along_y = jnp.dot(
            jnp.concatenate([jnp.concatenate(p, axis=1) for p in parts], axis=0),
            wy_ref[...],
            preferred_element_type=F32,
        )
        for q in range(4):
            u = us[q]
            x = x_start + x0 + q
            pv = pot_ref[rows_of(x, nz), :]
            pr = pltpu.roll(pv, half, 1)
            optical = jnp.where(left, pv, pr) * u + jnp.where(left, pr, -pv) * pltpu.roll(u, half, 1)
            ay = along_y[q * nz : (q + 1) * nz]
            new = along_z[q] + ay[:, :width] + ay[:, width:] + scale * optical
            if with_prev:
                new = new - prev_ref[rows_of(x, prev_stride), :]
            out_ref[rows_of(x0 + q, stride), :] = new

    def repeat(count, unroll, body, carry):
        unroll = min(unroll, count)

        def some(i, carry):
            for q in range(unroll):
                carry = body(i * unroll + q, carry)
            return carry

        return lax.fori_loop(0, count // unroll, some, carry)

    def only(body):
        def with_carry(i, carry):
            body(i)
            return carry

        return with_carry

    if last:
        repeat(nx, 16, only(fixed), 0)
    repeat(out_x // 4, 8, only(lambda i: local_four(i * 4)), 0)
    if fix:
        for q in range(chip):
            rows_ref[q * nz : (q + 1) * nz, :] = col_ref[rows_of(scal[0] + q, stride), :]

    def across_four(i, bridge):
        z0 = i * 4
        us = [col_ref[pl.ds(z0 + q, nx, stride=stride), :] for q in range(4)]
        along_x, _ = product(kx_ref, us)
        for q in range(4):
            at = pl.ds(z0 + q, out_x, stride=stride)
            new = out_ref[at, :] + along_x[q]
            out_ref[at, :] = new
            if not last:
                bridge = bridge + wvec_ref[pl.ds(z0 + q, 1), :] * new
        return bridge

    bridge = repeat(nz // 4, 8, across_four, jnp.zeros((out_x, width), F32))
    if not last:
        bridge_ref[...] = bridge
        first_ref[...] = out_ref[pl.ds(0, nx, stride=stride), :]


def vm():
    return pl.BlockSpec(memory_space=pltpu.VMEM)


def in_vmem(*shape):
    return pltpu.VMEM(shape, F32)


def step(scal, cur, halo, prev, pot, kz, kx, wy, rcol, wvec, nx, nz, chip, last):
    fix, with_prev = halo is not None, prev is not None
    width = cur.shape[-1]
    stride = nz + PAD
    ins = [cur] + (list(halo) if fix else []) + ([prev] if with_prev else [])
    ins += [pot, kz, kx, wy, rcol, wvec]
    outs = [in_vmem((chip if last else nx) * stride, width)]
    if not last:
        outs += [in_vmem(nx, width), in_vmem(nx, width)]
    if fix:
        outs += [in_vmem(chip * nz, width)]
    scratch = []
    if fix and not last:
        outs += [in_vmem(nx * stride, width)]
    else:
        scratch = [pltpu.VMEM((nx * stride, width), F32)]
    strides = (cur.shape[0] // nx, prev.shape[0] // nx if with_prev else 0)
    body = functools.partial(step_body, fix, with_prev, last, nx, nz, width, chip, strides)
    return pl.pallas_call(
        body,
        out_shape=outs,
        in_specs=[pl.BlockSpec(memory_space=pltpu.SMEM)] + [vm()] * len(ins),
        out_specs=[vm()] * len(outs),
        scratch_shapes=scratch,
        compiler_params=pltpu.CompilerParams(vmem_limit_bytes=LIMIT),
        cost_estimate=pl.CostEstimate(flops=4 * 10**9, bytes_accessed=8 * 10**6, transcendentals=0),
        name="step",
    )(scal, *ins)


def finish_body(nz, rows, scal, last_ref, pin_ref, bin_ref, rcol_ref, *refs):
    cols = refs[: POWERS - 1]
    keep_ref, send_ref = refs[POWERS - 1 :]
    core = scal[1]
    size = rows * nz
    width = last_ref.shape[-1]
    top = lax.broadcasted_iota(jnp.int32, (8, width), 0) == 0
    for ref, where in ((keep_ref, core), (send_ref, 1 - core)):
        at = pl.ds(pl.multiple_of(where * size, size), size)
        for k in range(POWERS - 1):
            ref[k] = cols[k][at, :]
        for r in range(rows):
            x = where * rows + r
            u = last_ref[pl.ds(pl.multiple_of(x * (nz + PAD), 8), nz), :]
            u = u + rcol_ref[...] * pin_ref[pl.ds(x, 1), :]
            head = u[0:8] + jnp.where(top, bin_ref[pl.ds(x, 1), :], 0.0)
            ref[POWERS - 1, r * nz : (r + 1) * nz, :] = jnp.concatenate([head, u[8:]], axis=0)


def gram_body(scal, packets_ref, keep_ref, recv_ref, cols_ref, gram_ref, acc_ref):
    core = scal[1]
    ncol, size, width = cols_ref.shape
    npow = ncol // 2
    half = width // 2
    cols_ref[0] = packets_ref[0]
    cols_ref[npow] = packets_ref[1]
    for k in range(npow - 1):
        cols_ref[core * npow + 1 + k] = keep_ref[k]
        cols_ref[(1 - core) * npow + 1 + k] = recv_ref[k]
    acc_ref[...] = jnp.zeros_like(acc_ref)
    sign = jnp.where(lax.broadcasted_iota(jnp.int32, (8, width), 1) < half, 1.0, -1.0)
    first, second = list(range(npow)), list(range(npow, ncol))
    groups = [
        [(a, b) for a in first for b in first if a <= b],
        [(a, b) for a in second for b in second if a <= b],
        [(a, b) for a in first for b in second[:3]],
        [(a, b) for a in first for b in second[3:]],
    ]
    unroll = 16
    for pairs in groups:
        used = sorted({c for pair in pairs for c in pair})
        turned = sorted({b for a, b in pairs if a != b})

        def chunk(i, sums, pairs=pairs, used=used, turned=turned):
            sums = list(sums)
            for q in range(unroll):
                at = pl.ds(pl.multiple_of((i * unroll + q) * 8, 8), 8)
                v = {c: cols_ref[c, at, :] for c in used}
                t = {c: pltpu.roll(v[c], half, 1) for c in turned}
                n = 0
                for a, b in pairs:
                    sums[n] = sums[n] + v[a] * v[b]
                    n += 1
                    if a != b:
                        sums[n] = sums[n] + v[a] * t[b]
                        n += 1
            return tuple(sums)

        count = sum(1 if a == b else 2 for a, b in pairs)
        sums = lax.fori_loop(
            0, size // (8 * unroll), chunk, tuple(jnp.zeros((8, width), F32) for _ in range(count))
        )
        n = 0
        for a, b in pairs:
            acc_ref[a * ncol + b : a * ncol + b + 1, :] = jnp.sum(sums[n], axis=0, keepdims=True)
            n += 1
            if a != b:
                acc_ref[b * ncol + a : b * ncol + a + 1, :] = jnp.sum(
                    sums[n] * sign, axis=0, keepdims=True
                )
                n += 1
    row = jnp.sum(acc_ref[...].T, axis=0, keepdims=True)
    gram_ref[...] = jnp.broadcast_to(row[None], gram_ref.shape)


def basis_body(cells, rows, gram_ref, cols_ref, basis_ref, factor_ref, coef_ref, out_ref, sems):
    ncol, size, width = cols_ref.shape
    half = width // 2
    row = jnp.sum(gram_ref[...], axis=0) * (1.0 / cells)
    r = lax.broadcasted_iota(jnp.int32, (16, width), 0)
    c = lax.broadcasted_iota(jnp.int32, (16, width), 1)
    packed = jnp.zeros((16, width), F32)
    for j in range(ncol):
        moved = row if j == 0 else pltpu.roll(row, width - ncol * j, 1)
        packed = jnp.where(r == j, moved, packed)
    turned = jnp.concatenate([packed, jnp.zeros((width - 16, width), F32)], axis=0).T[:16]
    inside = (r < ncol) & (c < ncol)
    re = jnp.where(inside, jnp.where(r <= c, packed, turned), 0.0)
    im = jnp.where(inside & (r != c), jnp.where(r < c, turned, -packed), 0.0)
    re = jnp.where(c == r + 16, 1.0, re)
    up_re = jnp.zeros((16, width), F32)
    up_im = jnp.zeros((16, width), F32)
    for j in range(ncol):
        pivot = jnp.sqrt(re[j : j + 1, j : j + 1])
        inverse = 1.0 / pivot
        row_re = re[j : j + 1, :] * inverse
        row_im = im[j : j + 1, :] * inverse
        col_re = re[:, j : j + 1] * inverse
        col_im = im[:, j : j + 1] * inverse
        up_re = jnp.where(r == j, row_re, up_re)
        up_im = jnp.where(r == j, row_im, up_im)
        below = r > j
        re = re - jnp.where(below, col_re * row_re - col_im * row_im, 0.0)
        im = im - jnp.where(below, col_re * row_im + col_im * row_re, 0.0)
    keep = (c >= r) & (c < ncol)
    factor_ref[0] = jnp.where(keep, up_re, 0.0)
    factor_ref[1] = jnp.where(keep & (c > r), up_im, 0.0)
    sign = jnp.where(lax.broadcasted_iota(jnp.int32, (8, width), 1) < half, 1.0, -1.0)
    for k in range(ncol):
        for i in range(k + 1):
            coef_ref[0, k * ncol + i] = jnp.broadcast_to(up_re[k : k + 1, 16 + i : 17 + i], (8, width))
            coef_ref[1, k * ncol + i] = (
                jnp.broadcast_to(up_im[k : k + 1, 16 + i : 17 + i], (8, width)) * sign
            )
    group = 4
    each = size // rows
    copies = []
    for r in range(rows):
        for start in range(r * each, (r + 1) * each, 8 * group):
            slots = [slice(start + 8 * g, start + 8 * g + 8) for g in range(group)]
            v = [[cols_ref[i, s, :] for s in slots] for i in range(ncol)]
            t = [[pltpu.roll(x, half, 1) for x in xs] for xs in v]
            for k in range(ncol):
                total = [None] * group
                for i in range(k + 1):
                    re = coef_ref[0, k * ncol + i]
                    im = coef_ref[1, k * ncol + i]
                    for g in range(group):
                        term = re * v[i][g]
                        if i < k:
                            term = term + im * t[i][g]
                        total[g] = term if total[g] is None else total[g] + term
                for g in range(group):
                    out_ref[k, slots[g], :] = total[g]
        part = pl.ds(r * each, each)
        copy = pltpu.make_async_copy(out_ref.at[:, part, :], basis_ref.at[:, part, :], sems.at[r])
        copy.start()
        copies.append(copy)
    for copy in copies:
        copy.wait()


def shards(packets, kinetic_x, kinetic_y, element_kinetic, potential):
    npack, rows, nz, width = packets.shape
    trans = lax.axis_size("trans")
    nx = rows * trans
    ncol = npack * (POWERS + 1)
    me = lax.axis_index("trans")
    core = me % 2
    chip = 2 * rows
    scal = jnp.stack([(me // 2) * chip, core]).astype(jnp.int32)

    pot = lax.all_gather(potential.reshape(rows * nz, width), "trans", axis=0, tiled=True)
    sent = packets.reshape(npack, rows * nz, width)
    sent = jnp.concatenate([sent] * (trans // npack), axis=0)
    cur = lax.all_to_all(sent, "trans", 0, 0, tiled=True).reshape(nx * nz, width)

    corner = element_kinetic[nz, nz] * (lax.axis_index("beam") > 0).astype(F32)
    kz = element_kinetic[:nz, :nz].at[0, 0].add(corner)
    wrow = element_kinetic[nz, :nz]
    rcol = element_kinetic[:nz, nz]

    def parts_of(k):
        high = lax.reduce_precision(k, 8, 7)
        return high.astype(BF16), (k - high).astype(BF16)

    def left_weights(k):
        high, low = parts_of(k)
        none = jnp.zeros_like(high)
        block = jnp.concatenate(
            [jnp.concatenate([high, high], axis=1), jnp.concatenate([low, none], axis=1)], axis=0
        )
        none = jnp.zeros_like(block)
        return jnp.concatenate(
            [jnp.concatenate([block, none], axis=1), jnp.concatenate([none, block], axis=1)], axis=0
        )

    ky_high, ky_low = parts_of(jnp.kron(jnp.eye(2, dtype=F32), kinetic_y).T)
    wy = jnp.concatenate(
        [
            jnp.concatenate([ky_high, ky_low], axis=1),
            jnp.concatenate([ky_high, jnp.zeros_like(ky_low)], axis=1),
        ],
        axis=0,
    )
    kz1, kx1 = left_weights(kz), left_weights(kinetic_x)
    kz2, kx2, wy2 = kz1 * 2, kx1 * 2, wy * 2
    kx_last = left_weights(2.0 * lax.dynamic_slice_in_dim(kinetic_x, scal[0], chip, 0))
    rcol1 = jnp.broadcast_to(rcol[:, None], (nz, width))
    rcol2 = rcol1 * 2.0
    wvec = jnp.broadcast_to(wrow[:, None], (nz, width))

    def halo(first, bridge, pin, bin_, scale):
        if pin is not None:
            bridge = bridge + (scale * jnp.dot(wrow, rcol, precision="highest")) * pin
            bridge = bridge + (scale * wrow[0]) * bin_
            first = first + (scale * rcol[0]) * pin + scale * bin_
        return passed(first, -1), passed(bridge, 1)

    whole = cur.reshape(nx, nz, width)
    halos = [halo(whole[:, 0], jnp.sum(whole * wvec, axis=1), None, None, 1.0)]
    columns = []
    prev = None
    local, first, bridge = step(
        scal, cur, None, None, pot, kz1, kx1, wy, rcol1, wvec, nx, nz, chip, False
    )
    prev = cur
    for k in range(1, POWERS):
        scale = 1.0 if k == 1 else 2.0
        pin, bin_ = halos[-1]
        fresh = halo(first, bridge, pin, bin_, scale)
        last = k == POWERS - 1
        got = step(
            scal,
            local,
            (pin, scale * bin_),
            prev,
            pot,
            kz2,
            kx_last if last else kx2,
            wy2,
            rcol1 if k == 1 else rcol2,
            wvec,
            nx,
            nz,
            chip,
            last,
        )
        if last:
            local, col_rows = got
        else:
            prev_next = got[4]
            local, first, bridge, col_rows = got[:4]
            prev = prev_next
        columns.append(col_rows)
        halos.append(fresh)
    pin, bin_ = halos[-1]
    pin = lax.dynamic_slice_in_dim(pin, scal[0], chip, 0)
    bin_ = lax.dynamic_slice_in_dim(2.0 * bin_, scal[0], chip, 0)
    size = rows * nz
    keep, send = pl.pallas_call(
        functools.partial(finish_body, nz, rows),
        out_shape=[in_vmem(POWERS, size, width)] * 2,
        in_specs=[pl.BlockSpec(memory_space=pltpu.SMEM)] + [vm()] * (4 + POWERS - 1),
        out_specs=[vm()] * 2,
        compiler_params=pltpu.CompilerParams(vmem_limit_bytes=LIMIT),
        name="finish",
    )(scal, local, pin, bin_, rcol2, *columns)
    recv = lax.ppermute(send, "trans", [(i, i ^ 1) for i in range(trans)])
    cols, gram = pl.pallas_call(
        gram_body,
        out_shape=[in_vmem(ncol, size, width), in_vmem(trans, 1, width)],
        in_specs=[pl.BlockSpec(memory_space=pltpu.SMEM)] + [vm()] * 3,
        out_specs=[vm()] * 2,
        scratch_shapes=[pltpu.VMEM((128, width), F32)],
        compiler_params=pltpu.CompilerParams(vmem_limit_bytes=LIMIT),
        name="gram",
    )(scal, packets.reshape(npack, size, width), keep, recv)
    beam = lax.axis_size("beam")
    gram = jnp.sum(lax.all_to_all(gram, "trans", 0, 0, tiled=True), axis=0, keepdims=True)
    gram = lax.all_to_all(jnp.broadcast_to(gram, (beam, 1, width)), "beam", 0, 0, tiled=True)
    cells = float(nx * (width // 2) * nz * beam)
    basis, factor = pl.pallas_call(
        functools.partial(basis_body, cells, rows),
        out_shape=[
            jax.ShapeDtypeStruct((ncol, size, width), F32),
            jax.ShapeDtypeStruct((2, 16, width), F32),
        ],
        in_specs=[vm(), vm()],
        out_specs=[pl.BlockSpec(memory_space=pl.ANY), vm()],
        scratch_shapes=[
            pltpu.VMEM((2, ncol * ncol, 8, width), F32),
            pltpu.VMEM((ncol, size, width), F32),
            pltpu.SemaphoreType.DMA((rows,)),
        ],
        compiler_params=pltpu.CompilerParams(vmem_limit_bytes=LIMIT),
        name="basis",
    )(gram, cols)
    return basis.reshape(ncol, rows, nz, width), factor[:, :ncol, :ncol]


def solution(mesh):
    in_specs = (P(None, "trans", "beam", None), P(), P(), P(), P("trans", "beam", None))
    out_specs = (P(None, "trans", "beam", None), P())
    return jax.shard_map(shards, mesh=mesh, in_specs=in_specs, out_specs=out_specs, check_vma=False)
```

```python
import functools

import jax
import jax.numpy as jnp
from jax import lax
from jax.experimental import pallas as pl
from jax.experimental.pallas import tpu as pltpu
from jax.sharding import PartitionSpec as P

POWERS = 4
F32 = jnp.float32
BF16 = jnp.bfloat16
LIMIT = 16 * 1024 * 1024


def split(v):
    high = v.astype(BF16)
    return high, (v - high.astype(F32)).astype(BF16)


def passed(x, by):
    peers = lax.axis_size("beam")
    return lax.ppermute(x, "beam", [(i, i + by) for i in range(peers) if 0 <= i + by < peers])


PAD = 8


def apply_local(nx, nz, width, refs, col, load, prev, halo, scale, out, bridge_ref):
    pot_ref, kz_ref, kx_ref, wy_ref, wvec_ref = refs
    col_ref, stride = col
    out_ref, x_start, out_x = out
    out_stride = nz + PAD
    half = width // 2
    left = lax.broadcasted_iota(jnp.int32, (nz, width), 1) < half

    def product(k_ref, us):
        parts = [split(u) for u in us]
        rows = []
        for p, q in (parts[0:2], parts[2:4]):
            rows += [jnp.concatenate([p[0], q[0]], axis=1), jnp.concatenate([p[1], q[1]], axis=1)]
        got = jnp.dot(k_ref[...], jnp.concatenate(rows, axis=0), preferred_element_type=F32)
        m = got.shape[0] // 4
        outs = []
        for i in range(2):
            both = got[2 * i * m : (2 * i + 1) * m] + got[(2 * i + 1) * m : (2 * i + 2) * m]
            outs += [both[:, :width], both[:, width:]]
        return outs, parts

    def local_four(x0):
        us = [load(x_start + x0 + q) for q in range(4)]
        along_z, parts = product(kz_ref, us)
        along_y = jnp.dot(
            jnp.concatenate([jnp.concatenate(p, axis=1) for p in parts], axis=0),
            wy_ref[...],
            preferred_element_type=F32,
        )
        for q in range(4):
            x = x_start + x0 + q
            ay = along_y[q * nz : (q + 1) * nz]
            new = along_z[q] + ay[:, :width] + ay[:, width:]
            new = new + scale * optical(us[q], pot_ref[rows_of(x, nz, nz), :], left)
            if prev is not None:
                new = new - prev[0][rows_of(x, prev[1], nz), :]
            if halo is not None:
                new = with_halo(new, halo, x)
            out_ref[rows_of(x0 + q, out_stride, nz), :] = new

    repeat(out_x // 4, 8, only(lambda i: local_four(i * 4)), 0)

    def across_four(i, bridge):
        z0 = i * 4
        us = [col_ref[pl.ds(z0 + q, nx, stride=stride), :] for q in range(4)]
        along_x, _ = product(kx_ref, us)
        for q in range(4):
            at = pl.ds(z0 + q, out_x, stride=out_stride)
            new = out_ref[at, :] + along_x[q]
            out_ref[at, :] = new
            if bridge_ref is not None:
                bridge = bridge + wvec_ref[pl.ds(z0 + q, 1), :] * new
        return bridge

    bridge = repeat(nz // 4, 8, across_four, jnp.zeros((out_x, width), F32))
    if bridge_ref is not None:
        bridge_ref[...] = bridge


def rows_of(x, stride, nz):
    return pl.ds(pl.multiple_of(x * stride, 8), nz)


def optical(u, pot, left):
    half = u.shape[-1] // 2
    turned = pltpu.roll(pot, half, 1)
    return jnp.where(left, pot, turned) * u + jnp.where(left, turned, -pot) * pltpu.roll(u, half, 1)


def with_halo(u, halo, x):
    column_ref, plane_ref, sum_ref = halo
    top = lax.broadcasted_iota(jnp.int32, (8, u.shape[-1]), 0) == 0
    u = u + column_ref[...] * plane_ref[pl.ds(x, 1), :]
    head = u[0:8] + jnp.where(top, sum_ref[pl.ds(x, 1), :], 0.0)
    return jnp.concatenate([head, u[8:]], axis=0)


def repeat(count, unroll, body, carry):
    unroll = min(unroll, count)

    def some(i, carry):
        for q in range(unroll):
            carry = body(i * unroll + q, carry)
        return carry

    return lax.fori_loop(0, count // unroll, some, carry)


def only(body):
    def with_carry(i, carry):
        body(i)
        return carry

    return with_carry


def copies_body(packets_ref, sent_ref, sems):
    npack = packets_ref.shape[0]
    copies = [
        pltpu.make_async_copy(packets_ref, sent_ref.at[pl.ds(i * npack, npack)], sems.at[i])
        for i in range(sent_ref.shape[0] // npack)
    ]
    for copy in copies:
        copy.start()
    for copy in copies:
        copy.wait()


def planes_body(nz, packets_ref, pot_ref, wvec_ref, kvec_ref, mvec_ref, first_ref, bridge_ref, zrest_ref, brest_ref):
    npack, size, width = packets_ref.shape
    rows = size // nz
    left = lax.broadcasted_iota(jnp.int32, (nz, width), 1) < width // 2
    for p in range(npack):
        for x in range(rows):
            u = packets_ref[p, x * nz : (x + 1) * nz, :]
            v = optical(u, pot_ref[x * nz : (x + 1) * nz, :], left)
            at = slice(p * rows + x, p * rows + x + 1)
            first_ref[at, :] = u[0:1]
            bridge_ref[at, :] = jnp.sum(wvec_ref[...] * u, axis=0, keepdims=True)
            zrest_ref[at, :] = v[0:1] + jnp.sum(kvec_ref[...] * u, axis=0, keepdims=True)
            brest_ref[at, :] = jnp.sum(wvec_ref[...] * v + mvec_ref[...] * u, axis=0, keepdims=True)


def pair_body(nx, nz, width, chip, scal, cur_ref, planes_ref, pot_ref, *refs):
    kz1, kx1, wy1, kz2, kx2, wy2, kx_ref, ky_ref, rcol1, rcol2, wvec = refs[:11]
    one_ref, two_ref, first_ref, bridge_ref, rows1_ref, rows2_ref, col_ref, halo_ref = refs[11:]
    stride = nz + PAD

    def packed(x):
        u = cur_ref[rows_of(x, nz, nz), :]
        col_ref[rows_of(x, stride, nz), :] = u
        return u

    precise = lax.Precision.HIGHEST
    for q in range(2):
        plane = planes_ref[q]
        moved = jnp.dot(kx_ref[...], plane, precision=precise, preferred_element_type=F32)
        moved = moved + jnp.dot(plane, ky_ref[...], precision=precise, preferred_element_type=F32)
        moved = moved + planes_ref[2 + q]
        halo_ref[q] = moved if q == 0 else 2.0 * moved
    apply_local(
        nx, nz, width, (pot_ref, kz1, kx1, wy1, wvec), (col_ref, stride), packed, None,
        (rcol1, planes_ref.at[0], planes_ref.at[1]), 1.0, (one_ref, 0, nx), None,
    )
    apply_local(
        nx, nz, width, (pot_ref, kz2, kx2, wy2, wvec), (one_ref, stride),
        lambda x: one_ref[rows_of(x, stride, nz), :], (cur_ref, nz),
        (rcol2, halo_ref.at[0], halo_ref.at[1]), 2.0, (two_ref, 0, nx), bridge_ref,
    )
    first_ref[...] = two_ref[pl.ds(0, nx, stride=stride), :]
    for ref, rows_ref in ((one_ref, rows1_ref), (two_ref, rows2_ref)):
        for q in range(chip):
            rows_ref[q * nz : (q + 1) * nz, :] = ref[rows_of(scal[0] + q, stride, nz), :]


def third_body(nx, nz, width, cur_ref, prev_ref, pot_ref, kz, kx, wy, wvec, out_ref, first_ref, bridge_ref):
    stride = nz + PAD
    apply_local(
        nx, nz, width, (pot_ref, kz, kx, wy, wvec), (cur_ref, stride),
        lambda x: cur_ref[rows_of(x, stride, nz), :], (prev_ref, stride), None, 2.0,
        (out_ref, 0, nx), bridge_ref,
    )
    first_ref[...] = out_ref[pl.ds(0, nx, stride=stride), :]


def fourth_body(nx, nz, width, chip, scal, cur_ref, pin_ref, bin_ref, prev_ref, pot_ref, *refs):
    kz, kx, wy, wvec, rcol, out_ref, rows_ref, col_ref = refs
    stride = nz + PAD

    def complete(x):
        u = with_halo(cur_ref[rows_of(x, stride, nz), :], (rcol, pin_ref, bin_ref), x)
        col_ref[rows_of(x, stride, nz), :] = u

    repeat(nx, 16, only(complete), 0)
    for q in range(chip):
        rows_ref[q * nz : (q + 1) * nz, :] = col_ref[rows_of(scal[0] + q, stride, nz), :]
    apply_local(
        nx, nz, width, (pot_ref, kz, kx, wy, wvec), (col_ref, stride),
        lambda x: col_ref[rows_of(x, stride, nz), :], (prev_ref, stride), None, 2.0,
        (out_ref, scal[0], chip), None,
    )


def vm():
    return pl.BlockSpec(memory_space=pltpu.VMEM)


def in_vmem(*shape):
    return pltpu.VMEM(shape, F32)


def call(name, body, outs, *ins, scal=None, scratch=(), cost=4):
    specs = [vm()] * len(ins)
    if scal is not None:
        specs = [pl.BlockSpec(memory_space=pltpu.SMEM)] + specs
        ins = (scal,) + ins
    return pl.pallas_call(
        body,
        out_shape=outs,
        in_specs=specs,
        out_specs=[vm()] * len(outs),
        scratch_shapes=list(scratch),
        compiler_params=pltpu.CompilerParams(vmem_limit_bytes=LIMIT),
        cost_estimate=pl.CostEstimate(
            flops=cost * 10**9, bytes_accessed=2 * cost * 10**6, transcendentals=0
        ),
        name=name,
    )(*ins)


def finish_body(nz, rows, scal, last_ref, pin_ref, bin_ref, rcol_ref, *refs):
    cols = refs[: POWERS - 1]
    keep_ref, send_ref = refs[POWERS - 1 :]
    core = scal[1]
    size = rows * nz
    width = last_ref.shape[-1]
    top = lax.broadcasted_iota(jnp.int32, (8, width), 0) == 0
    for ref, where in ((keep_ref, core), (send_ref, 1 - core)):
        at = pl.ds(pl.multiple_of(where * size, size), size)
        for k in range(POWERS - 1):
            ref[k] = cols[k][at, :]
        for r in range(rows):
            x = where * rows + r
            u = last_ref[pl.ds(pl.multiple_of(x * (nz + PAD), 8), nz), :]
            u = u + rcol_ref[...] * pin_ref[pl.ds(x, 1), :]
            head = u[0:8] + jnp.where(top, bin_ref[pl.ds(x, 1), :], 0.0)
            ref[POWERS - 1, r * nz : (r + 1) * nz, :] = jnp.concatenate([head, u[8:]], axis=0)


def gram_body(scal, packets_ref, keep_ref, recv_ref, cols_ref, gram_ref, acc_ref):
    core = scal[1]
    ncol, size, width = cols_ref.shape
    npow = ncol // 2
    half = width // 2
    cols_ref[0] = packets_ref[0]
    cols_ref[npow] = packets_ref[1]
    for k in range(npow - 1):
        cols_ref[core * npow + 1 + k] = keep_ref[k]
        cols_ref[(1 - core) * npow + 1 + k] = recv_ref[k]
    acc_ref[...] = jnp.zeros_like(acc_ref)
    sign = jnp.where(lax.broadcasted_iota(jnp.int32, (8, width), 1) < half, 1.0, -1.0)
    first, second = list(range(npow)), list(range(npow, ncol))
    groups = [
        [(a, b) for a in first for b in first if a <= b],
        [(a, b) for a in second for b in second if a <= b],
        [(a, b) for a in first for b in second[:3]],
        [(a, b) for a in first for b in second[3:]],
    ]
    unroll = 16
    for pairs in groups:
        used = sorted({c for pair in pairs for c in pair})
        turned = sorted({b for a, b in pairs if a != b})

        def chunk(i, sums, pairs=pairs, used=used, turned=turned):
            sums = list(sums)
            for q in range(unroll):
                at = pl.ds(pl.multiple_of((i * unroll + q) * 8, 8), 8)
                v = {c: cols_ref[c, at, :] for c in used}
                t = {c: pltpu.roll(v[c], half, 1) for c in turned}
                n = 0
                for a, b in pairs:
                    sums[n] = sums[n] + v[a] * v[b]
                    n += 1
                    if a != b:
                        sums[n] = sums[n] + v[a] * t[b]
                        n += 1
            return tuple(sums)

        count = sum(1 if a == b else 2 for a, b in pairs)
        sums = lax.fori_loop(
            0, size // (8 * unroll), chunk, tuple(jnp.zeros((8, width), F32) for _ in range(count))
        )
        n = 0
        for a, b in pairs:
            acc_ref[a * ncol + b : a * ncol + b + 1, :] = jnp.sum(sums[n], axis=0, keepdims=True)
            n += 1
            if a != b:
                acc_ref[b * ncol + a : b * ncol + a + 1, :] = jnp.sum(
                    sums[n] * sign, axis=0, keepdims=True
                )
                n += 1
    row = jnp.sum(acc_ref[...].T, axis=0, keepdims=True)
    gram_ref[...] = jnp.broadcast_to(row[None], gram_ref.shape)


def basis_body(cells, rows, gram_ref, cols_ref, basis_ref, factor_ref, coef_ref, out_ref, sems):
    ncol, size, width = cols_ref.shape
    half = width // 2
    row = jnp.sum(gram_ref[...], axis=0) * (1.0 / cells)
    r = lax.broadcasted_iota(jnp.int32, (16, width), 0)
    c = lax.broadcasted_iota(jnp.int32, (16, width), 1)
    packed = jnp.zeros((16, width), F32)
    for j in range(ncol):
        moved = row if j == 0 else pltpu.roll(row, width - ncol * j, 1)
        packed = jnp.where(r == j, moved, packed)
    turned = jnp.concatenate([packed, jnp.zeros((width - 16, width), F32)], axis=0).T[:16]
    inside = (r < ncol) & (c < ncol)
    re = jnp.where(inside, jnp.where(r <= c, packed, turned), 0.0)
    im = jnp.where(inside & (r != c), jnp.where(r < c, turned, -packed), 0.0)
    re = jnp.where(c == r + 16, 1.0, re)
    up_re = jnp.zeros((16, width), F32)
    up_im = jnp.zeros((16, width), F32)
    for j in range(ncol):
        pivot = jnp.sqrt(re[j : j + 1, j : j + 1])
        inverse = 1.0 / pivot
        row_re = re[j : j + 1, :] * inverse
        row_im = im[j : j + 1, :] * inverse
        col_re = re[:, j : j + 1] * inverse
        col_im = im[:, j : j + 1] * inverse
        up_re = jnp.where(r == j, row_re, up_re)
        up_im = jnp.where(r == j, row_im, up_im)
        below = r > j
        re = re - jnp.where(below, col_re * row_re - col_im * row_im, 0.0)
        im = im - jnp.where(below, col_re * row_im + col_im * row_re, 0.0)
    keep = (c >= r) & (c < ncol)
    factor_ref[0] = jnp.where(keep, up_re, 0.0)
    factor_ref[1] = jnp.where(keep & (c > r), up_im, 0.0)
    sign = jnp.where(lax.broadcasted_iota(jnp.int32, (8, width), 1) < half, 1.0, -1.0)
    for k in range(ncol):
        for i in range(k + 1):
            coef_ref[0, k * ncol + i] = jnp.broadcast_to(up_re[k : k + 1, 16 + i : 17 + i], (8, width))
            coef_ref[1, k * ncol + i] = (
                jnp.broadcast_to(up_im[k : k + 1, 16 + i : 17 + i], (8, width)) * sign
            )
    group = 4
    each = size // rows
    copies = []
    for r in range(rows):
        for start in range(r * each, (r + 1) * each, 8 * group):
            slots = [slice(start + 8 * g, start + 8 * g + 8) for g in range(group)]
            v = [[cols_ref[i, s, :] for s in slots] for i in range(ncol)]
            t = [[pltpu.roll(x, half, 1) for x in xs] for xs in v]
            for k in range(ncol):
                total = [None] * group
                for i in range(k + 1):
                    re = coef_ref[0, k * ncol + i]
                    im = coef_ref[1, k * ncol + i]
                    for g in range(group):
                        term = re * v[i][g]
                        if i < k:
                            term = term + im * t[i][g]
                        total[g] = term if total[g] is None else total[g] + term
                for g in range(group):
                    out_ref[k, slots[g], :] = total[g]
        part = pl.ds(r * each, each)
        copy = pltpu.make_async_copy(out_ref.at[:, part, :], basis_ref.at[:, part, :], sems.at[r])
        copy.start()
        copies.append(copy)
    for copy in copies:
        copy.wait()


def shards(packets, kinetic_x, kinetic_y, element_kinetic, potential):
    npack, rows, nz, width = packets.shape
    trans = lax.axis_size("trans")
    nx = rows * trans
    ncol = npack * (POWERS + 1)
    me = lax.axis_index("trans")
    core = me % 2
    chip = 2 * rows
    scal = jnp.stack([(me // 2) * chip, core]).astype(jnp.int32)

    size = rows * nz
    flat = packets.reshape(npack, size, width)
    mine = potential.reshape(size, width)
    pot = lax.all_gather(mine, "trans", axis=0, tiled=True)
    sent = pl.pallas_call(
        copies_body,
        out_shape=jax.ShapeDtypeStruct((trans, size, width), F32),
        in_specs=[vm()],
        out_specs=pl.BlockSpec(memory_space=pl.ANY),
        scratch_shapes=[pltpu.SemaphoreType.DMA((trans // npack,))],
        compiler_params=pltpu.CompilerParams(vmem_limit_bytes=LIMIT),
        name="copies",
    )(flat)
    cur = lax.all_to_all(sent, "trans", 0, 0, tiled=True).reshape(nx * nz, width)
    sent, flat_late, mine_late = lax.optimization_barrier((sent, flat, mine))

    corner = element_kinetic[nz, nz] * (lax.axis_index("beam") > 0).astype(F32)
    kz = element_kinetic[:nz, :nz].at[0, 0].add(corner)
    wrow = element_kinetic[nz, :nz]
    rcol = element_kinetic[:nz, nz]
    mrow = jnp.sum(wrow[:, None] * kz, axis=0)
    wr = jnp.sum(wrow * rcol)

    def parts_of(k):
        high = lax.reduce_precision(k, 8, 7)
        return high.astype(BF16), (k - high).astype(BF16)

    def left_weights(k):
        high, low = parts_of(k)
        none = jnp.zeros_like(high)
        block = jnp.concatenate(
            [jnp.concatenate([high, high], axis=1), jnp.concatenate([low, none], axis=1)], axis=0
        )
        none = jnp.zeros_like(block)
        return jnp.concatenate(
            [jnp.concatenate([block, none], axis=1), jnp.concatenate([none, block], axis=1)], axis=0
        )

    none = jnp.zeros_like(kinetic_y)
    ky = jnp.concatenate(
        [jnp.concatenate([kinetic_y.T, none], axis=1), jnp.concatenate([none, kinetic_y.T], axis=1)],
        axis=0,
    )
    ky_high, ky_low = parts_of(ky)
    wy = jnp.concatenate(
        [
            jnp.concatenate([ky_high, ky_low], axis=1),
            jnp.concatenate([ky_high, jnp.zeros_like(ky_low)], axis=1),
        ],
        axis=0,
    )
    kz1, kx1 = left_weights(kz), left_weights(kinetic_x)
    kz2, kx2, wy2 = kz1 * 2, kx1 * 2, wy * 2
    kx_last = left_weights(2.0 * lax.dynamic_slice_in_dim(kinetic_x, scal[0], chip, 0))

    def wide(column):
        return jnp.broadcast_to(column[:, None], (nz, width))

    rcol1, wvec = wide(rcol), wide(wrow)
    rcol2 = rcol1 * 2.0

    plane = in_vmem(npack * rows, width)
    first, bridge, zrest, brest = call(
        "planes", functools.partial(planes_body, nz), [plane] * 4,
        flat_late, mine_late, wvec, wide(kz[0]), wide(mrow), cost=1,
    )
    pin, bin_ = passed(first, -1), passed(bridge, 1)
    pnext = passed(zrest + rcol[0] * pin + bin_, -1)
    bnext = passed(brest + wr * pin + wrow[0] * bin_, 1)
    planes = jnp.stack([pin, bin_, pnext, bnext])
    planes = lax.all_gather(planes, "trans").reshape(trans, 4, npack, rows, width)
    planes = lax.dynamic_index_in_dim(planes, core, 2, keepdims=False)
    planes = planes.transpose(1, 0, 2, 3).reshape(4, nx, width)

    full, edge = in_vmem(nx * (nz + PAD), width), in_vmem(nx, width)
    here = in_vmem(chip * nz, width)
    col1, col2, first, bridge, rows1, rows2 = call(
        "pair", functools.partial(pair_body, nx, nz, width, chip), [full, full, edge, edge, here, here],
        cur, planes, pot, kz1, kx1, wy, kz2, kx2, wy2, kinetic_x, ky, rcol1, rcol2, wvec,
        scal=scal, scratch=[full, in_vmem(2, nx, width)], cost=8,
    )
    pin, bin_ = passed(first, -1), 2.0 * passed(bridge, 1)
    col3, first, bridge = call(
        "third", functools.partial(third_body, nx, nz, width), [full, edge, edge],
        col2, col1, pot, kz2, kx2, wy2, wvec,
    )
    first = first + (2.0 * rcol[0]) * pin + bin_
    bridge = bridge + (2.0 * wr) * pin + wrow[0] * bin_
    plast, blast = passed(first, -1), 2.0 * passed(bridge, 1)
    local, rows3 = call(
        "fourth", functools.partial(fourth_body, nx, nz, width, chip),
        [in_vmem(chip * (nz + PAD), width), here],
        col3, pin, bin_, col2, pot, kz2, kx_last, wy2, wvec, rcol2,
        scal=scal, scratch=[full], cost=2,
    )
    columns = [rows1, rows2, rows3]
    pin = lax.dynamic_slice_in_dim(plast, scal[0], chip, 0)
    bin_ = lax.dynamic_slice_in_dim(blast, scal[0], chip, 0)
    keep, send = pl.pallas_call(
        functools.partial(finish_body, nz, rows),
        out_shape=[in_vmem(POWERS, size, width)] * 2,
        in_specs=[pl.BlockSpec(memory_space=pltpu.SMEM)] + [vm()] * (4 + POWERS - 1),
        out_specs=[vm()] * 2,
        compiler_params=pltpu.CompilerParams(vmem_limit_bytes=LIMIT),
        name="finish",
    )(scal, local, pin, bin_, rcol2, *columns)
    recv = lax.ppermute(send, "trans", [(i, i ^ 1) for i in range(trans)])
    cols, gram = pl.pallas_call(
        gram_body,
        out_shape=[in_vmem(ncol, size, width), in_vmem(trans, 1, width)],
        in_specs=[pl.BlockSpec(memory_space=pltpu.SMEM)] + [vm()] * 3,
        out_specs=[vm()] * 2,
        scratch_shapes=[pltpu.VMEM((128, width), F32)],
        compiler_params=pltpu.CompilerParams(vmem_limit_bytes=LIMIT),
        name="gram",
    )(scal, packets.reshape(npack, size, width), keep, recv)
    beam = lax.axis_size("beam")
    gram = jnp.sum(lax.all_to_all(gram, "trans", 0, 0, tiled=True), axis=0, keepdims=True)
    gram = lax.all_to_all(jnp.broadcast_to(gram, (beam, 1, width)), "beam", 0, 0, tiled=True)
    cells = float(nx * (width // 2) * nz * beam)
    basis, factor = pl.pallas_call(
        functools.partial(basis_body, cells, rows),
        out_shape=[
            jax.ShapeDtypeStruct((ncol, size, width), F32),
            jax.ShapeDtypeStruct((2, 16, width), F32),
        ],
        in_specs=[vm(), vm()],
        out_specs=[pl.BlockSpec(memory_space=pl.ANY), vm()],
        scratch_shapes=[
            pltpu.VMEM((2, ncol * ncol, 8, width), F32),
            pltpu.VMEM((ncol, size, width), F32),
            pltpu.SemaphoreType.DMA((rows,)),
        ],
        compiler_params=pltpu.CompilerParams(vmem_limit_bytes=LIMIT),
        name="basis",
    )(gram, cols)
    return basis.reshape(ncol, rows, nz, width), factor[:, :ncol, :ncol]


def solution(mesh):
    in_specs = (P(None, "trans", "beam", None), P(), P(), P(), P("trans", "beam", None))
    out_specs = (P(None, "trans", "beam", None), P())
    return jax.shard_map(shards, mesh=mesh, in_specs=in_specs, out_specs=out_specs, check_vma=False)
```

```python
import functools

import jax
import jax.numpy as jnp
from jax import lax
from jax.experimental import pallas as pl
from jax.experimental.pallas import tpu as pltpu
from jax.sharding import PartitionSpec as P

POWERS = 4
F32 = jnp.float32
BF16 = jnp.bfloat16
LIMIT = 16 * 1024 * 1024


def split(v):
    high = v.astype(BF16)
    return high, (v - high.astype(F32)).astype(BF16)


def passed(x, by):
    peers = lax.axis_size("beam")
    return lax.ppermute(x, "beam", [(i, i + by) for i in range(peers) if 0 <= i + by < peers])


PAD = 8


def apply_local(nx, nz, width, refs, col, load, prev, halo, scale, out, bridge_ref, ready=None):
    pot_ref, kz_ref, kx_ref, wy_ref, wvec_ref = refs
    col_ref, stride = col
    out_ref, x_start, out_x = out
    out_stride = nz + PAD
    half = width // 2
    left = lax.broadcasted_iota(jnp.int32, (nz, width), 1) < half

    def product(k_ref, us):
        parts = [split(u) for u in us]
        rows = []
        for p, q in (parts[0:2], parts[2:4]):
            rows += [jnp.concatenate([p[0], q[0]], axis=1), jnp.concatenate([p[1], q[1]], axis=1)]
        got = jnp.dot(k_ref[...], jnp.concatenate(rows, axis=0), preferred_element_type=F32)
        m = got.shape[0] // 4
        outs = []
        for i in range(2):
            both = got[2 * i * m : (2 * i + 1) * m] + got[(2 * i + 1) * m : (2 * i + 2) * m]
            outs += [both[:, :width], both[:, width:]]
        return outs, parts

    def local_four(x0):
        us = [load(x_start + x0 + q) for q in range(4)]
        along_z, parts = product(kz_ref, us)
        along_y = jnp.dot(
            jnp.concatenate([jnp.concatenate(p, axis=1) for p in parts], axis=0),
            wy_ref[...],
            preferred_element_type=F32,
        )
        for q in range(4):
            x = x_start + x0 + q
            ay = along_y[q * nz : (q + 1) * nz]
            new = along_z[q] + ay[:, :width] + ay[:, width:]
            new = new + scale * optical(us[q], pot_ref[rows_of(x, nz, nz), :], left)
            if prev is not None:
                new = new - prev[0][rows_of(x, prev[1], nz), :]
            if halo is not None:
                new = with_halo(new, halo, x)
            out_ref[rows_of(x0 + q, out_stride, nz), :] = new

    if ready is None:
        repeat(out_x // 4, 8, only(lambda i: local_four(i * 4)), 0)
    else:
        for h in range(2):
            ready(h)
            repeat(out_x // 8, 8, only(lambda i, h=h: local_four((h * out_x // 8 + i) * 4)), 0)

    def across_four(i, bridge):
        z0 = i * 4
        us = [col_ref[pl.ds(z0 + q, nx, stride=stride), :] for q in range(4)]
        along_x, _ = product(kx_ref, us)
        for q in range(4):
            at = pl.ds(z0 + q, out_x, stride=out_stride)
            new = out_ref[at, :] + along_x[q]
            out_ref[at, :] = new
            if bridge_ref is not None:
                bridge = bridge + wvec_ref[pl.ds(z0 + q, 1), :] * new
        return bridge

    bridge = repeat(nz // 4, 8, across_four, jnp.zeros((out_x, width), F32))
    if bridge_ref is not None:
        bridge_ref[...] = bridge


def rows_of(x, stride, nz):
    return pl.ds(pl.multiple_of(x * stride, 8), nz)


def optical(u, pot, left):
    half = u.shape[-1] // 2
    turned = pltpu.roll(pot, half, 1)
    return jnp.where(left, pot, turned) * u + jnp.where(left, turned, -pot) * pltpu.roll(u, half, 1)


def with_halo(u, halo, x):
    column_ref, plane_ref, sum_ref, scale = halo
    top = lax.broadcasted_iota(jnp.int32, (8, u.shape[-1]), 0) == 0
    u = u + column_ref[...] * (scale * plane_ref[pl.ds(x, 1), :])
    head = u[0:8] + jnp.where(top, scale * sum_ref[pl.ds(x, 1), :], 0.0)
    return jnp.concatenate([head, u[8:]], axis=0)


def repeat(count, unroll, body, carry):
    unroll = min(unroll, count)

    def some(i, carry):
        for q in range(unroll):
            carry = body(i * unroll + q, carry)
        return carry

    return lax.fori_loop(0, count // unroll, some, carry)


def only(body):
    def with_carry(i, carry):
        body(i)
        return carry

    return with_carry


def copies_body(packets_ref, sent_ref, sems):
    npack = packets_ref.shape[0]
    copies = [
        pltpu.make_async_copy(packets_ref, sent_ref.at[pl.ds(i * npack, npack)], sems.at[i])
        for i in range(sent_ref.shape[0] // npack)
    ]
    for copy in copies:
        copy.start()
    for copy in copies:
        copy.wait()


def planes_body(nz, packets_ref, pot_ref, wvec_ref, kvec_ref, mvec_ref, first_ref, bridge_ref, zrest_ref, brest_ref):
    npack, size, width = packets_ref.shape
    rows = size // nz
    left = lax.broadcasted_iota(jnp.int32, (nz, width), 1) < width // 2
    for p in range(npack):
        for x in range(rows):
            u = packets_ref[p, x * nz : (x + 1) * nz, :]
            v = optical(u, pot_ref[x * nz : (x + 1) * nz, :], left)
            at = slice(p * rows + x, p * rows + x + 1)
            first_ref[at, :] = u[0:1]
            bridge_ref[at, :] = jnp.sum(wvec_ref[...] * u, axis=0, keepdims=True)
            zrest_ref[at, :] = v[0:1] + jnp.sum(kvec_ref[...] * u, axis=0, keepdims=True)
            brest_ref[at, :] = jnp.sum(wvec_ref[...] * v + mvec_ref[...] * u, axis=0, keepdims=True)


def element_matrix(scal, ek):
    nz = ek.shape[0] - 1
    r = lax.broadcasted_iota(jnp.int32, (nz, nz), 0)
    c = lax.broadcasted_iota(jnp.int32, (nz, nz), 1)
    corner = (r == 0) & (c == 0) & (scal[2] > 0)
    return ek[0:nz, 0:nz] + jnp.where(corner, ek[nz : nz + 1, nz : nz + 1], 0.0)


def vectors_body(scal, ek_ref, rcol, kvec, mvec, coef):
    nz, width = rcol.shape
    kz = element_matrix(scal, ek_ref)
    edge_vectors(ek_ref, rcol, coef)
    kvec[...] = jnp.broadcast_to(kz[:, 0:1], (nz, width))
    bridge = ek_ref[nz : nz + 1, 0:nz]
    mvec[...] = jnp.broadcast_to(jnp.sum(kz * bridge, axis=1, keepdims=True), (nz, width))


def edge_vectors(ek_ref, rcol, coef):
    nz, width = rcol.shape
    rcol[...] = jnp.broadcast_to(ek_ref[0:nz, nz : nz + 1], (nz, width))
    coef[...] = jnp.zeros_like(coef)
    coef[0:1, :] = rcol[0:1, :]
    coef[1:2, :] = jnp.sum(rcol[...] * rcol[...], axis=0, keepdims=True)


def matrices(scal, kx_ref, ky_ref, ek_ref, kz1, kx1, wy1, kz2, kx2, wy2, kx4, kyd):
    chip = kx4.shape[0] // 4

    def split_wide(k):
        high = k.astype(BF16).astype(F32)
        return high, k - high

    def left_weights(k):
        high, low = split_wide(k)
        none = jnp.zeros_like(high)
        block = jnp.concatenate(
            [jnp.concatenate([high, high], axis=1), jnp.concatenate([low, none], axis=1)], axis=0
        )
        none = jnp.zeros_like(block)
        return jnp.concatenate(
            [jnp.concatenate([block, none], axis=1), jnp.concatenate([none, block], axis=1)], axis=0
        )

    for one, two, k in ((kz1, kz2, element_matrix(scal, ek_ref)), (kx1, kx2, kx_ref[...])):
        block = left_weights(k)
        one[...] = block.astype(BF16)
        two[...] = (2.0 * block).astype(BF16)
    kx4[...] = left_weights(2.0 * kx_ref[pl.ds(pl.multiple_of(scal[0], 8), chip), :]).astype(BF16)
    ky = ky_ref[...]
    none = jnp.zeros_like(ky)
    ky = jnp.concatenate(
        [jnp.concatenate([ky, none], axis=1), jnp.concatenate([none, ky], axis=1)], axis=0
    )
    kyd[...] = ky
    high, low = split_wide(ky)
    block = jnp.concatenate(
        [jnp.concatenate([high, low], axis=1), jnp.concatenate([high, jnp.zeros_like(low)], axis=1)],
        axis=0,
    )
    wy1[...] = block.astype(BF16)
    wy2[...] = (2.0 * block).astype(BF16)


def edges_body(scale, first_ref, bridge_ref, pin_ref, bin_ref, coef_ref, out_first, out_bridge):
    head, square = coef_ref[0:1, :], coef_ref[1:2, :]
    pin, bin_ = scale * pin_ref[...], scale * bin_ref[...]
    out_first[...] = first_ref[...] + head * pin + bin_
    out_bridge[...] = bridge_ref[...] + square * pin + head * bin_


def pair_body(nx, nz, width, chip, scal, cur_ref, gathered_ref, pot_hbm, kx_hbm, ky_hbm, ek_hbm, *refs):
    one_ref, two_ref, first_ref, bridge_ref, rows1_ref, rows2_ref, pot_ref = refs[:7]
    kz2, kx2, wy2, kx4, rcol, coef = refs[7:13]
    col_ref, planes_ref, halo_ref, sems, kx_ref, ky_raw, ek_ref, kz1, kx1, wy1, ky_ref = refs[13:]
    stride = nz + PAD
    small = [
        pltpu.make_async_copy(src, dst, sems.at[2 + i])
        for i, (src, dst) in enumerate(((kx_hbm, kx_ref), (ky_hbm, ky_raw), (ek_hbm, ek_ref)))
    ]
    for copy in small:
        copy.start()
    part = nx * nz // 2
    copies = [
        pltpu.make_async_copy(
            pot_hbm.at[pl.ds(h * part, part), :], pot_ref.at[pl.ds(h * part, part), :], sems.at[h]
        )
        for h in range(2)
    ]
    for copy in copies:
        copy.start()

    trans, planes, each, _ = gathered_ref.shape
    each = each // 2
    for t in range(trans):
        for q in range(planes):
            planes_ref[q, t * each : (t + 1) * each, :] = gathered_ref[
                t, q, pl.ds(pl.multiple_of(scal[1] * each, 8), each), :
            ]
    for copy in small:
        copy.wait()
    matrices(scal, kx_ref, ky_raw, ek_ref, kz1, kx1, wy1, kz2, kx2, wy2, kx4, ky_ref)
    edge_vectors(ek_ref, rcol, coef)
    precise = lax.Precision.HIGHEST
    for q in range(2):
        plane = planes_ref[q]
        moved = jnp.dot(kx_ref[...], plane, precision=precise, preferred_element_type=F32)
        moved = moved + jnp.dot(plane, ky_ref[...], precision=precise, preferred_element_type=F32)
        halo_ref[q] = moved + planes_ref[2 + q]

    def packed(x):
        u = cur_ref[rows_of(x, nz, nz), :]
        col_ref[rows_of(x, stride, nz), :] = u
        return u

    apply_local(
        nx, nz, width, (pot_ref, kz1, kx1, wy1, rcol), (col_ref, stride), packed, None,
        (rcol, planes_ref.at[0], planes_ref.at[1], 1.0), 1.0, (one_ref, 0, nx), None,
        ready=lambda h: copies[h].wait(),
    )
    apply_local(
        nx, nz, width, (pot_ref, kz2, kx2, wy2, rcol), (one_ref, stride),
        lambda x: one_ref[rows_of(x, stride, nz), :], (cur_ref, nz),
        (rcol, halo_ref.at[0], halo_ref.at[1], 2.0), 2.0, (two_ref, 0, nx), bridge_ref,
    )
    first_ref[...] = two_ref[pl.ds(0, nx, stride=stride), :]
    for ref, rows_ref in ((one_ref, rows1_ref), (two_ref, rows2_ref)):
        for q in range(chip):
            rows_ref[q * nz : (q + 1) * nz, :] = ref[rows_of(scal[0] + q, stride, nz), :]


def third_body(nx, nz, width, cur_ref, prev_ref, pot_ref, kz, kx, wy, rcol, out_ref, first_ref, bridge_ref):
    stride = nz + PAD
    apply_local(
        nx, nz, width, (pot_ref, kz, kx, wy, rcol), (cur_ref, stride),
        lambda x: cur_ref[rows_of(x, stride, nz), :], (prev_ref, stride), None, 2.0,
        (out_ref, 0, nx), bridge_ref,
    )
    first_ref[...] = out_ref[pl.ds(0, nx, stride=stride), :]


def fourth_body(nx, nz, width, chip, scal, cur_ref, pin_ref, bin_ref, prev_ref, pot_ref, *refs):
    kz, kx, wy, rcol, out_ref, rows_ref, col_ref = refs
    stride = nz + PAD

    def complete(x):
        u = with_halo(cur_ref[rows_of(x, stride, nz), :], (rcol, pin_ref, bin_ref, 2.0), x)
        col_ref[rows_of(x, stride, nz), :] = u

    repeat(nx, 16, only(complete), 0)
    for q in range(chip):
        rows_ref[q * nz : (q + 1) * nz, :] = col_ref[rows_of(scal[0] + q, stride, nz), :]
    apply_local(
        nx, nz, width, (pot_ref, kz, kx, wy, rcol), (col_ref, stride),
        lambda x: col_ref[rows_of(x, stride, nz), :], (prev_ref, stride), None, 2.0,
        (out_ref, scal[0], chip), None,
    )


def vm():
    return pl.BlockSpec(memory_space=pltpu.VMEM)


def in_vmem(*shape):
    return pltpu.VMEM(shape, F32)


def call(name, body, outs, *ins, scal=None, scratch=(), cost=4, away=()):
    specs = [pl.BlockSpec(memory_space=pltpu.HBM) if i in away else vm() for i in range(len(ins))]
    ins = tuple(
        pltpu.with_memory_space_constraint(x, pltpu.HBM) if i in away else x for i, x in enumerate(ins)
    )
    if scal is not None:
        specs = [pl.BlockSpec(memory_space=pltpu.SMEM)] + specs
        ins = (scal,) + ins
    return pl.pallas_call(
        body,
        out_shape=outs,
        in_specs=specs,
        out_specs=[vm()] * len(outs),
        scratch_shapes=list(scratch),
        compiler_params=pltpu.CompilerParams(vmem_limit_bytes=LIMIT),
        cost_estimate=pl.CostEstimate(
            flops=cost * 10**9, bytes_accessed=2 * cost * 10**6, transcendentals=0
        ),
        name=name,
    )(*ins)


def finish_body(nz, rows, scal, last_ref, pin_ref, bin_ref, rcol_ref, *refs):
    cols = refs[: POWERS - 1]
    keep_ref, send_ref = refs[POWERS - 1 :]
    core = scal[1]
    size = rows * nz
    halo = (rcol_ref, pin_ref, bin_ref, 2.0)
    for ref, where in ((keep_ref, core), (send_ref, 1 - core)):
        at = pl.ds(pl.multiple_of(where * size, size), size)
        for k in range(POWERS - 1):
            ref[k] = cols[k][at, :]
        for r in range(rows):
            x = where * rows + r
            u = with_halo(last_ref[rows_of(x, nz + PAD, nz), :], halo, scal[0] + x)
            ref[POWERS - 1, r * nz : (r + 1) * nz, :] = u


def gram_body(scal, packets_ref, keep_ref, recv_ref, cols_ref, gram_ref, acc_ref):
    core = scal[1]
    ncol, size, width = cols_ref.shape
    npow = ncol // 2
    half = width // 2
    cols_ref[0] = packets_ref[0]
    cols_ref[npow] = packets_ref[1]
    for k in range(npow - 1):
        cols_ref[core * npow + 1 + k] = keep_ref[k]
        cols_ref[(1 - core) * npow + 1 + k] = recv_ref[k]
    acc_ref[...] = jnp.zeros_like(acc_ref)
    sign = jnp.where(lax.broadcasted_iota(jnp.int32, (8, width), 1) < half, 1.0, -1.0)
    first, second = list(range(npow)), list(range(npow, ncol))
    groups = [
        [(a, b) for a in first for b in first if a <= b],
        [(a, b) for a in second for b in second if a <= b],
        [(a, b) for a in first for b in second[:3]],
        [(a, b) for a in first for b in second[3:]],
    ]
    unroll = 16
    for pairs in groups:
        used = sorted({c for pair in pairs for c in pair})
        turned = sorted({b for a, b in pairs if a != b})

        def chunk(i, sums, pairs=pairs, used=used, turned=turned):
            sums = list(sums)
            for q in range(unroll):
                at = pl.ds(pl.multiple_of((i * unroll + q) * 8, 8), 8)
                v = {c: cols_ref[c, at, :] for c in used}
                t = {c: pltpu.roll(v[c], half, 1) for c in turned}
                n = 0
                for a, b in pairs:
                    sums[n] = sums[n] + v[a] * v[b]
                    n += 1
                    if a != b:
                        sums[n] = sums[n] + v[a] * t[b]
                        n += 1
            return tuple(sums)

        count = sum(1 if a == b else 2 for a, b in pairs)
        sums = lax.fori_loop(
            0, size // (8 * unroll), chunk, tuple(jnp.zeros((8, width), F32) for _ in range(count))
        )
        n = 0
        for a, b in pairs:
            acc_ref[a * ncol + b : a * ncol + b + 1, :] = jnp.sum(sums[n], axis=0, keepdims=True)
            n += 1
            if a != b:
                acc_ref[b * ncol + a : b * ncol + a + 1, :] = jnp.sum(
                    sums[n] * sign, axis=0, keepdims=True
                )
                n += 1
    row = jnp.sum(acc_ref[...].T, axis=0, keepdims=True)
    gram_ref[...] = jnp.broadcast_to(row[None], gram_ref.shape)


def basis_body(cells, rows, gram_ref, cols_ref, basis_ref, factor_ref, coef_ref, out_ref, sems):
    ncol, size, width = cols_ref.shape
    half = width // 2
    row = jnp.sum(gram_ref[...], axis=0) * (1.0 / cells)
    r = lax.broadcasted_iota(jnp.int32, (16, width), 0)
    c = lax.broadcasted_iota(jnp.int32, (16, width), 1)
    packed = jnp.zeros((16, width), F32)
    for j in range(ncol):
        moved = row if j == 0 else pltpu.roll(row, width - ncol * j, 1)
        packed = jnp.where(r == j, moved, packed)
    turned = jnp.concatenate([packed, jnp.zeros((width - 16, width), F32)], axis=0).T[:16]
    inside = (r < ncol) & (c < ncol)
    re = jnp.where(inside, jnp.where(r <= c, packed, turned), 0.0)
    im = jnp.where(inside & (r != c), jnp.where(r < c, turned, -packed), 0.0)
    re = jnp.where(c == r + 16, 1.0, re)
    up_re = jnp.zeros((16, width), F32)
    up_im = jnp.zeros((16, width), F32)
    for j in range(ncol):
        pivot = jnp.sqrt(re[j : j + 1, j : j + 1])
        inverse = 1.0 / pivot
        row_re = re[j : j + 1, :] * inverse
        row_im = im[j : j + 1, :] * inverse
        col_re = re[:, j : j + 1] * inverse
        col_im = im[:, j : j + 1] * inverse
        up_re = jnp.where(r == j, row_re, up_re)
        up_im = jnp.where(r == j, row_im, up_im)
        below = r > j
        re = re - jnp.where(below, col_re * row_re - col_im * row_im, 0.0)
        im = im - jnp.where(below, col_re * row_im + col_im * row_re, 0.0)
    keep = (c >= r) & (c < ncol)
    factor_ref[0] = jnp.where(keep, up_re, 0.0)
    factor_ref[1] = jnp.where(keep & (c > r), up_im, 0.0)
    sign = jnp.where(lax.broadcasted_iota(jnp.int32, (8, width), 1) < half, 1.0, -1.0)
    for k in range(ncol):
        for i in range(k + 1):
            coef_ref[0, k * ncol + i] = jnp.broadcast_to(up_re[k : k + 1, 16 + i : 17 + i], (8, width))
            coef_ref[1, k * ncol + i] = (
                jnp.broadcast_to(up_im[k : k + 1, 16 + i : 17 + i], (8, width)) * sign
            )
    group = 4
    each = size // rows
    copies = []
    for r in range(rows):
        for start in range(r * each, (r + 1) * each, 8 * group):
            slots = [slice(start + 8 * g, start + 8 * g + 8) for g in range(group)]
            v = [[cols_ref[i, s, :] for s in slots] for i in range(ncol)]
            t = [[pltpu.roll(x, half, 1) for x in xs] for xs in v]
            for k in range(ncol):
                total = [None] * group
                for i in range(k + 1):
                    re = coef_ref[0, k * ncol + i]
                    im = coef_ref[1, k * ncol + i]
                    for g in range(group):
                        term = re * v[i][g]
                        if i < k:
                            term = term + im * t[i][g]
                        total[g] = term if total[g] is None else total[g] + term
                for g in range(group):
                    out_ref[k, slots[g], :] = total[g]
        part = pl.ds(r * each, each)
        copy = pltpu.make_async_copy(out_ref.at[:, part, :], basis_ref.at[:, part, :], sems.at[r])
        copy.start()
        copies.append(copy)
    for copy in copies:
        copy.wait()


def shards(packets, kinetic_x, kinetic_y, element_kinetic, potential):
    npack, rows, nz, width = packets.shape
    trans = lax.axis_size("trans")
    nx = rows * trans
    ncol = npack * (POWERS + 1)
    me = lax.axis_index("trans")
    core = me % 2
    chip = 2 * rows
    scal = jnp.stack([(me // 2) * chip, core, lax.axis_index("beam")]).astype(jnp.int32)

    size = rows * nz
    flat = packets.reshape(npack, size, width)
    mine = potential.reshape(size, width)
    pot = lax.all_gather(mine, "trans", axis=0, tiled=True)
    sent = pl.pallas_call(
        copies_body,
        out_shape=jax.ShapeDtypeStruct((trans, size, width), F32),
        in_specs=[vm()],
        out_specs=pl.BlockSpec(memory_space=pl.ANY),
        scratch_shapes=[pltpu.SemaphoreType.DMA((trans // npack,))],
        compiler_params=pltpu.CompilerParams(vmem_limit_bytes=LIMIT),
        name="copies",
    )(flat)
    cur = lax.all_to_all(sent, "trans", 0, 0, tiled=True).reshape(nx * nz, width)
    sent, flat_late, mine_late, ek_late = lax.optimization_barrier(
        (sent, flat, mine, element_kinetic)
    )

    def half_wide(*shape):
        return pltpu.VMEM(shape, BF16)

    square, column = half_wide(4 * nz, 4 * nz), in_vmem(nz, width)
    across = half_wide(4 * nx, 4 * nx)
    wide = half_wide(2 * width, 2 * width)
    rcol, kvec, mvec, coef = call(
        "vectors", vectors_body, [column, column, column, in_vmem(8, width)], ek_late, scal=scal, cost=1
    )

    plane = in_vmem(npack * rows, width)
    first, bridge, zrest, brest = call(
        "planes", functools.partial(planes_body, nz), [plane] * 4,
        flat_late, mine_late, rcol, kvec, mvec, cost=1,
    )
    pin, bin_ = passed(first, -1), passed(bridge, 1)
    pnext, bnext = call(
        "edges", functools.partial(edges_body, 1.0), [plane] * 2, zrest, brest, pin, bin_, coef, cost=1
    )
    planes = jnp.stack([pin, bin_, passed(pnext, -1), passed(bnext, 1)])
    planes = lax.all_gather(planes, "trans")

    full, edge = in_vmem(nx * (nz + PAD), width), in_vmem(nx, width)
    here = in_vmem(chip * nz, width)
    col1, col2, first, bridge, rows1, rows2, pot, kz2, kx2, wy2, kx4, rcol, coef = call(
        "pair", functools.partial(pair_body, nx, nz, width, chip),
        [full, full, edge, edge, here, here, in_vmem(nx * nz, width),
         square, across, wide, half_wide(4 * chip, 4 * nx), column, in_vmem(8, width)],
        cur, planes, pot, kinetic_x, kinetic_y, element_kinetic,
        scal=scal, cost=8, away=(2, 3, 4, 5),
        scratch=[full, in_vmem(4, nx, width), in_vmem(2, nx, width), pltpu.SemaphoreType.DMA((5,)),
                 in_vmem(*kinetic_x.shape), in_vmem(*kinetic_y.shape), in_vmem(*element_kinetic.shape),
                 square, across, wide, in_vmem(width, width)],
    )
    pin, bin_ = passed(first, -1), passed(bridge, 1)
    col3, first, bridge = call(
        "third", functools.partial(third_body, nx, nz, width), [full, edge, edge],
        col2, col1, pot, kz2, kx2, wy2, rcol,
    )
    first, bridge = call(
        "edges", functools.partial(edges_body, 2.0), [edge] * 2, first, bridge, pin, bin_, coef, cost=1
    )
    plast, blast = passed(first, -1), passed(bridge, 1)
    local, rows3 = call(
        "fourth", functools.partial(fourth_body, nx, nz, width, chip),
        [in_vmem(chip * (nz + PAD), width), here],
        col3, pin, bin_, col2, pot, kz2, kx4, wy2, rcol,
        scal=scal, scratch=[full], cost=2,
    )
    columns = [rows1, rows2, rows3]
    keep, send = pl.pallas_call(
        functools.partial(finish_body, nz, rows),
        out_shape=[in_vmem(POWERS, size, width)] * 2,
        in_specs=[pl.BlockSpec(memory_space=pltpu.SMEM)] + [vm()] * (4 + POWERS - 1),
        out_specs=[vm()] * 2,
        compiler_params=pltpu.CompilerParams(vmem_limit_bytes=LIMIT),
        name="finish",
    )(scal, local, plast, blast, rcol, *columns)
    recv = lax.ppermute(send, "trans", [(i, i ^ 1) for i in range(trans)])
    cols, gram = pl.pallas_call(
        gram_body,
        out_shape=[in_vmem(ncol, size, width), in_vmem(trans, 1, width)],
        in_specs=[pl.BlockSpec(memory_space=pltpu.SMEM)] + [vm()] * 3,
        out_specs=[vm()] * 2,
        scratch_shapes=[pltpu.VMEM((128, width), F32)],
        compiler_params=pltpu.CompilerParams(vmem_limit_bytes=LIMIT),
        name="gram",
    )(scal, packets.reshape(npack, size, width), keep, recv)
    beam = lax.axis_size("beam")
    gram = jnp.sum(lax.all_to_all(gram, "trans", 0, 0, tiled=True), axis=0, keepdims=True)
    gram = lax.all_to_all(jnp.broadcast_to(gram, (beam, 1, width)), "beam", 0, 0, tiled=True)
    cells = float(nx * (width // 2) * nz * beam)
    basis, factor = pl.pallas_call(
        functools.partial(basis_body, cells, rows),
        out_shape=[
            jax.ShapeDtypeStruct((ncol, size, width), F32),
            jax.ShapeDtypeStruct((2, 16, width), F32),
        ],
        in_specs=[vm(), vm()],
        out_specs=[pl.BlockSpec(memory_space=pl.ANY), vm()],
        scratch_shapes=[
            pltpu.VMEM((2, ncol * ncol, 8, width), F32),
            pltpu.VMEM((ncol, size, width), F32),
            pltpu.SemaphoreType.DMA((rows,)),
        ],
        compiler_params=pltpu.CompilerParams(vmem_limit_bytes=LIMIT),
        name="basis",
    )(gram, cols)
    return basis.reshape(ncol, rows, nz, width), factor[:, :ncol, :ncol]


def solution(mesh):
    in_specs = (P(None, "trans", "beam", None), P(), P(), P(), P("trans", "beam", None))
    out_specs = (P(None, "trans", "beam", None), P())
    return jax.shard_map(shards, mesh=mesh, in_specs=in_specs, out_specs=out_specs, check_vma=False)
```

```python
import functools

import jax
import jax.numpy as jnp
from jax import lax
from jax.experimental import pallas as pl
from jax.experimental.pallas import tpu as pltpu
from jax.sharding import PartitionSpec as P

POWERS = 4
F32 = jnp.float32
BF16 = jnp.bfloat16
LIMIT = 16 * 1024 * 1024


def split(v):
    high = v.astype(BF16)
    return high, (v - high.astype(F32)).astype(BF16)


def passed(x, by):
    peers = lax.axis_size("beam")
    return lax.ppermute(x, "beam", [(i, i + by) for i in range(peers) if 0 <= i + by < peers])


PAD = 8


def apply_local(nx, nz, width, refs, col, load, prev, halo, scale, out, bridge_ref, ready=None):
    pot_ref, kz_ref, kx_ref, wy_ref, wvec_ref = refs
    col_ref, stride = col
    out_ref, x_start, out_x = out
    out_stride = nz + PAD
    half = width // 2
    left = lax.broadcasted_iota(jnp.int32, (nz, width), 1) < half

    def product(k_ref, us):
        parts = [split(u) for u in us]
        rows = []
        for p, q in (parts[0:2], parts[2:4]):
            rows += [jnp.concatenate([p[0], q[0]], axis=1), jnp.concatenate([p[1], q[1]], axis=1)]
        got = jnp.dot(k_ref[...], jnp.concatenate(rows, axis=0), preferred_element_type=F32)
        m = got.shape[0] // 4
        outs = []
        for i in range(2):
            both = got[2 * i * m : (2 * i + 1) * m] + got[(2 * i + 1) * m : (2 * i + 2) * m]
            outs += [both[:, :width], both[:, width:]]
        return outs, parts

    def local_four(x0):
        us = [load(x_start + x0 + q) for q in range(4)]
        along_z, parts = product(kz_ref, us)
        along_y = jnp.dot(
            jnp.concatenate([jnp.concatenate(p, axis=1) for p in parts], axis=0),
            wy_ref[...],
            preferred_element_type=F32,
        )
        for q in range(4):
            x = x_start + x0 + q
            ay = along_y[q * nz : (q + 1) * nz]
            new = along_z[q] + ay[:, :width] + ay[:, width:]
            new = new + scale * optical(us[q], pot_ref[rows_of(x, nz, nz), :], left)
            if prev is not None:
                new = new - prev[0][rows_of(x, prev[1], nz), :]
            if halo is not None:
                new = with_halo(new, halo, x)
            out_ref[rows_of(x0 + q, out_stride, nz), :] = new

    if ready is None:
        repeat(out_x // 4, 8, only(lambda i: local_four(i * 4)), 0)
    else:
        for h in range(2):
            ready(h)
            repeat(out_x // 8, 8, only(lambda i, h=h: local_four((h * out_x // 8 + i) * 4)), 0)

    def across_four(i, bridge):
        z0 = i * 4
        us = [col_ref[pl.ds(z0 + q, nx, stride=stride), :] for q in range(4)]
        along_x, _ = product(kx_ref, us)
        for q in range(4):
            at = pl.ds(z0 + q, out_x, stride=out_stride)
            new = out_ref[at, :] + along_x[q]
            out_ref[at, :] = new
            if bridge_ref is not None:
                bridge = bridge + wvec_ref[pl.ds(z0 + q, 1), :] * new
        return bridge

    bridge = repeat(nz // 4, 8, across_four, jnp.zeros((out_x, width), F32))
    if bridge_ref is not None:
        bridge_ref[...] = bridge


def rows_of(x, stride, nz):
    return pl.ds(pl.multiple_of(x * stride, 8), nz)


def optical(u, pot, left):
    half = u.shape[-1] // 2
    turned = pltpu.roll(pot, half, 1)
    return jnp.where(left, pot, turned) * u + jnp.where(left, turned, -pot) * pltpu.roll(u, half, 1)


def with_halo(u, halo, x):
    column_ref, plane_ref, sum_ref, scale = halo
    top = lax.broadcasted_iota(jnp.int32, (8, u.shape[-1]), 0) == 0
    u = u + column_ref[...] * (scale * plane_ref[pl.ds(x, 1), :])
    head = u[0:8] + jnp.where(top, scale * sum_ref[pl.ds(x, 1), :], 0.0)
    return jnp.concatenate([head, u[8:]], axis=0)


def repeat(count, unroll, body, carry):
    unroll = min(unroll, count)

    def some(i, carry):
        for q in range(unroll):
            carry = body(i * unroll + q, carry)
        return carry

    return lax.fori_loop(0, count // unroll, some, carry)


def only(body):
    def with_carry(i, carry):
        body(i)
        return carry

    return with_carry


def copies_body(packets_ref, sent_ref, sems):
    npack = packets_ref.shape[0]
    copies = [
        pltpu.make_async_copy(packets_ref, sent_ref.at[pl.ds(i * npack, npack)], sems.at[i])
        for i in range(sent_ref.shape[0] // npack)
    ]
    for copy in copies:
        copy.start()
    for copy in copies:
        copy.wait()


def planes_body(nz, packets_ref, pot_ref, wvec_ref, kvec_ref, mvec_ref, left_ref, right_ref, first_ref, bridge_ref):
    npack, size, width = packets_ref.shape
    rows = size // nz
    count = npack * rows
    left = lax.broadcasted_iota(jnp.int32, (nz, width), 1) < width // 2
    for p in range(npack):
        for x in range(rows):
            u = packets_ref[p, x * nz : (x + 1) * nz, :]
            v = optical(u, pot_ref[x * nz : (x + 1) * nz, :], left)
            n = p * rows + x
            left_ref[n : n + 1, :] = u[0:1]
            right_ref[n : n + 1, :] = jnp.sum(wvec_ref[...] * u, axis=0, keepdims=True)
            left_ref[count + n : count + n + 1, :] = v[0:1] + jnp.sum(
                kvec_ref[...] * u, axis=0, keepdims=True
            )
            right_ref[count + n : count + n + 1, :] = jnp.sum(
                wvec_ref[...] * v + mvec_ref[...] * u, axis=0, keepdims=True
            )
    first_ref[...] = left_ref[0:count, :]
    bridge_ref[...] = right_ref[0:count, :]


def element_matrix(scal, ek):
    nz = ek.shape[0] - 1
    r = lax.broadcasted_iota(jnp.int32, (nz, nz), 0)
    c = lax.broadcasted_iota(jnp.int32, (nz, nz), 1)
    corner = (r == 0) & (c == 0) & (scal[2] > 0)
    return ek[0:nz, 0:nz] + jnp.where(corner, ek[nz : nz + 1, nz : nz + 1], 0.0)


def vectors_body(scal, ek_ref, rcol, kvec, mvec, coef):
    nz, width = rcol.shape
    kz = element_matrix(scal, ek_ref)
    rcol[...] = jnp.broadcast_to(ek_ref[0:nz, nz : nz + 1], (nz, width))
    kvec[...] = jnp.broadcast_to(kz[:, 0:1], (nz, width))
    bridge = ek_ref[nz : nz + 1, 0:nz]
    mvec[...] = jnp.broadcast_to(jnp.sum(kz * bridge, axis=1, keepdims=True), (nz, width))
    coef[...] = jnp.zeros_like(coef)
    coef[0:1, :] = rcol[0:1, :]
    coef[1:2, :] = jnp.sum(rcol[...] * rcol[...], axis=0, keepdims=True)


def matrices(scal, kx_ref, ky_ref, ek_ref, kz1, kx1, wy1, kz2, kx2, wy2, kx4, kyd):
    chip = kx4.shape[0] // 4

    def split_wide(k):
        high = k.astype(BF16).astype(F32)
        return high, k - high

    def left_weights(k):
        high, low = split_wide(k)
        none = jnp.zeros_like(high)
        block = jnp.concatenate(
            [jnp.concatenate([high, high], axis=1), jnp.concatenate([low, none], axis=1)], axis=0
        )
        none = jnp.zeros_like(block)
        return jnp.concatenate(
            [jnp.concatenate([block, none], axis=1), jnp.concatenate([none, block], axis=1)], axis=0
        )

    for one, two, k in ((kz1, kz2, element_matrix(scal, ek_ref)), (kx1, kx2, kx_ref[...])):
        block = left_weights(k)
        one[...] = block.astype(BF16)
        two[...] = (2.0 * block).astype(BF16)
    kx4[...] = left_weights(2.0 * kx_ref[pl.ds(pl.multiple_of(scal[0], 8), chip), :]).astype(BF16)
    ky = ky_ref[...]
    none = jnp.zeros_like(ky)
    ky = jnp.concatenate(
        [jnp.concatenate([ky, none], axis=1), jnp.concatenate([none, ky], axis=1)], axis=0
    )
    kyd[...] = ky
    high, low = split_wide(ky)
    block = jnp.concatenate(
        [jnp.concatenate([high, low], axis=1), jnp.concatenate([high, jnp.zeros_like(low)], axis=1)],
        axis=0,
    )
    wy1[...] = block.astype(BF16)
    wy2[...] = (2.0 * block).astype(BF16)


def edge_rests(scal, left_ref, right_ref, left2_ref, right2_ref, first_ref, bridge_ref, coef_ref):
    count = left2_ref.shape[0]
    head, square = coef_ref[0:1, :], coef_ref[1:2, :]
    has_right = jnp.where(scal[2] < scal[3] - 1, 1.0, 0.0)
    has_left = jnp.where(scal[2] > 0, 1.0, 0.0)
    plane = left_ref[count : 2 * count, :] + head * left2_ref[...] + has_right * bridge_ref[...]
    bridge = (
        right_ref[count : 2 * count, :] + head * right2_ref[...] + (has_left * square) * first_ref[...]
    )
    return plane, bridge


def edges_body(scal, left_ref, right_ref, left2_ref, right2_ref, first_ref, bridge_ref, coef_ref, out_ref):
    count = left2_ref.shape[0]
    plane, bridge = edge_rests(
        scal, left_ref, right_ref, left2_ref, right2_ref, first_ref, bridge_ref, coef_ref
    )
    out_ref[0] = left_ref[0:count, :]
    out_ref[1] = right_ref[0:count, :]
    out_ref[2] = plane
    out_ref[3] = bridge


def transverse(kx_ref, ky_ref, plane):
    precise = lax.Precision.HIGHEST
    moved = jnp.dot(kx_ref[...], plane, precision=precise, preferred_element_type=F32)
    return moved + jnp.dot(plane, ky_ref[...], precision=precise, preferred_element_type=F32)


def pair_body(nx, nz, width, chip, scal, cur_ref, gathered_ref, pot_hbm, kx_hbm, ky_hbm, ek_hbm, *refs):
    one_ref, two_ref, left_ref, right_ref, first_ref, bridge_ref, rows1_ref, rows2_ref = refs[:8]
    pot_ref, kz2, kx2, wy2, kx4, kx_ref, ky_ref, halo_ref = refs[8:16]
    rcol, kvec, mvec, coef = refs[16:20]
    col_ref, planes_ref, sems, ky_raw, ek_ref, kz1, kx1, wy1 = refs[20:]
    stride = nz + PAD
    small = [
        pltpu.make_async_copy(src, dst, sems.at[2 + i])
        for i, (src, dst) in enumerate(((kx_hbm, kx_ref), (ky_hbm, ky_raw), (ek_hbm, ek_ref)))
    ]
    for copy in small:
        copy.start()
    part = nx * nz // 2
    copies = [
        pltpu.make_async_copy(
            pot_hbm.at[pl.ds(h * part, part), :], pot_ref.at[pl.ds(h * part, part), :], sems.at[h]
        )
        for h in range(2)
    ]
    for copy in copies:
        copy.start()

    trans, planes, each, _ = gathered_ref.shape
    each = each // 2
    for t in range(trans):
        for q in range(planes):
            planes_ref[q, t * each : (t + 1) * each, :] = gathered_ref[
                t, q, pl.ds(pl.multiple_of(scal[1] * each, 8), each), :
            ]
    for copy in small:
        copy.wait()
    matrices(scal, kx_ref, ky_raw, ek_ref, kz1, kx1, wy1, kz2, kx2, wy2, kx4, ky_ref)
    vectors_body(scal, ek_ref, rcol, kvec, mvec, coef)
    for q in range(2):
        halo_ref[q] = transverse(kx_ref, ky_ref, planes_ref[q]) + planes_ref[2 + q]

    def packed(x):
        u = cur_ref[rows_of(x, nz, nz), :]
        col_ref[rows_of(x, stride, nz), :] = u
        return u

    apply_local(
        nx, nz, width, (pot_ref, kz1, kx1, wy1, rcol), (col_ref, stride), packed, None,
        (rcol, planes_ref.at[0], planes_ref.at[1], 1.0), 1.0, (one_ref, 0, nx), None,
        ready=lambda h: copies[h].wait(),
    )
    apply_local(
        nx, nz, width, (pot_ref, kz2, kx2, wy2, rcol), (one_ref, stride),
        lambda x: one_ref[rows_of(x, stride, nz), :], (cur_ref, nz),
        (rcol, halo_ref.at[0], halo_ref.at[1], 2.0), 2.0, (two_ref, 0, nx), bridge_ref,
    )
    first = two_ref[pl.ds(0, nx, stride=stride), :]
    first_ref[...] = first
    left_ref[0:nx, :] = first
    right_ref[0:nx, :] = bridge_ref[...]
    left = lax.broadcasted_iota(jnp.int32, (nz, width), 1) < width // 2

    def fold(v):
        while v.shape[0] > 8:
            half = v.shape[0] // 2
            v = v[:half] + v[half:]
        return jnp.sum(v, axis=0, keepdims=True)

    def rests(x):
        u = two_ref[rows_of(x, stride, nz), :]
        v = optical(u, pot_ref[rows_of(x, nz, nz), :], left)
        left_ref[pl.ds(nx + x, 1), :] = v[0:1] + fold(kvec[...] * u)
        right_ref[pl.ds(nx + x, 1), :] = fold(rcol[...] * v + mvec[...] * u)

    repeat(nx, 16, only(rests), 0)
    for ref, rows_ref in ((one_ref, rows1_ref), (two_ref, rows2_ref)):
        for q in range(chip):
            rows_ref[q * nz : (q + 1) * nz, :] = ref[rows_of(scal[0] + q, stride, nz), :]


def third_body(nx, nz, width, cur_ref, prev_ref, pot_ref, kz, kx, wy, rcol, out_ref):
    stride = nz + PAD
    apply_local(
        nx, nz, width, (pot_ref, kz, kx, wy, rcol), (cur_ref, stride),
        lambda x: cur_ref[rows_of(x, stride, nz), :], (prev_ref, stride), None, 2.0,
        (out_ref, 0, nx), None,
    )


def fourth_body(nx, nz, width, chip, scal, cur_ref, prev_ref, pot_ref, *refs):
    kz, kx, wy, rcol, kx_ref, ky_ref, before_ref = refs[:7]
    edges, rows1_ref, rows2_ref = refs[7:14], refs[14], refs[15]
    keep_ref, send_ref, col_ref, out_ref, halo_ref = refs[16:]
    left_ref, right_ref = edges[:2]
    stride = nz + PAD
    rests = edge_rests(scal, *edges)
    for q, near in enumerate((left_ref, right_ref)):
        moved = transverse(kx_ref, ky_ref, near[0:nx, :])
        halo_ref[q] = 2.0 * (moved + rests[q]) - before_ref[q]
    now = (rcol, left_ref, right_ref, 2.0)

    def complete(x):
        u = with_halo(cur_ref[rows_of(x, stride, nz), :], now, x)
        col_ref[rows_of(x, stride, nz), :] = u

    repeat(nx, 16, only(complete), 0)
    apply_local(
        nx, nz, width, (pot_ref, kz, kx, wy, rcol), (col_ref, stride),
        lambda x: col_ref[rows_of(x, stride, nz), :], (prev_ref, stride),
        (rcol, halo_ref.at[0], halo_ref.at[1], 2.0), 2.0, (out_ref, scal[0], chip), None,
    )
    rows = chip // 2
    size = rows * nz
    for ref, where in ((keep_ref, scal[1]), (send_ref, 1 - scal[1])):
        at = pl.ds(pl.multiple_of(where * size, size), size)
        ref[0] = rows1_ref[at, :]
        ref[1] = rows2_ref[at, :]
        for r in range(rows):
            x = where * rows + r
            ref[2, r * nz : (r + 1) * nz, :] = col_ref[rows_of(scal[0] + x, stride, nz), :]
            ref[3, r * nz : (r + 1) * nz, :] = out_ref[rows_of(x, stride, nz), :]


def vm():
    return pl.BlockSpec(memory_space=pltpu.VMEM)


def in_vmem(*shape):
    return pltpu.VMEM(shape, F32)


def call(name, body, outs, *ins, scal=None, scratch=(), cost=4, away=()):
    specs = [pl.BlockSpec(memory_space=pltpu.HBM) if i in away else vm() for i in range(len(ins))]
    ins = tuple(
        pltpu.with_memory_space_constraint(x, pltpu.HBM) if i in away else x for i, x in enumerate(ins)
    )
    if scal is not None:
        specs = [pl.BlockSpec(memory_space=pltpu.SMEM)] + specs
        ins = (scal,) + ins
    return pl.pallas_call(
        body,
        out_shape=outs,
        in_specs=specs,
        out_specs=[vm()] * len(outs),
        scratch_shapes=list(scratch),
        compiler_params=pltpu.CompilerParams(vmem_limit_bytes=LIMIT),
        cost_estimate=pl.CostEstimate(
            flops=cost * 10**9, bytes_accessed=2 * cost * 10**6, transcendentals=0
        ),
        name=name,
    )(*ins)


def gram_body(scal, packets_ref, keep_ref, recv_ref, cols_ref, gram_ref, acc_ref):
    core = scal[1]
    ncol, size, width = cols_ref.shape
    npow = ncol // 2
    half = width // 2
    cols_ref[0] = packets_ref[0]
    cols_ref[npow] = packets_ref[1]
    for k in range(npow - 1):
        cols_ref[core * npow + 1 + k] = keep_ref[k]
        cols_ref[(1 - core) * npow + 1 + k] = recv_ref[k]
    acc_ref[...] = jnp.zeros_like(acc_ref)
    sign = jnp.where(lax.broadcasted_iota(jnp.int32, (8, width), 1) < half, 1.0, -1.0)
    first, second = list(range(npow)), list(range(npow, ncol))
    groups = [
        [(a, b) for a in first for b in first if a <= b],
        [(a, b) for a in second for b in second if a <= b],
        [(a, b) for a in first for b in second[:3]],
        [(a, b) for a in first for b in second[3:]],
    ]
    unroll = 16
    for pairs in groups:
        used = sorted({c for pair in pairs for c in pair})
        turned = sorted({b for a, b in pairs if a != b})

        def chunk(i, sums, pairs=pairs, used=used, turned=turned):
            sums = list(sums)
            for q in range(unroll):
                at = pl.ds(pl.multiple_of((i * unroll + q) * 8, 8), 8)
                v = {c: cols_ref[c, at, :] for c in used}
                t = {c: pltpu.roll(v[c], half, 1) for c in turned}
                n = 0
                for a, b in pairs:
                    sums[n] = sums[n] + v[a] * v[b]
                    n += 1
                    if a != b:
                        sums[n] = sums[n] + v[a] * t[b]
                        n += 1
            return tuple(sums)

        count = sum(1 if a == b else 2 for a, b in pairs)
        sums = lax.fori_loop(
            0, size // (8 * unroll), chunk, tuple(jnp.zeros((8, width), F32) for _ in range(count))
        )
        n = 0
        for a, b in pairs:
            acc_ref[a * ncol + b : a * ncol + b + 1, :] = jnp.sum(sums[n], axis=0, keepdims=True)
            n += 1
            if a != b:
                acc_ref[b * ncol + a : b * ncol + a + 1, :] = jnp.sum(
                    sums[n] * sign, axis=0, keepdims=True
                )
                n += 1
    row = jnp.sum(acc_ref[...].T, axis=0, keepdims=True)
    gram_ref[...] = jnp.broadcast_to(row[None], gram_ref.shape)


def basis_body(cells, rows, gram_ref, cols_ref, basis_ref, factor_ref, coef_ref, out_ref, sems):
    ncol, size, width = cols_ref.shape
    half = width // 2
    row = jnp.sum(gram_ref[...], axis=0) * (1.0 / cells)
    r = lax.broadcasted_iota(jnp.int32, (16, width), 0)
    c = lax.broadcasted_iota(jnp.int32, (16, width), 1)
    packed = jnp.zeros((16, width), F32)
    for j in range(ncol):
        moved = row if j == 0 else pltpu.roll(row, width - ncol * j, 1)
        packed = jnp.where(r == j, moved, packed)
    turned = jnp.concatenate([packed, jnp.zeros((width - 16, width), F32)], axis=0).T[:16]
    inside = (r < ncol) & (c < ncol)
    re = jnp.where(inside, jnp.where(r <= c, packed, turned), 0.0)
    im = jnp.where(inside & (r != c), jnp.where(r < c, turned, -packed), 0.0)
    re = jnp.where(c == r + 16, 1.0, re)
    up_re = jnp.zeros((16, width), F32)
    up_im = jnp.zeros((16, width), F32)
    for j in range(ncol):
        pivot = jnp.sqrt(re[j : j + 1, j : j + 1])
        inverse = 1.0 / pivot
        row_re = re[j : j + 1, :] * inverse
        row_im = im[j : j + 1, :] * inverse
        col_re = re[:, j : j + 1] * inverse
        col_im = im[:, j : j + 1] * inverse
        up_re = jnp.where(r == j, row_re, up_re)
        up_im = jnp.where(r == j, row_im, up_im)
        below = r > j
        re = re - jnp.where(below, col_re * row_re - col_im * row_im, 0.0)
        im = im - jnp.where(below, col_re * row_im + col_im * row_re, 0.0)
    keep = (c >= r) & (c < ncol)
    factor_ref[0] = jnp.where(keep, up_re, 0.0)
    factor_ref[1] = jnp.where(keep & (c > r), up_im, 0.0)
    sign = jnp.where(lax.broadcasted_iota(jnp.int32, (8, width), 1) < half, 1.0, -1.0)
    for k in range(ncol):
        for i in range(k + 1):
            coef_ref[0, k * ncol + i] = jnp.broadcast_to(up_re[k : k + 1, 16 + i : 17 + i], (8, width))
            coef_ref[1, k * ncol + i] = (
                jnp.broadcast_to(up_im[k : k + 1, 16 + i : 17 + i], (8, width)) * sign
            )
    group = 4
    each = size // rows
    copies = []
    for r in range(rows):
        for start in range(r * each, (r + 1) * each, 8 * group):
            slots = [slice(start + 8 * g, start + 8 * g + 8) for g in range(group)]
            v = [[cols_ref[i, s, :] for s in slots] for i in range(ncol)]
            t = [[pltpu.roll(x, half, 1) for x in xs] for xs in v]
            for k in range(ncol):
                total = [None] * group
                for i in range(k + 1):
                    re = coef_ref[0, k * ncol + i]
                    im = coef_ref[1, k * ncol + i]
                    for g in range(group):
                        term = re * v[i][g]
                        if i < k:
                            term = term + im * t[i][g]
                        total[g] = term if total[g] is None else total[g] + term
                for g in range(group):
                    out_ref[k, slots[g], :] = total[g]
        part = pl.ds(r * each, each)
        copy = pltpu.make_async_copy(out_ref.at[:, part, :], basis_ref.at[:, part, :], sems.at[r])
        copy.start()
        copies.append(copy)
    for copy in copies:
        copy.wait()


def shards(packets, kinetic_x, kinetic_y, element_kinetic, potential):
    npack, rows, nz, width = packets.shape
    trans = lax.axis_size("trans")
    nx = rows * trans
    ncol = npack * (POWERS + 1)
    me = lax.axis_index("trans")
    core = me % 2
    chip = 2 * rows
    beam = lax.axis_size("beam")
    scal = jnp.stack([(me // 2) * chip, core, lax.axis_index("beam"), beam]).astype(jnp.int32)

    size = rows * nz
    flat = packets.reshape(npack, size, width)
    mine = potential.reshape(size, width)
    pot = lax.all_gather(mine, "trans", axis=0, tiled=True)
    sent = pl.pallas_call(
        copies_body,
        out_shape=jax.ShapeDtypeStruct((trans, size, width), F32),
        in_specs=[vm()],
        out_specs=pl.BlockSpec(memory_space=pl.ANY),
        scratch_shapes=[pltpu.SemaphoreType.DMA((trans // npack,))],
        compiler_params=pltpu.CompilerParams(vmem_limit_bytes=LIMIT),
        name="copies",
    )(flat)
    cur = lax.all_to_all(sent, "trans", 0, 0, tiled=True).reshape(nx * nz, width)
    sent, flat_late, mine_late, ek_late = lax.optimization_barrier(
        (sent, flat, mine, element_kinetic)
    )

    def half_wide(*shape):
        return pltpu.VMEM(shape, BF16)

    square, column = half_wide(4 * nz, 4 * nz), in_vmem(nz, width)
    across = half_wide(4 * nx, 4 * nx)
    wide = half_wide(2 * width, 2 * width)
    rcol, kvec, mvec, coef = call(
        "vectors", vectors_body, [column, column, column, in_vmem(8, width)], ek_late, scal=scal, cost=1
    )

    count = npack * rows
    plane, double = in_vmem(count, width), in_vmem(2 * count, width)
    left, right, first, bridge = call(
        "planes", functools.partial(planes_body, nz), [double, double, plane, plane],
        flat_late, mine_late, rcol, kvec, mvec, cost=1,
    )
    (planes,) = call(
        "edges", edges_body, [in_vmem(4, count, width)],
        passed(left, -1), passed(right, 1), passed(first, -2), passed(bridge, 2), first, bridge, coef,
        scal=scal, cost=1,
    )
    planes = lax.all_gather(planes, "trans")

    full, edge, two_edges = in_vmem(nx * (nz + PAD), width), in_vmem(nx, width), in_vmem(2 * nx, width)
    here = in_vmem(chip * nz, width)
    got = call(
        "pair", functools.partial(pair_body, nx, nz, width, chip),
        [full, full, two_edges, two_edges, edge, edge, here, here, in_vmem(nx * nz, width),
         square, across, wide, half_wide(4 * chip, 4 * nx), in_vmem(*kinetic_x.shape),
         in_vmem(width, width), in_vmem(2, nx, width), column, column, column, in_vmem(8, width)],
        cur, planes, pot, kinetic_x, kinetic_y, element_kinetic,
        scal=scal, cost=8, away=(2, 3, 4, 5),
        scratch=[full, in_vmem(4, nx, width), pltpu.SemaphoreType.DMA((5,)), in_vmem(*kinetic_y.shape),
                 in_vmem(*element_kinetic.shape), square, across, wide],
    )
    col1, col2, left, right, first, bridge, rows1, rows2, pot = got[:9]
    kz2, kx2, wy2, kx4, kx, ky, before, rcol, _, _, coef = got[9:]
    edges = [passed(left, -1), passed(right, 1), passed(first, -2), passed(bridge, 2), first, bridge, coef]
    (col3,) = call(
        "third", functools.partial(third_body, nx, nz, width), [full], col2, col1, pot, kz2, kx2, wy2, rcol
    )
    keep, send = call(
        "fourth", functools.partial(fourth_body, nx, nz, width, chip),
        [in_vmem(POWERS, size, width)] * 2,
        col3, col2, pot, kz2, kx4, wy2, rcol, kx, ky, before, *edges, rows1, rows2,
        scal=scal, cost=2, scratch=[full, in_vmem(chip * (nz + PAD), width), in_vmem(2, nx, width)],
    )
    recv = lax.ppermute(send, "trans", [(i, i ^ 1) for i in range(trans)])
    cols, gram = pl.pallas_call(
        gram_body,
        out_shape=[in_vmem(ncol, size, width), in_vmem(trans, 1, width)],
        in_specs=[pl.BlockSpec(memory_space=pltpu.SMEM)] + [vm()] * 3,
        out_specs=[vm()] * 2,
        scratch_shapes=[pltpu.VMEM((128, width), F32)],
        compiler_params=pltpu.CompilerParams(vmem_limit_bytes=LIMIT),
        name="gram",
    )(scal, packets.reshape(npack, size, width), keep, recv)
    gram = jnp.sum(lax.all_to_all(gram, "trans", 0, 0, tiled=True), axis=0, keepdims=True)
    gram = lax.all_to_all(jnp.broadcast_to(gram, (beam, 1, width)), "beam", 0, 0, tiled=True)
    cells = float(nx * (width // 2) * nz * beam)
    basis, factor = pl.pallas_call(
        functools.partial(basis_body, cells, rows),
        out_shape=[
            jax.ShapeDtypeStruct((ncol, size, width), F32),
            jax.ShapeDtypeStruct((2, 16, width), F32),
        ],
        in_specs=[vm(), vm()],
        out_specs=[pl.BlockSpec(memory_space=pl.ANY), vm()],
        scratch_shapes=[
            pltpu.VMEM((2, ncol * ncol, 8, width), F32),
            pltpu.VMEM((ncol, size, width), F32),
            pltpu.SemaphoreType.DMA((rows,)),
        ],
        compiler_params=pltpu.CompilerParams(vmem_limit_bytes=LIMIT),
        name="basis",
    )(gram, cols)
    return basis.reshape(ncol, rows, nz, width), factor[:, :ncol, :ncol]


def solution(mesh):
    in_specs = (P(None, "trans", "beam", None), P(), P(), P(), P("trans", "beam", None))
    out_specs = (P(None, "trans", "beam", None), P())
    return jax.shard_map(shards, mesh=mesh, in_specs=in_specs, out_specs=out_specs, check_vma=False)
```

```python
import functools

import jax
import jax.numpy as jnp
from jax import lax
from jax.experimental import pallas as pl
from jax.experimental.pallas import tpu as pltpu
from jax.sharding import PartitionSpec as P

POWERS = 4
F32 = jnp.float32
BF16 = jnp.bfloat16
LIMIT = 16 * 1024 * 1024


def split(v):
    high = v.astype(BF16)
    return high, (v - high.astype(F32)).astype(BF16)


def passed(x, by):
    peers = lax.axis_size("beam")
    return lax.ppermute(x, "beam", [(i, i + by) for i in range(peers) if 0 <= i + by < peers])


PAD = 8


def apply_local(nx, nz, width, refs, col, load, prev, halo, scale, out, bridge_ref, ready=None):
    pot_ref, kz_ref, kx_ref, wy_ref, wvec_ref = refs
    col_ref, stride = col
    out_ref, x_start, out_x = out
    out_stride = nz + PAD
    half = width // 2
    left = lax.broadcasted_iota(jnp.int32, (nz, width), 1) < half

    def product(k_ref, us):
        parts = [split(u) for u in us]
        rows = []
        for p, q in (parts[0:2], parts[2:4]):
            rows += [jnp.concatenate([p[0], q[0]], axis=1), jnp.concatenate([p[1], q[1]], axis=1)]
        got = jnp.dot(k_ref[...], jnp.concatenate(rows, axis=0), preferred_element_type=F32)
        m = got.shape[0] // 4
        outs = []
        for i in range(2):
            both = got[2 * i * m : (2 * i + 1) * m] + got[(2 * i + 1) * m : (2 * i + 2) * m]
            outs += [both[:, :width], both[:, width:]]
        return outs, parts

    def local_four(x0):
        us = [load(x_start + x0 + q) for q in range(4)]
        along_z, parts = product(kz_ref, us)
        along_y = jnp.dot(
            jnp.concatenate([jnp.concatenate(p, axis=1) for p in parts], axis=0),
            wy_ref[...],
            preferred_element_type=F32,
        )
        for q in range(4):
            x = x_start + x0 + q
            ay = along_y[q * nz : (q + 1) * nz]
            new = along_z[q] + ay[:, :width] + ay[:, width:]
            new = new + scale * optical(us[q], pot_ref[rows_of(x, nz, nz), :], left)
            if prev is not None:
                new = new - prev[0][rows_of(x, prev[1], nz), :]
            if halo is not None:
                new = with_halo(new, halo, x)
            out_ref[rows_of(x0 + q, out_stride, nz), :] = new

    if ready is None:
        repeat(out_x // 4, 8, only(lambda i: local_four(i * 4)), 0)
    else:
        for h in range(2):
            ready(h)
            repeat(out_x // 8, 8, only(lambda i, h=h: local_four((h * out_x // 8 + i) * 4)), 0)

    def across_four(i, bridge):
        z0 = i * 4
        us = [col_ref[pl.ds(z0 + q, nx, stride=stride), :] for q in range(4)]
        along_x, _ = product(kx_ref, us)
        for q in range(4):
            at = pl.ds(z0 + q, out_x, stride=out_stride)
            new = out_ref[at, :] + along_x[q]
            out_ref[at, :] = new
            if bridge_ref is not None:
                bridge = bridge + wvec_ref[pl.ds(z0 + q, 1), :] * new
        return bridge

    bridge = repeat(nz // 4, 8, across_four, jnp.zeros((out_x, width), F32))
    if bridge_ref is not None:
        bridge_ref[...] = bridge


def rows_of(x, stride, nz):
    return pl.ds(pl.multiple_of(x * stride, 8), nz)


def optical(u, pot, left):
    half = u.shape[-1] // 2
    turned = pltpu.roll(pot, half, 1)
    return jnp.where(left, pot, turned) * u + jnp.where(left, turned, -pot) * pltpu.roll(u, half, 1)


def with_halo(u, halo, x):
    column_ref, plane_ref, sum_ref, scale = halo
    top = lax.broadcasted_iota(jnp.int32, (8, u.shape[-1]), 0) == 0
    u = u + column_ref[...] * (scale * plane_ref[pl.ds(x, 1), :])
    head = u[0:8] + jnp.where(top, scale * sum_ref[pl.ds(x, 1), :], 0.0)
    return jnp.concatenate([head, u[8:]], axis=0)


def repeat(count, unroll, body, carry):
    unroll = min(unroll, count)

    def some(i, carry):
        for q in range(unroll):
            carry = body(i * unroll + q, carry)
        return carry

    return lax.fori_loop(0, count // unroll, some, carry)


def only(body):
    def with_carry(i, carry):
        body(i)
        return carry

    return with_carry


def copies_body(packets_ref, sent_ref, sems):
    npack = packets_ref.shape[0]
    copies = [
        pltpu.make_async_copy(packets_ref, sent_ref.at[pl.ds(i * npack, npack)], sems.at[i])
        for i in range(sent_ref.shape[0] // npack)
    ]
    for copy in copies:
        copy.start()
    for copy in copies:
        copy.wait()


def planes_body(nz, packets_ref, pot_ref, wvec_ref, kvec_ref, mvec_ref, first_ref, bridge_ref, zrest_ref, brest_ref):
    npack, size, width = packets_ref.shape
    rows = size // nz
    left = lax.broadcasted_iota(jnp.int32, (nz, width), 1) < width // 2
    for p in range(npack):
        for x in range(rows):
            u = packets_ref[p, x * nz : (x + 1) * nz, :]
            v = optical(u, pot_ref[x * nz : (x + 1) * nz, :], left)
            at = slice(p * rows + x, p * rows + x + 1)
            first_ref[at, :] = u[0:1]
            bridge_ref[at, :] = jnp.sum(wvec_ref[...] * u, axis=0, keepdims=True)
            zrest_ref[at, :] = v[0:1] + jnp.sum(kvec_ref[...] * u, axis=0, keepdims=True)
            brest_ref[at, :] = jnp.sum(wvec_ref[...] * v + mvec_ref[...] * u, axis=0, keepdims=True)


def element_matrix(scal, ek):
    nz = ek.shape[0] - 1
    r = lax.broadcasted_iota(jnp.int32, (nz, nz), 0)
    c = lax.broadcasted_iota(jnp.int32, (nz, nz), 1)
    corner = (r == 0) & (c == 0) & (scal[2] > 0)
    return ek[0:nz, 0:nz] + jnp.where(corner, ek[nz : nz + 1, nz : nz + 1], 0.0)


def vectors_body(scal, ek_ref, rcol, kvec, mvec, coef):
    nz, width = rcol.shape
    kz = element_matrix(scal, ek_ref)
    edge_vectors(ek_ref, rcol, coef)
    kvec[...] = jnp.broadcast_to(kz[:, 0:1], (nz, width))
    bridge = ek_ref[nz : nz + 1, 0:nz]
    mvec[...] = jnp.broadcast_to(jnp.sum(kz * bridge, axis=1, keepdims=True), (nz, width))


def edge_vectors(ek_ref, rcol, coef):
    nz, width = rcol.shape
    rcol[...] = jnp.broadcast_to(ek_ref[0:nz, nz : nz + 1], (nz, width))
    coef[...] = jnp.zeros_like(coef)
    coef[0:1, :] = rcol[0:1, :]
    coef[1:2, :] = jnp.sum(rcol[...] * rcol[...], axis=0, keepdims=True)


def matrices(scal, kx_ref, ky_ref, ek_ref, kz1, kx1, wy1, kz2, kx2, wy2, kx4, kyd):
    chip = kx4.shape[0] // 4

    def split_wide(k):
        high = k.astype(BF16).astype(F32)
        return high, k - high

    def left_weights(k):
        high, low = split_wide(k)
        none = jnp.zeros_like(high)
        block = jnp.concatenate(
            [jnp.concatenate([high, high], axis=1), jnp.concatenate([low, none], axis=1)], axis=0
        )
        none = jnp.zeros_like(block)
        return jnp.concatenate(
            [jnp.concatenate([block, none], axis=1), jnp.concatenate([none, block], axis=1)], axis=0
        )

    for one, two, k in ((kz1, kz2, element_matrix(scal, ek_ref)), (kx1, kx2, kx_ref[...])):
        block = left_weights(k)
        one[...] = block.astype(BF16)
        two[...] = (2.0 * block).astype(BF16)
    kx4[...] = left_weights(2.0 * kx_ref[pl.ds(pl.multiple_of(scal[0], 8), chip), :]).astype(BF16)
    ky = ky_ref[...]
    none = jnp.zeros_like(ky)
    ky = jnp.concatenate(
        [jnp.concatenate([ky, none], axis=1), jnp.concatenate([none, ky], axis=1)], axis=0
    )
    kyd[...] = ky
    high, low = split_wide(ky)
    block = jnp.concatenate(
        [jnp.concatenate([high, low], axis=1), jnp.concatenate([high, jnp.zeros_like(low)], axis=1)],
        axis=0,
    )
    wy1[...] = block.astype(BF16)
    wy2[...] = (2.0 * block).astype(BF16)


def edges_body(scale, first_ref, bridge_ref, pin_ref, bin_ref, coef_ref, out_first, out_bridge):
    head, square = coef_ref[0:1, :], coef_ref[1:2, :]
    pin, bin_ = scale * pin_ref[...], scale * bin_ref[...]
    out_first[...] = first_ref[...] + head * pin + bin_
    out_bridge[...] = bridge_ref[...] + square * pin + head * bin_


def pair_body(nx, nz, width, chip, scal, cur_ref, gathered_ref, pot_hbm, kx_hbm, ky_hbm, ek_hbm, *refs):
    one_ref, two_ref, first_ref, bridge_ref, pot_ref = refs[:5]
    kz2, kx2, wy2, kx4, rcol, coef = refs[5:11]
    col_ref, planes_ref, halo_ref, sems, kx_ref, ky_raw, ek_ref, kz1, kx1, wy1, ky_ref = refs[11:]
    stride = nz + PAD
    small = [
        pltpu.make_async_copy(src, dst, sems.at[2 + i])
        for i, (src, dst) in enumerate(((kx_hbm, kx_ref), (ky_hbm, ky_raw), (ek_hbm, ek_ref)))
    ]
    for copy in small:
        copy.start()
    part = nx * nz // 2
    copies = [
        pltpu.make_async_copy(
            pot_hbm.at[pl.ds(h * part, part), :], pot_ref.at[pl.ds(h * part, part), :], sems.at[h]
        )
        for h in range(2)
    ]
    for copy in copies:
        copy.start()

    trans, planes, each, _ = gathered_ref.shape
    each = each // 2
    for t in range(trans):
        for q in range(planes):
            planes_ref[q, t * each : (t + 1) * each, :] = gathered_ref[
                t, q, pl.ds(pl.multiple_of(scal[1] * each, 8), each), :
            ]
    for copy in small:
        copy.wait()
    matrices(scal, kx_ref, ky_raw, ek_ref, kz1, kx1, wy1, kz2, kx2, wy2, kx4, ky_ref)
    edge_vectors(ek_ref, rcol, coef)
    precise = lax.Precision.HIGHEST
    for q in range(2):
        plane = planes_ref[q]
        moved = jnp.dot(kx_ref[...], plane, precision=precise, preferred_element_type=F32)
        moved = moved + jnp.dot(plane, ky_ref[...], precision=precise, preferred_element_type=F32)
        halo_ref[q] = moved + planes_ref[2 + q]

    def packed(x):
        u = cur_ref[rows_of(x, nz, nz), :]
        col_ref[rows_of(x, stride, nz), :] = u
        return u

    apply_local(
        nx, nz, width, (pot_ref, kz1, kx1, wy1, rcol), (col_ref, stride), packed, None,
        (rcol, planes_ref.at[0], planes_ref.at[1], 1.0), 1.0, (one_ref, 0, nx), None,
        ready=lambda h: copies[h].wait(),
    )
    apply_local(
        nx, nz, width, (pot_ref, kz2, kx2, wy2, rcol), (one_ref, stride),
        lambda x: one_ref[rows_of(x, stride, nz), :], (cur_ref, nz),
        (rcol, halo_ref.at[0], halo_ref.at[1], 2.0), 2.0, (two_ref, 0, nx), bridge_ref,
    )
    first_ref[...] = two_ref[pl.ds(0, nx, stride=stride), :]


def part_rows(scal, chip, nz, ref, stride, base, keep_ref, send_ref, k):
    rows = chip // 2
    for to_ref, core in ((keep_ref, scal[1]), (send_ref, 1 - scal[1])):
        for r in range(rows):
            to_ref[k, r * nz : (r + 1) * nz, :] = ref[rows_of(base + core * rows + r, stride, nz), :]


def third_body(nx, nz, width, chip, scal, cur_ref, prev_ref, pot_ref, kz, kx, wy, rcol, *outs):
    out_ref, first_ref, bridge_ref, keep_ref, send_ref = outs
    stride = nz + PAD
    apply_local(
        nx, nz, width, (pot_ref, kz, kx, wy, rcol), (cur_ref, stride),
        lambda x: cur_ref[rows_of(x, stride, nz), :], (prev_ref, stride), None, 2.0,
        (out_ref, 0, nx), bridge_ref,
    )
    first_ref[...] = out_ref[pl.ds(0, nx, stride=stride), :]
    for k, ref in enumerate((prev_ref, cur_ref)):
        part_rows(scal, chip, nz, ref, stride, scal[0], keep_ref, send_ref, k)


def fourth_body(nx, nz, width, chip, scal, cur_ref, pin_ref, bin_ref, prev_ref, pot_ref, *refs):
    kz, kx, wy, rcol, out_ref, keep_ref, send_ref, col_ref = refs
    stride = nz + PAD

    def complete(x):
        u = with_halo(cur_ref[rows_of(x, stride, nz), :], (rcol, pin_ref, bin_ref, 2.0), x)
        col_ref[rows_of(x, stride, nz), :] = u

    repeat(nx, 16, only(complete), 0)
    part_rows(scal, chip, nz, col_ref, stride, scal[0], keep_ref, send_ref, 0)
    apply_local(
        nx, nz, width, (pot_ref, kz, kx, wy, rcol), (col_ref, stride),
        lambda x: col_ref[rows_of(x, stride, nz), :], (prev_ref, stride), None, 2.0,
        (out_ref, scal[0], chip), None,
    )


def vm():
    return pl.BlockSpec(memory_space=pltpu.VMEM)


def in_vmem(*shape):
    return pltpu.VMEM(shape, F32)


def call(name, body, outs, *ins, scal=None, scratch=(), cost=4, away=()):
    specs = [pl.BlockSpec(memory_space=pltpu.HBM) if i in away else vm() for i in range(len(ins))]
    ins = tuple(
        pltpu.with_memory_space_constraint(x, pltpu.HBM) if i in away else x for i, x in enumerate(ins)
    )
    if scal is not None:
        specs = [pl.BlockSpec(memory_space=pltpu.SMEM)] + specs
        ins = (scal,) + ins
    return pl.pallas_call(
        body,
        out_shape=outs,
        in_specs=specs,
        out_specs=[vm()] * len(outs),
        scratch_shapes=list(scratch),
        compiler_params=pltpu.CompilerParams(vmem_limit_bytes=LIMIT),
        cost_estimate=pl.CostEstimate(
            flops=cost * 10**9, bytes_accessed=2 * cost * 10**6, transcendentals=0
        ),
        name=name,
    )(*ins)


def finish_body(nz, rows, scal, last_ref, pin_ref, bin_ref, rcol_ref, keep_ref, send_ref):
    halo = (rcol_ref, pin_ref, bin_ref, 2.0)
    for ref, where in ((keep_ref, scal[1]), (send_ref, 1 - scal[1])):
        for r in range(rows):
            x = where * rows + r
            u = with_halo(last_ref[rows_of(x, nz + PAD, nz), :], halo, scal[0] + x)
            ref[0, r * nz : (r + 1) * nz, :] = u


EARLY = 3


def at_column(cols, c):
    p, k = divmod(c, POWERS + 1)
    if k < EARLY:
        return cols[0], p * EARLY + k
    return cols[1], p * (POWERS + 1 - EARLY) + k - EARLY


def add_products(cols, groups, acc_ref):
    ncol = 2 * (POWERS + 1)
    _, size, width = cols[0].shape
    half = width // 2
    sign = jnp.where(lax.broadcasted_iota(jnp.int32, (8, width), 1) < half, 1.0, -1.0)
    unroll = 32
    for pairs in groups:
        used = sorted({c for pair in pairs for c in pair})
        turned = sorted({b for a, b in pairs if a != b})

        def chunk(i, sums, pairs=pairs, used=used, turned=turned):
            sums = list(sums)
            for q in range(unroll):
                at = pl.ds(pl.multiple_of((i * unroll + q) * 8, 8), 8)
                v = {}
                for c in used:
                    ref, n = at_column(cols, c)
                    v[c] = ref[n, at, :]
                t = {c: pltpu.roll(v[c], half, 1) for c in turned}
                n = 0
                for a, b in pairs:
                    sums[n] = sums[n] + v[a] * v[b]
                    n += 1
                    if a != b:
                        sums[n] = sums[n] + v[a] * t[b]
                        n += 1
            return tuple(sums)

        count = sum(1 if a == b else 2 for a, b in pairs)
        sums = lax.fori_loop(
            0, size // (8 * unroll), chunk, tuple(jnp.zeros((8, width), F32) for _ in range(count))
        )
        n = 0
        for a, b in pairs:
            acc_ref[a * ncol + b : a * ncol + b + 1, :] = jnp.sum(sums[n], axis=0, keepdims=True)
            n += 1
            if a != b:
                acc_ref[b * ncol + a : b * ncol + a + 1, :] = jnp.sum(
                    sums[n] * sign, axis=0, keepdims=True
                )
                n += 1


def column_sets():
    first = list(range(POWERS + 1))
    second = [POWERS + 1 + k for k in first]
    old = lambda c: c % (POWERS + 1) < EARLY
    inside = [[(a, b) for a in cols for b in cols if a <= b] for cols in (first, second)]
    across = [(a, b) for a in first for b in second]
    early = [[p for p in inside[0] + inside[1] if old(p[0]) and old(p[1])]]
    early.append([p for p in across if old(p[0]) and old(p[1])])
    late = [[p for p in pairs if not (old(p[0]) and old(p[1]))] for pairs in inside]
    late.append([p for p in across if old(p[0]) and not old(p[1])])
    late.append([p for p in across if not old(p[0])])
    return early, late


def early_body(scal, packets_ref, keep_ref, recv_ref, cols_ref, acc_ref):
    core = scal[1]
    for p in range(2):
        cols_ref[p * EARLY] = packets_ref[p]
    for k in range(EARLY - 1):
        cols_ref[core * EARLY + 1 + k] = keep_ref[k]
        cols_ref[(1 - core) * EARLY + 1 + k] = recv_ref[k]
    acc_ref[...] = jnp.zeros_like(acc_ref)
    add_products((cols_ref, None), column_sets()[0], acc_ref)


def gram_body(scal, early_ref, part_ref, keep3, recv3, keep4, recv4, cols_ref, gram_ref, acc_ref):
    core = scal[1]
    later = POWERS + 1 - EARLY
    for k, (mine, other) in enumerate(((keep3, recv3), (keep4, recv4))):
        cols_ref[core * later + k] = mine[0]
        cols_ref[(1 - core) * later + k] = other[0]
    acc_ref[...] = part_ref[...]
    add_products((early_ref, cols_ref), column_sets()[1], acc_ref)
    row = jnp.sum(acc_ref[...].T, axis=0, keepdims=True)
    gram_ref[...] = jnp.broadcast_to(row[None], gram_ref.shape)


def basis_body(cells, rows, gram_ref, early_ref, late_ref, basis_ref, factor_ref, coef_ref, out_ref, sems):
    ncol, size, width = out_ref.shape
    cols = (early_ref, late_ref)
    half = width // 2
    row = jnp.sum(gram_ref[...], axis=0) * (1.0 / cells)
    r = lax.broadcasted_iota(jnp.int32, (16, width), 0)
    c = lax.broadcasted_iota(jnp.int32, (16, width), 1)
    packed = jnp.zeros((16, width), F32)
    for j in range(ncol):
        moved = row if j == 0 else pltpu.roll(row, width - ncol * j, 1)
        packed = jnp.where(r == j, moved, packed)
    turned = jnp.concatenate([packed, jnp.zeros((width - 16, width), F32)], axis=0).T[:16]
    inside = (r < ncol) & (c < ncol)
    re = jnp.where(inside, jnp.where(r <= c, packed, turned), 0.0)
    im = jnp.where(inside & (r != c), jnp.where(r < c, turned, -packed), 0.0)
    re = jnp.where(c == r + 16, 1.0, re)
    up_re = jnp.zeros((16, width), F32)
    up_im = jnp.zeros((16, width), F32)
    for j in range(ncol):
        pivot = jnp.sqrt(re[j : j + 1, j : j + 1])
        inverse = 1.0 / pivot
        row_re = re[j : j + 1, :] * inverse
        row_im = im[j : j + 1, :] * inverse
        col_re = re[:, j : j + 1] * inverse
        col_im = im[:, j : j + 1] * inverse
        up_re = jnp.where(r == j, row_re, up_re)
        up_im = jnp.where(r == j, row_im, up_im)
        below = r > j
        re = re - jnp.where(below, col_re * row_re - col_im * row_im, 0.0)
        im = im - jnp.where(below, col_re * row_im + col_im * row_re, 0.0)
    for q, up in ((0, jnp.where(c >= r, up_re, 0.0)), (1, jnp.where(c > r, up_im, 0.0))):
        for k in range(ncol):
            factor_ref[k, q : q + 1, :] = up[k : k + 1, :ncol]
    sign = jnp.where(lax.broadcasted_iota(jnp.int32, (8, width), 1) < half, 1.0, -1.0)
    for k in range(ncol):
        for i in range(k + 1):
            coef_ref[0, k * ncol + i] = jnp.broadcast_to(up_re[k : k + 1, 16 + i : 17 + i], (8, width))
            coef_ref[1, k * ncol + i] = (
                jnp.broadcast_to(up_im[k : k + 1, 16 + i : 17 + i], (8, width)) * sign
            )
    group = 4
    each = size // rows

    def row(r, carry):
        for start in range(0, each, 8 * group):
            slots = [pl.ds(pl.multiple_of(r * each + start + 8 * g, 8), 8) for g in range(group)]
            v = []
            for i in range(ncol):
                ref, n = at_column(cols, i)
                v.append([ref[n, s, :] for s in slots])
            t = [[pltpu.roll(x, half, 1) for x in xs] for xs in v]
            for k in range(ncol):
                total = [None] * group
                for i in range(k + 1):
                    re = coef_ref[0, k * ncol + i]
                    im = coef_ref[1, k * ncol + i]
                    for g in range(group):
                        term = re * v[i][g]
                        if i < k:
                            term = term + im * t[i][g]
                        total[g] = term if total[g] is None else total[g] + term
                for g in range(group):
                    out_ref[k, slots[g], :] = total[g]
        copy(r).start()
        return carry

    def copy(r):
        part = pl.ds(pl.multiple_of(r * each, 8), each)
        return pltpu.make_async_copy(out_ref.at[:, part, :], basis_ref.at[:, part, :], sems.at[r])

    lax.fori_loop(0, rows, row, 0)
    for r in range(rows):
        copy(r).wait()


def shards(packets, kinetic_x, kinetic_y, element_kinetic, potential):
    npack, rows, nz, width = packets.shape
    trans = lax.axis_size("trans")
    nx = rows * trans
    ncol = npack * (POWERS + 1)
    me = lax.axis_index("trans")
    beam = lax.axis_size("beam")
    core = me % 2
    chip = 2 * rows
    scal = jnp.stack([(me // 2) * chip, core, lax.axis_index("beam")]).astype(jnp.int32)

    size = rows * nz
    flat = packets.reshape(npack, size, width)
    mine = potential.reshape(size, width)
    pot = lax.all_gather(mine, "trans", axis=0, tiled=True)
    sent = pl.pallas_call(
        copies_body,
        out_shape=jax.ShapeDtypeStruct((trans, size, width), F32),
        in_specs=[vm()],
        out_specs=pl.BlockSpec(memory_space=pl.ANY),
        scratch_shapes=[pltpu.SemaphoreType.DMA((trans // npack,))],
        compiler_params=pltpu.CompilerParams(vmem_limit_bytes=LIMIT),
        name="copies",
    )(flat)
    cur = lax.all_to_all(sent, "trans", 0, 0, tiled=True).reshape(nx * nz, width)
    sent, flat_late, mine_late, ek_late = lax.optimization_barrier(
        (sent, flat, mine, element_kinetic)
    )

    def half_wide(*shape):
        return pltpu.VMEM(shape, BF16)

    square, column = half_wide(4 * nz, 4 * nz), in_vmem(nz, width)
    across = half_wide(4 * nx, 4 * nx)
    wide = half_wide(2 * width, 2 * width)
    rcol, kvec, mvec, coef = call(
        "vectors", vectors_body, [column, column, column, in_vmem(8, width)], ek_late, scal=scal, cost=1
    )

    plane = in_vmem(npack * rows, width)
    first, bridge, zrest, brest = call(
        "planes", functools.partial(planes_body, nz), [plane] * 4,
        flat_late, mine_late, rcol, kvec, mvec, cost=1,
    )
    pin, bin_ = passed(first, -1), passed(bridge, 1)
    pnext, bnext = call(
        "edges", functools.partial(edges_body, 1.0), [plane] * 2, zrest, brest, pin, bin_, coef, cost=1
    )
    planes = jnp.stack([pin, bin_, passed(pnext, -1), passed(bnext, 1)])
    planes = lax.all_gather(planes, "trans")

    full, edge = in_vmem(nx * (nz + PAD), width), in_vmem(nx, width)
    col1, col2, first, bridge, pot, kz2, kx2, wy2, kx4, rcol, coef = call(
        "pair", functools.partial(pair_body, nx, nz, width, chip),
        [full, full, edge, edge, in_vmem(nx * nz, width),
         square, across, wide, half_wide(4 * chip, 4 * nx), column, in_vmem(8, width)],
        cur, planes, pot, kinetic_x, kinetic_y, element_kinetic,
        scal=scal, cost=8, away=(2, 3, 4, 5),
        scratch=[full, in_vmem(4, nx, width), in_vmem(2, nx, width), pltpu.SemaphoreType.DMA((5,)),
                 in_vmem(*kinetic_x.shape), in_vmem(*kinetic_y.shape), in_vmem(*element_kinetic.shape),
                 square, across, wide, in_vmem(width, width)],
    )
    pin, bin_ = passed(first, -1), passed(bridge, 1)
    col3, first, bridge, keep, send = call(
        "third", functools.partial(third_body, nx, nz, width, chip),
        [full, edge, edge, in_vmem(2, size, width), in_vmem(2, size, width)],
        col2, col1, pot, kz2, kx2, wy2, rcol, scal=scal,
    )

    def other_core(x):
        return lax.ppermute(x, "trans", [(i, i ^ 1) for i in range(trans)])

    recv = other_core(send)
    first, bridge = call(
        "edges", functools.partial(edges_body, 2.0), [edge] * 2, first, bridge, pin, bin_, coef, cost=1
    )
    plast, blast = passed(first, -1), passed(bridge, 1)
    one = in_vmem(1, size, width)
    local, keep3, send3 = call(
        "fourth", functools.partial(fourth_body, nx, nz, width, chip),
        [in_vmem(chip * (nz + PAD), width), one, one],
        col3, pin, bin_, col2, pot, kz2, kx4, wy2, rcol,
        scal=scal, scratch=[full], cost=2,
    )
    recv3 = other_core(send3)
    early, part = call(
        "early", early_body, [in_vmem(npack * EARLY, size, width), in_vmem(128, width)],
        flat, keep, recv, scal=scal, cost=1,
    )
    keep4, send4 = call(
        "finish", functools.partial(finish_body, nz, rows), [one, one],
        local, plast, blast, rcol, scal=scal, cost=1,
    )
    recv4 = other_core(send4)
    late, gram = call(
        "gram", gram_body, [in_vmem(ncol - npack * EARLY, size, width), in_vmem(trans, 1, width)],
        early, part, keep3, recv3, keep4, recv4, scal=scal, scratch=[in_vmem(128, width)], cost=1,
    )
    gram = jnp.sum(lax.all_to_all(gram, "trans", 0, 0, tiled=True), axis=0, keepdims=True)
    gram = lax.all_to_all(jnp.broadcast_to(gram, (beam, 1, width)), "beam", 0, 0, tiled=True)
    cells = float(nx * (width // 2) * nz * beam)
    basis, factor = pl.pallas_call(
        functools.partial(basis_body, cells, rows),
        out_shape=[
            jax.ShapeDtypeStruct((ncol, size, width), F32),
            jax.ShapeDtypeStruct((ncol, 2, ncol), F32),
        ],
        in_specs=[vm(), vm(), vm()],
        out_specs=[pl.BlockSpec(memory_space=pl.ANY), vm()],
        scratch_shapes=[
            pltpu.VMEM((2, ncol * ncol, 8, width), F32),
            pltpu.VMEM((ncol, size, width), F32),
            pltpu.SemaphoreType.DMA((rows,)),
        ],
        compiler_params=pltpu.CompilerParams(vmem_limit_bytes=LIMIT),
        name="basis",
    )(gram, early, late)
    return basis.reshape(ncol, rows, nz, width), factor.transpose(1, 0, 2)


def solution(mesh):
    in_specs = (P(None, "trans", "beam", None), P(), P(), P(), P("trans", "beam", None))
    out_specs = (P(None, "trans", "beam", None), P())
    return jax.shard_map(shards, mesh=mesh, in_specs=in_specs, out_specs=out_specs, check_vma=False)
```

```python
import functools

import jax
import jax.numpy as jnp
from jax import lax
from jax.experimental import pallas as pl
from jax.experimental.pallas import tpu as pltpu
from jax.sharding import PartitionSpec as P

POWERS = 4
F32 = jnp.float32
BF16 = jnp.bfloat16
LIMIT = 16 * 1024 * 1024


def split(v):
    high = v.astype(BF16)
    return high, (v - high.astype(F32)).astype(BF16)


def passed(x, by):
    peers = lax.axis_size("beam")
    return lax.ppermute(x, "beam", [(i, i + by) for i in range(peers) if 0 <= i + by < peers])


PAD = 8


def apply_local(nx, nz, width, refs, col, load, prev, halo, scale, out, bridge_ref, ready=None):
    pot_ref, kz_ref, kx_ref, wy_ref, wvec_ref = refs
    col_ref, stride = col
    out_ref, x_start, out_x = out
    out_stride = nz + PAD
    half = width // 2
    left = lax.broadcasted_iota(jnp.int32, (nz, width), 1) < half

    def product(k_ref, us):
        parts = [split(u) for u in us]
        rows = []
        for p, q in (parts[0:2], parts[2:4]):
            rows += [jnp.concatenate([p[0], q[0]], axis=1), jnp.concatenate([p[1], q[1]], axis=1)]
        got = jnp.dot(k_ref[...], jnp.concatenate(rows, axis=0), preferred_element_type=F32)
        m = got.shape[0] // 4
        outs = []
        for i in range(2):
            both = got[2 * i * m : (2 * i + 1) * m] + got[(2 * i + 1) * m : (2 * i + 2) * m]
            outs += [both[:, :width], both[:, width:]]
        return outs, parts

    def local_four(x0):
        us = [load(x_start + x0 + q) for q in range(4)]
        along_z, parts = product(kz_ref, us)
        along_y = jnp.dot(
            jnp.concatenate([jnp.concatenate(p, axis=1) for p in parts], axis=0),
            wy_ref[...],
            preferred_element_type=F32,
        )
        for q in range(4):
            x = x_start + x0 + q
            ay = along_y[q * nz : (q + 1) * nz]
            new = along_z[q] + ay[:, :width] + ay[:, width:]
            new = new + scale * optical(us[q], pot_ref[rows_of(x, nz, nz), :], left)
            if prev is not None:
                new = new - prev[0][rows_of(x, prev[1], nz), :]
            if halo is not None:
                new = with_halo(new, halo, x)
            out_ref[rows_of(x0 + q, out_stride, nz), :] = new

    if ready is None:
        repeat(out_x // 4, 8, only(lambda i: local_four(i * 4)), 0)
    else:
        for h in range(2):
            ready(h)
            repeat(out_x // 8, 8, only(lambda i, h=h: local_four((h * out_x // 8 + i) * 4)), 0)

    def across_four(i, bridge):
        z0 = i * 4
        us = [col_ref[pl.ds(z0 + q, nx, stride=stride), :] for q in range(4)]
        along_x, _ = product(kx_ref, us)
        for q in range(4):
            at = pl.ds(z0 + q, out_x, stride=out_stride)
            new = out_ref[at, :] + along_x[q]
            out_ref[at, :] = new
            if bridge_ref is not None:
                bridge = bridge + wvec_ref[pl.ds(z0 + q, 1), :] * new
        return bridge

    bridge = repeat(nz // 4, 8, across_four, jnp.zeros((out_x, width), F32))
    if bridge_ref is not None:
        bridge_ref[...] = bridge


def rows_of(x, stride, nz):
    return pl.ds(pl.multiple_of(x * stride, 8), nz)


def optical(u, pot, left):
    half = u.shape[-1] // 2
    turned = pltpu.roll(pot, half, 1)
    return jnp.where(left, pot, turned) * u + jnp.where(left, turned, -pot) * pltpu.roll(u, half, 1)


def with_halo(u, halo, x):
    column_ref, plane_ref, sum_ref, scale = halo
    top = lax.broadcasted_iota(jnp.int32, (8, u.shape[-1]), 0) == 0
    u = u + column_ref[...] * (scale * plane_ref[pl.ds(x, 1), :])
    head = u[0:8] + jnp.where(top, scale * sum_ref[pl.ds(x, 1), :], 0.0)
    return jnp.concatenate([head, u[8:]], axis=0)


def repeat(count, unroll, body, carry):
    unroll = min(unroll, count)

    def some(i, carry):
        for q in range(unroll):
            carry = body(i * unroll + q, carry)
        return carry

    return lax.fori_loop(0, count // unroll, some, carry)


def only(body):
    def with_carry(i, carry):
        body(i)
        return carry

    return with_carry


def copies_body(packets_ref, sent_ref, sems):
    npack = packets_ref.shape[0]
    copies = [
        pltpu.make_async_copy(packets_ref, sent_ref.at[pl.ds(i * npack, npack)], sems.at[i])
        for i in range(sent_ref.shape[0] // npack)
    ]
    for copy in copies:
        copy.start()
    for copy in copies:
        copy.wait()


def planes_body(nz, packets_ref, pot_ref, wvec_ref, kvec_ref, mvec_ref, first_ref, bridge_ref, zrest_ref, brest_ref):
    npack, size, width = packets_ref.shape
    rows = size // nz
    left = lax.broadcasted_iota(jnp.int32, (nz, width), 1) < width // 2
    for p in range(npack):
        for x in range(rows):
            u = packets_ref[p, x * nz : (x + 1) * nz, :]
            v = optical(u, pot_ref[x * nz : (x + 1) * nz, :], left)
            at = slice(p * rows + x, p * rows + x + 1)
            first_ref[at, :] = u[0:1]
            bridge_ref[at, :] = jnp.sum(wvec_ref[...] * u, axis=0, keepdims=True)
            zrest_ref[at, :] = v[0:1] + jnp.sum(kvec_ref[...] * u, axis=0, keepdims=True)
            brest_ref[at, :] = jnp.sum(wvec_ref[...] * v + mvec_ref[...] * u, axis=0, keepdims=True)


def element_matrix(scal, ek):
    nz = ek.shape[0] - 1
    r = lax.broadcasted_iota(jnp.int32, (nz, nz), 0)
    c = lax.broadcasted_iota(jnp.int32, (nz, nz), 1)
    corner = (r == 0) & (c == 0) & (scal[2] > 0)
    return ek[0:nz, 0:nz] + jnp.where(corner, ek[nz : nz + 1, nz : nz + 1], 0.0)


def vectors_body(scal, ek_ref, rcol, kvec, mvec, coef):
    nz, width = rcol.shape
    kz = element_matrix(scal, ek_ref)
    edge_vectors(ek_ref, rcol, coef)
    kvec[...] = jnp.broadcast_to(kz[:, 0:1], (nz, width))
    bridge = ek_ref[nz : nz + 1, 0:nz]
    mvec[...] = jnp.broadcast_to(jnp.sum(kz * bridge, axis=1, keepdims=True), (nz, width))


def edge_vectors(ek_ref, rcol, coef):
    nz, width = rcol.shape
    rcol[...] = jnp.broadcast_to(ek_ref[0:nz, nz : nz + 1], (nz, width))
    coef[...] = jnp.zeros_like(coef)
    coef[0:1, :] = rcol[0:1, :]
    coef[1:2, :] = jnp.sum(rcol[...] * rcol[...], axis=0, keepdims=True)


def matrices(scal, kx_ref, ky_ref, ek_ref, kz1, kx1, wy1, kz2, kx2, wy2, kx4, kyd):
    chip = kx4.shape[0] // 4

    def split_wide(k):
        high = k.astype(BF16).astype(F32)
        return high, k - high

    def left_weights(k):
        high, low = split_wide(k)
        none = jnp.zeros_like(high)
        block = jnp.concatenate(
            [jnp.concatenate([high, high], axis=1), jnp.concatenate([low, none], axis=1)], axis=0
        )
        none = jnp.zeros_like(block)
        return jnp.concatenate(
            [jnp.concatenate([block, none], axis=1), jnp.concatenate([none, block], axis=1)], axis=0
        )

    for one, two, k in ((kz1, kz2, element_matrix(scal, ek_ref)), (kx1, kx2, kx_ref[...])):
        block = left_weights(k)
        one[...] = block.astype(BF16)
        two[...] = (2.0 * block).astype(BF16)
    kx4[...] = left_weights(2.0 * kx_ref[pl.ds(pl.multiple_of(scal[0], 8), chip), :]).astype(BF16)
    ky = ky_ref[...]
    none = jnp.zeros_like(ky)
    ky = jnp.concatenate(
        [jnp.concatenate([ky, none], axis=1), jnp.concatenate([none, ky], axis=1)], axis=0
    )
    kyd[...] = ky
    high, low = split_wide(ky)
    block = jnp.concatenate(
        [jnp.concatenate([high, low], axis=1), jnp.concatenate([high, jnp.zeros_like(low)], axis=1)],
        axis=0,
    )
    wy1[...] = block.astype(BF16)
    wy2[...] = (2.0 * block).astype(BF16)


def edges_body(scale, first_ref, bridge_ref, pin_ref, bin_ref, coef_ref, out_first, out_bridge):
    head, square = coef_ref[0:1, :], coef_ref[1:2, :]
    pin, bin_ = scale * pin_ref[...], scale * bin_ref[...]
    out_first[...] = first_ref[...] + head * pin + bin_
    out_bridge[...] = bridge_ref[...] + square * pin + head * bin_


def pair_body(nx, nz, width, chip, scal, cur_ref, gathered_ref, pot_hbm, kx_hbm, ky_hbm, ek_hbm, *refs):
    one_ref, two_ref, first_ref, bridge_ref, rows1_ref, rows2_ref, pot_ref = refs[:7]
    kz2, kx2, wy2, kx4, rcol, coef = refs[7:13]
    col_ref, planes_ref, halo_ref, sems, kx_ref, ky_raw, ek_ref, kz1, kx1, wy1, ky_ref = refs[13:]
    stride = nz + PAD
    small = [
        pltpu.make_async_copy(src, dst, sems.at[2 + i])
        for i, (src, dst) in enumerate(((kx_hbm, kx_ref), (ky_hbm, ky_raw), (ek_hbm, ek_ref)))
    ]
    for copy in small:
        copy.start()
    part = nx * nz // 2
    copies = [
        pltpu.make_async_copy(
            pot_hbm.at[pl.ds(h * part, part), :], pot_ref.at[pl.ds(h * part, part), :], sems.at[h]
        )
        for h in range(2)
    ]
    for copy in copies:
        copy.start()

    trans, planes, each, _ = gathered_ref.shape
    each = each // 2
    for t in range(trans):
        for q in range(planes):
            planes_ref[q, t * each : (t + 1) * each, :] = gathered_ref[
                t, q, pl.ds(pl.multiple_of(scal[1] * each, 8), each), :
            ]
    for copy in small:
        copy.wait()
    matrices(scal, kx_ref, ky_raw, ek_ref, kz1, kx1, wy1, kz2, kx2, wy2, kx4, ky_ref)
    edge_vectors(ek_ref, rcol, coef)
    precise = lax.Precision.HIGHEST
    for q in range(2):
        plane = planes_ref[q]
        moved = jnp.dot(kx_ref[...], plane, precision=precise, preferred_element_type=F32)
        moved = moved + jnp.dot(plane, ky_ref[...], precision=precise, preferred_element_type=F32)
        halo_ref[q] = moved + planes_ref[2 + q]

    def packed(x):
        u = cur_ref[rows_of(x, nz, nz), :]
        col_ref[rows_of(x, stride, nz), :] = u
        return u

    apply_local(
        nx, nz, width, (pot_ref, kz1, kx1, wy1, rcol), (col_ref, stride), packed, None,
        (rcol, planes_ref.at[0], planes_ref.at[1], 1.0), 1.0, (one_ref, 0, nx), None,
        ready=lambda h: copies[h].wait(),
    )
    apply_local(
        nx, nz, width, (pot_ref, kz2, kx2, wy2, rcol), (one_ref, stride),
        lambda x: one_ref[rows_of(x, stride, nz), :], (cur_ref, nz),
        (rcol, halo_ref.at[0], halo_ref.at[1], 2.0), 2.0, (two_ref, 0, nx), bridge_ref,
    )
    first_ref[...] = two_ref[pl.ds(0, nx, stride=stride), :]
    for ref, rows_ref in ((one_ref, rows1_ref), (two_ref, rows2_ref)):
        for q in range(chip):
            rows_ref[q * nz : (q + 1) * nz, :] = ref[rows_of(scal[0] + q, stride, nz), :]


def third_body(nx, nz, width, cur_ref, prev_ref, pot_ref, kz, kx, wy, rcol, out_ref, first_ref, bridge_ref):
    stride = nz + PAD
    apply_local(
        nx, nz, width, (pot_ref, kz, kx, wy, rcol), (cur_ref, stride),
        lambda x: cur_ref[rows_of(x, stride, nz), :], (prev_ref, stride), None, 2.0,
        (out_ref, 0, nx), bridge_ref,
    )
    first_ref[...] = out_ref[pl.ds(0, nx, stride=stride), :]


def fourth_body(nx, nz, width, chip, scal, cur_ref, pin_ref, bin_ref, prev_ref, pot_ref, *refs):
    kz, kx, wy, rcol, out_ref, rows_ref, col_ref = refs
    stride = nz + PAD

    def complete(x):
        u = with_halo(cur_ref[rows_of(x, stride, nz), :], (rcol, pin_ref, bin_ref, 2.0), x)
        col_ref[rows_of(x, stride, nz), :] = u

    repeat(nx, 16, only(complete), 0)
    for q in range(chip):
        rows_ref[q * nz : (q + 1) * nz, :] = col_ref[rows_of(scal[0] + q, stride, nz), :]
    apply_local(
        nx, nz, width, (pot_ref, kz, kx, wy, rcol), (col_ref, stride),
        lambda x: col_ref[rows_of(x, stride, nz), :], (prev_ref, stride), None, 2.0,
        (out_ref, scal[0], chip), None,
    )


def vm():
    return pl.BlockSpec(memory_space=pltpu.VMEM)


def in_vmem(*shape):
    return pltpu.VMEM(shape, F32)


def call(name, body, outs, *ins, scal=None, scratch=(), cost=4, away=()):
    specs = [pl.BlockSpec(memory_space=pltpu.HBM) if i in away else vm() for i in range(len(ins))]
    ins = tuple(
        pltpu.with_memory_space_constraint(x, pltpu.HBM) if i in away else x for i, x in enumerate(ins)
    )
    if scal is not None:
        specs = [pl.BlockSpec(memory_space=pltpu.SMEM)] + specs
        ins = (scal,) + ins
    return pl.pallas_call(
        body,
        out_shape=outs,
        in_specs=specs,
        out_specs=[vm()] * len(outs),
        scratch_shapes=list(scratch),
        compiler_params=pltpu.CompilerParams(vmem_limit_bytes=LIMIT),
        cost_estimate=pl.CostEstimate(
            flops=cost * 10**9, bytes_accessed=2 * cost * 10**6, transcendentals=0
        ),
        name=name,
    )(*ins)


def finish_body(nz, rows, scal, last_ref, pin_ref, bin_ref, rcol_ref, *refs):
    cols = refs[: POWERS - 1]
    keep_ref, send_ref = refs[POWERS - 1 :]
    core = scal[1]
    size = rows * nz
    halo = (rcol_ref, pin_ref, bin_ref, 2.0)
    for ref, where in ((keep_ref, core), (send_ref, 1 - core)):
        at = pl.ds(pl.multiple_of(where * size, size), size)
        for k in range(POWERS - 1):
            ref[k] = cols[k][at, :]
        for r in range(rows):
            x = where * rows + r
            u = with_halo(last_ref[rows_of(x, nz + PAD, nz), :], halo, scal[0] + x)
            ref[POWERS - 1, r * nz : (r + 1) * nz, :] = u


def gram_body(scal, packets_ref, keep_ref, recv_ref, cols_ref, gram_ref, acc_ref):
    core = scal[1]
    ncol, size, width = cols_ref.shape
    npow = ncol // 2
    half = width // 2
    cols_ref[0] = packets_ref[0]
    cols_ref[npow] = packets_ref[1]
    for k in range(npow - 1):
        cols_ref[core * npow + 1 + k] = keep_ref[k]
        cols_ref[(1 - core) * npow + 1 + k] = recv_ref[k]
    acc_ref[...] = jnp.zeros_like(acc_ref)
    sign = jnp.where(lax.broadcasted_iota(jnp.int32, (8, width), 1) < half, 1.0, -1.0)
    first, second = list(range(npow)), list(range(npow, ncol))
    groups = [
        [(a, b) for a in first for b in first if a <= b],
        [(a, b) for a in second for b in second if a <= b],
        [(a, b) for a in first for b in second[:3]],
        [(a, b) for a in first for b in second[3:]],
    ]
    unroll = 32
    for pairs in groups:
        used = sorted({c for pair in pairs for c in pair})
        turned = sorted({b for a, b in pairs if a != b})

        def chunk(i, sums, pairs=pairs, used=used, turned=turned):
            sums = list(sums)
            for q in range(unroll):
                at = pl.ds(pl.multiple_of((i * unroll + q) * 8, 8), 8)
                v = {c: cols_ref[c, at, :] for c in used}
                t = {c: pltpu.roll(v[c], half, 1) for c in turned}
                n = 0
                for a, b in pairs:
                    sums[n] = sums[n] + v[a] * v[b]
                    n += 1
                    if a != b:
                        sums[n] = sums[n] + v[a] * t[b]
                        n += 1
            return tuple(sums)

        count = sum(1 if a == b else 2 for a, b in pairs)
        sums = lax.fori_loop(
            0, size // (8 * unroll), chunk, tuple(jnp.zeros((8, width), F32) for _ in range(count))
        )
        n = 0
        for a, b in pairs:
            acc_ref[a * ncol + b : a * ncol + b + 1, :] = jnp.sum(sums[n], axis=0, keepdims=True)
            n += 1
            if a != b:
                acc_ref[b * ncol + a : b * ncol + a + 1, :] = jnp.sum(
                    sums[n] * sign, axis=0, keepdims=True
                )
                n += 1
    row = jnp.sum(acc_ref[...].T, axis=0, keepdims=True)
    gram_ref[...] = jnp.broadcast_to(row[None], gram_ref.shape)


def basis_body(cells, rows, gram_ref, cols_ref, basis_ref, factor_ref, coef_ref, out_ref, sems):
    ncol, size, width = cols_ref.shape
    half = width // 2
    row = jnp.sum(gram_ref[...], axis=0) * (1.0 / cells)
    r = lax.broadcasted_iota(jnp.int32, (16, width), 0)
    c = lax.broadcasted_iota(jnp.int32, (16, width), 1)
    packed = jnp.zeros((16, width), F32)
    for j in range(ncol):
        moved = row if j == 0 else pltpu.roll(row, width - ncol * j, 1)
        packed = jnp.where(r == j, moved, packed)
    turned = jnp.concatenate([packed, jnp.zeros((width - 16, width), F32)], axis=0).T[:16]
    inside = (r < ncol) & (c < ncol)
    re = jnp.where(inside, jnp.where(r <= c, packed, turned), 0.0)
    im = jnp.where(inside & (r != c), jnp.where(r < c, turned, -packed), 0.0)
    re = jnp.where(c == r + 16, 1.0, re)
    up_re = jnp.zeros((16, width), F32)
    up_im = jnp.zeros((16, width), F32)
    for j in range(ncol):
        pivot = jnp.sqrt(re[j : j + 1, j : j + 1])
        inverse = 1.0 / pivot
        row_re = re[j : j + 1, :] * inverse
        row_im = im[j : j + 1, :] * inverse
        col_re = re[:, j : j + 1] * inverse
        col_im = im[:, j : j + 1] * inverse
        up_re = jnp.where(r == j, row_re, up_re)
        up_im = jnp.where(r == j, row_im, up_im)
        below = r > j
        re = re - jnp.where(below, col_re * row_re - col_im * row_im, 0.0)
        im = im - jnp.where(below, col_re * row_im + col_im * row_re, 0.0)
    for q, up in ((0, jnp.where(c >= r, up_re, 0.0)), (1, jnp.where(c > r, up_im, 0.0))):
        for k in range(ncol):
            factor_ref[k, q : q + 1, :] = up[k : k + 1, :ncol]
    sign = jnp.where(lax.broadcasted_iota(jnp.int32, (8, width), 1) < half, 1.0, -1.0)
    for k in range(ncol):
        for i in range(k + 1):
            coef_ref[0, k * ncol + i] = jnp.broadcast_to(up_re[k : k + 1, 16 + i : 17 + i], (8, width))
            coef_ref[1, k * ncol + i] = (
                jnp.broadcast_to(up_im[k : k + 1, 16 + i : 17 + i], (8, width)) * sign
            )
    group = 4
    each = size // rows

    def row(r, carry):
        for start in range(0, each, 8 * group):
            slots = [pl.ds(pl.multiple_of(r * each + start + 8 * g, 8), 8) for g in range(group)]
            v = [[cols_ref[i, s, :] for s in slots] for i in range(ncol)]
            t = [[pltpu.roll(x, half, 1) for x in xs] for xs in v]
            for k in range(ncol):
                total = [None] * group
                for i in range(k + 1):
                    re = coef_ref[0, k * ncol + i]
                    im = coef_ref[1, k * ncol + i]
                    for g in range(group):
                        term = re * v[i][g]
                        if i < k:
                            term = term + im * t[i][g]
                        total[g] = term if total[g] is None else total[g] + term
                for g in range(group):
                    out_ref[k, slots[g], :] = total[g]
        copy(r).start()
        return carry

    def copy(r):
        part = pl.ds(pl.multiple_of(r * each, 8), each)
        return pltpu.make_async_copy(out_ref.at[:, part, :], basis_ref.at[:, part, :], sems.at[r])

    lax.fori_loop(0, rows, row, 0)
    for r in range(rows):
        copy(r).wait()


def shards(packets, kinetic_x, kinetic_y, element_kinetic, potential):
    npack, rows, nz, width = packets.shape
    trans = lax.axis_size("trans")
    nx = rows * trans
    ncol = npack * (POWERS + 1)
    me = lax.axis_index("trans")
    core = me % 2
    chip = 2 * rows
    scal = jnp.stack([(me // 2) * chip, core, lax.axis_index("beam")]).astype(jnp.int32)

    size = rows * nz
    flat = packets.reshape(npack, size, width)
    mine = potential.reshape(size, width)
    pot = lax.all_gather(mine, "trans", axis=0, tiled=True)
    sent = pl.pallas_call(
        copies_body,
        out_shape=jax.ShapeDtypeStruct((trans, size, width), F32),
        in_specs=[vm()],
        out_specs=pl.BlockSpec(memory_space=pl.ANY),
        scratch_shapes=[pltpu.SemaphoreType.DMA((trans // npack,))],
        compiler_params=pltpu.CompilerParams(vmem_limit_bytes=LIMIT),
        name="copies",
    )(flat)
    cur = lax.all_to_all(sent, "trans", 0, 0, tiled=True).reshape(nx * nz, width)
    sent, flat_late, mine_late, ek_late = lax.optimization_barrier(
        (sent, flat, mine, element_kinetic)
    )

    def half_wide(*shape):
        return pltpu.VMEM(shape, BF16)

    square, column = half_wide(4 * nz, 4 * nz), in_vmem(nz, width)
    across = half_wide(4 * nx, 4 * nx)
    wide = half_wide(2 * width, 2 * width)
    rcol, kvec, mvec, coef = call(
        "vectors", vectors_body, [column, column, column, in_vmem(8, width)], ek_late, scal=scal, cost=1
    )

    plane = in_vmem(npack * rows, width)
    first, bridge, zrest, brest = call(
        "planes", functools.partial(planes_body, nz), [plane] * 4,
        flat_late, mine_late, rcol, kvec, mvec, cost=1,
    )
    pin, bin_ = passed(first, -1), passed(bridge, 1)
    pnext, bnext = call(
        "edges", functools.partial(edges_body, 1.0), [plane] * 2, zrest, brest, pin, bin_, coef, cost=1
    )
    planes = jnp.stack([pin, bin_, passed(pnext, -1), passed(bnext, 1)])
    planes = lax.all_gather(planes, "trans")

    full, edge = in_vmem(nx * (nz + PAD), width), in_vmem(nx, width)
    here = in_vmem(chip * nz, width)
    col1, col2, first, bridge, rows1, rows2, pot, kz2, kx2, wy2, kx4, rcol, coef = call(
        "pair", functools.partial(pair_body, nx, nz, width, chip),
        [full, full, edge, edge, here, here, in_vmem(nx * nz, width),
         square, across, wide, half_wide(4 * chip, 4 * nx), column, in_vmem(8, width)],
        cur, planes, pot, kinetic_x, kinetic_y, element_kinetic,
        scal=scal, cost=8, away=(2, 3, 4, 5),
        scratch=[full, in_vmem(4, nx, width), in_vmem(2, nx, width), pltpu.SemaphoreType.DMA((5,)),
                 in_vmem(*kinetic_x.shape), in_vmem(*kinetic_y.shape), in_vmem(*element_kinetic.shape),
                 square, across, wide, in_vmem(width, width)],
    )
    pin, bin_ = passed(first, -1), passed(bridge, 1)
    col3, first, bridge = call(
        "third", functools.partial(third_body, nx, nz, width), [full, edge, edge],
        col2, col1, pot, kz2, kx2, wy2, rcol,
    )
    first, bridge = call(
        "edges", functools.partial(edges_body, 2.0), [edge] * 2, first, bridge, pin, bin_, coef, cost=1
    )
    plast, blast = passed(first, -1), passed(bridge, 1)
    local, rows3 = call(
        "fourth", functools.partial(fourth_body, nx, nz, width, chip),
        [in_vmem(chip * (nz + PAD), width), here],
        col3, pin, bin_, col2, pot, kz2, kx4, wy2, rcol,
        scal=scal, scratch=[full], cost=2,
    )
    columns = [rows1, rows2, rows3]
    keep, send = pl.pallas_call(
        functools.partial(finish_body, nz, rows),
        out_shape=[in_vmem(POWERS, size, width)] * 2,
        in_specs=[pl.BlockSpec(memory_space=pltpu.SMEM)] + [vm()] * (4 + POWERS - 1),
        out_specs=[vm()] * 2,
        compiler_params=pltpu.CompilerParams(vmem_limit_bytes=LIMIT),
        name="finish",
    )(scal, local, plast, blast, rcol, *columns)
    recv = lax.ppermute(send, "trans", [(i, i ^ 1) for i in range(trans)])
    cols, gram = pl.pallas_call(
        gram_body,
        out_shape=[in_vmem(ncol, size, width), in_vmem(trans, 1, width)],
        in_specs=[pl.BlockSpec(memory_space=pltpu.SMEM)] + [vm()] * 3,
        out_specs=[vm()] * 2,
        scratch_shapes=[pltpu.VMEM((128, width), F32)],
        compiler_params=pltpu.CompilerParams(vmem_limit_bytes=LIMIT),
        name="gram",
    )(scal, packets.reshape(npack, size, width), keep, recv)
    beam = lax.axis_size("beam")
    gram = jnp.sum(lax.all_to_all(gram, "trans", 0, 0, tiled=True), axis=0, keepdims=True)
    gram = lax.all_to_all(jnp.broadcast_to(gram, (beam, 1, width)), "beam", 0, 0, tiled=True)
    cells = float(nx * (width // 2) * nz * beam)
    basis, factor = pl.pallas_call(
        functools.partial(basis_body, cells, rows),
        out_shape=[
            jax.ShapeDtypeStruct((ncol, size, width), F32),
            jax.ShapeDtypeStruct((ncol, 2, ncol), F32),
        ],
        in_specs=[vm(), vm()],
        out_specs=[pl.BlockSpec(memory_space=pl.ANY), vm()],
        scratch_shapes=[
            pltpu.VMEM((2, ncol * ncol, 8, width), F32),
            pltpu.VMEM((ncol, size, width), F32),
            pltpu.SemaphoreType.DMA((rows,)),
        ],
        compiler_params=pltpu.CompilerParams(vmem_limit_bytes=LIMIT),
        name="basis",
    )(gram, cols)
    return basis.reshape(ncol, rows, nz, width), factor.transpose(1, 0, 2)


def solution(mesh):
    in_specs = (P(None, "trans", "beam", None), P(), P(), P(), P("trans", "beam", None))
    out_specs = (P(None, "trans", "beam", None), P())
    return jax.shard_map(shards, mesh=mesh, in_specs=in_specs, out_specs=out_specs, check_vma=False)
```

```python
import functools

import jax
import jax.numpy as jnp
from jax import lax
from jax.experimental import pallas as pl
from jax.experimental.pallas import tpu as pltpu
from jax.sharding import PartitionSpec as P

POWERS = 4
F32 = jnp.float32
BF16 = jnp.bfloat16
LIMIT = 16 * 1024 * 1024


def split(v):
    high = v.astype(BF16)
    return high, (v - high.astype(F32)).astype(BF16)


def passed(x, by):
    peers = lax.axis_size("beam")
    return lax.ppermute(x, "beam", [(i, i + by) for i in range(peers) if 0 <= i + by < peers])


PAD = 8


def apply_local(nx, nz, width, refs, col, load, prev, halo, scale, out, bridge_ref, ready=None):
    pot_ref, kz_ref, kx_ref, wy_ref, wvec_ref = refs
    col_ref, stride = col
    out_ref, x_start, out_x = out
    out_stride = nz + PAD
    half = width // 2
    left = lax.broadcasted_iota(jnp.int32, (nz, width), 1) < half

    def product(k_ref, us):
        parts = [split(u) for u in us]
        rows = []
        for p, q in (parts[0:2], parts[2:4]):
            rows += [jnp.concatenate([p[0], q[0]], axis=1), jnp.concatenate([p[1], q[1]], axis=1)]
        got = jnp.dot(k_ref[...], jnp.concatenate(rows, axis=0), preferred_element_type=F32)
        m = got.shape[0] // 4
        outs = []
        for i in range(2):
            both = got[2 * i * m : (2 * i + 1) * m] + got[(2 * i + 1) * m : (2 * i + 2) * m]
            outs += [both[:, :width], both[:, width:]]
        return outs, parts

    def local_four(x0):
        us = [load(x_start + x0 + q) for q in range(4)]
        along_z, parts = product(kz_ref, us)
        along_y = jnp.dot(
            jnp.concatenate([jnp.concatenate(p, axis=1) for p in parts], axis=0),
            wy_ref[...],
            preferred_element_type=F32,
        )
        for q in range(4):
            x = x_start + x0 + q
            ay = along_y[q * nz : (q + 1) * nz]
            new = along_z[q] + ay[:, :width] + ay[:, width:]
            new = new + scale * optical(us[q], pot_ref[rows_of(x, nz, nz), :], left)
            if prev is not None:
                new = new - prev[0][rows_of(x, prev[1], nz), :]
            if halo is not None:
                new = with_halo(new, halo, x)
            out_ref[rows_of(x0 + q, out_stride, nz), :] = new

    if ready is None:
        repeat(out_x // 4, 8, only(lambda i: local_four(i * 4)), 0)
    else:
        for h in range(2):
            ready(h)
            repeat(out_x // 8, 8, only(lambda i, h=h: local_four((h * out_x // 8 + i) * 4)), 0)

    def across_four(i, bridge):
        z0 = i * 4
        us = [col_ref[pl.ds(z0 + q, nx, stride=stride), :] for q in range(4)]
        along_x, _ = product(kx_ref, us)
        for q in range(4):
            at = pl.ds(z0 + q, out_x, stride=out_stride)
            new = out_ref[at, :] + along_x[q]
            out_ref[at, :] = new
            if bridge_ref is not None:
                bridge = bridge + wvec_ref[pl.ds(z0 + q, 1), :] * new
        return bridge

    bridge = repeat(nz // 4, 8, across_four, jnp.zeros((out_x, width), F32))
    if bridge_ref is not None:
        bridge_ref[...] = bridge


def rows_of(x, stride, nz):
    return pl.ds(pl.multiple_of(x * stride, 8), nz)


def optical(u, pot, left):
    half = u.shape[-1] // 2
    turned = pltpu.roll(pot, half, 1)
    return jnp.where(left, pot, turned) * u + jnp.where(left, turned, -pot) * pltpu.roll(u, half, 1)


def with_halo(u, halo, x):
    column_ref, plane_ref, sum_ref, scale = halo
    top = lax.broadcasted_iota(jnp.int32, (8, u.shape[-1]), 0) == 0
    u = u + column_ref[...] * (scale * plane_ref[pl.ds(x, 1), :])
    head = u[0:8] + jnp.where(top, scale * sum_ref[pl.ds(x, 1), :], 0.0)
    return jnp.concatenate([head, u[8:]], axis=0)


def repeat(count, unroll, body, carry):
    unroll = min(unroll, count)

    def some(i, carry):
        for q in range(unroll):
            carry = body(i * unroll + q, carry)
        return carry

    return lax.fori_loop(0, count // unroll, some, carry)


def only(body):
    def with_carry(i, carry):
        body(i)
        return carry

    return with_carry


def copies_body(packets_ref, sent_ref, sems):
    npack = packets_ref.shape[0]
    copies = [
        pltpu.make_async_copy(packets_ref, sent_ref.at[pl.ds(i * npack, npack)], sems.at[i])
        for i in range(sent_ref.shape[0] // npack)
    ]
    for copy in copies:
        copy.start()
    for copy in copies:
        copy.wait()


def planes_body(nz, packets_ref, pot_ref, wvec_ref, kvec_ref, mvec_ref, first_ref, bridge_ref, zrest_ref, brest_ref):
    npack, size, width = packets_ref.shape
    rows = size // nz
    left = lax.broadcasted_iota(jnp.int32, (nz, width), 1) < width // 2
    for p in range(npack):
        for x in range(rows):
            u = packets_ref[p, x * nz : (x + 1) * nz, :]
            v = optical(u, pot_ref[x * nz : (x + 1) * nz, :], left)
            at = slice(p * rows + x, p * rows + x + 1)
            first_ref[at, :] = u[0:1]
            bridge_ref[at, :] = jnp.sum(wvec_ref[...] * u, axis=0, keepdims=True)
            zrest_ref[at, :] = v[0:1] + jnp.sum(kvec_ref[...] * u, axis=0, keepdims=True)
            brest_ref[at, :] = jnp.sum(wvec_ref[...] * v + mvec_ref[...] * u, axis=0, keepdims=True)


def element_matrix(scal, ek):
    nz = ek.shape[0] - 1
    r = lax.broadcasted_iota(jnp.int32, (nz, nz), 0)
    c = lax.broadcasted_iota(jnp.int32, (nz, nz), 1)
    corner = (r == 0) & (c == 0) & (scal[2] > 0)
    return ek[0:nz, 0:nz] + jnp.where(corner, ek[nz : nz + 1, nz : nz + 1], 0.0)


def vectors_body(scal, ek_ref, rcol, kvec, mvec, coef):
    nz, width = rcol.shape
    kz = element_matrix(scal, ek_ref)
    edge_vectors(ek_ref, rcol, coef)
    kvec[...] = jnp.broadcast_to(kz[:, 0:1], (nz, width))
    bridge = ek_ref[nz : nz + 1, 0:nz]
    mvec[...] = jnp.broadcast_to(jnp.sum(kz * bridge, axis=1, keepdims=True), (nz, width))


def edge_vectors(ek_ref, rcol, coef):
    nz, width = rcol.shape
    rcol[...] = jnp.broadcast_to(ek_ref[0:nz, nz : nz + 1], (nz, width))
    coef[...] = jnp.zeros_like(coef)
    coef[0:1, :] = rcol[0:1, :]
    coef[1:2, :] = jnp.sum(rcol[...] * rcol[...], axis=0, keepdims=True)


def matrices(scal, kx_ref, ky_ref, ek_ref, kz1, kx1, wy1, kz2, kx2, wy2, kx4, kyd):
    chip = kx4.shape[0] // 4

    def split_wide(k):
        high = k.astype(BF16).astype(F32)
        return high, k - high

    def left_weights(k):
        high, low = split_wide(k)
        none = jnp.zeros_like(high)
        block = jnp.concatenate(
            [jnp.concatenate([high, high], axis=1), jnp.concatenate([low, none], axis=1)], axis=0
        )
        none = jnp.zeros_like(block)
        return jnp.concatenate(
            [jnp.concatenate([block, none], axis=1), jnp.concatenate([none, block], axis=1)], axis=0
        )

    for one, two, k in ((kz1, kz2, element_matrix(scal, ek_ref)), (kx1, kx2, kx_ref[...])):
        block = left_weights(k)
        one[...] = block.astype(BF16)
        two[...] = (2.0 * block).astype(BF16)
    kx4[...] = left_weights(2.0 * kx_ref[pl.ds(pl.multiple_of(scal[0], 8), chip), :]).astype(BF16)
    ky = ky_ref[...]
    none = jnp.zeros_like(ky)
    ky = jnp.concatenate(
        [jnp.concatenate([ky, none], axis=1), jnp.concatenate([none, ky], axis=1)], axis=0
    )
    kyd[...] = ky
    high, low = split_wide(ky)
    block = jnp.concatenate(
        [jnp.concatenate([high, low], axis=1), jnp.concatenate([high, jnp.zeros_like(low)], axis=1)],
        axis=0,
    )
    wy1[...] = block.astype(BF16)
    wy2[...] = (2.0 * block).astype(BF16)


def edges_body(scale, first_ref, bridge_ref, pin_ref, bin_ref, coef_ref, out_first, out_bridge):
    head, square = coef_ref[0:1, :], coef_ref[1:2, :]
    pin, bin_ = scale * pin_ref[...], scale * bin_ref[...]
    out_first[...] = first_ref[...] + head * pin + bin_
    out_bridge[...] = bridge_ref[...] + square * pin + head * bin_


def pair_body(nx, nz, width, chip, scal, cur_ref, gathered_ref, pot_hbm, kx_hbm, ky_hbm, ek_hbm, *refs):
    one_ref, two_ref, first_ref, bridge_ref, rows1_ref, rows2_ref, pot_ref = refs[:7]
    kz2, kx2, wy2, kx4, rcol, coef = refs[7:13]
    col_ref, planes_ref, halo_ref, sems, kx_ref, ky_raw, ek_ref, kz1, kx1, wy1, ky_ref = refs[13:]
    stride = nz + PAD
    small = [
        pltpu.make_async_copy(src, dst, sems.at[2 + i])
        for i, (src, dst) in enumerate(((kx_hbm, kx_ref), (ky_hbm, ky_raw), (ek_hbm, ek_ref)))
    ]
    for copy in small:
        copy.start()
    part = nx * nz // 2
    copies = [
        pltpu.make_async_copy(
            pot_hbm.at[pl.ds(h * part, part), :], pot_ref.at[pl.ds(h * part, part), :], sems.at[h]
        )
        for h in range(2)
    ]
    for copy in copies:
        copy.start()

    trans, planes, each, _ = gathered_ref.shape
    each = each // 2
    for t in range(trans):
        for q in range(planes):
            planes_ref[q, t * each : (t + 1) * each, :] = gathered_ref[
                t, q, pl.ds(pl.multiple_of(scal[1] * each, 8), each), :
            ]
    for copy in small:
        copy.wait()
    matrices(scal, kx_ref, ky_raw, ek_ref, kz1, kx1, wy1, kz2, kx2, wy2, kx4, ky_ref)
    edge_vectors(ek_ref, rcol, coef)
    precise = lax.Precision.HIGHEST
    for q in range(2):
        plane = planes_ref[q]
        moved = jnp.dot(kx_ref[...], plane, precision=precise, preferred_element_type=F32)
        moved = moved + jnp.dot(plane, ky_ref[...], precision=precise, preferred_element_type=F32)
        halo_ref[q] = moved + planes_ref[2 + q]

    def packed(x):
        u = cur_ref[rows_of(x, nz, nz), :]
        col_ref[rows_of(x, stride, nz), :] = u
        return u

    apply_local(
        nx, nz, width, (pot_ref, kz1, kx1, wy1, rcol), (col_ref, stride), packed, None,
        (rcol, planes_ref.at[0], planes_ref.at[1], 1.0), 1.0, (one_ref, 0, nx), None,
        ready=lambda h: copies[h].wait(),
    )
    apply_local(
        nx, nz, width, (pot_ref, kz2, kx2, wy2, rcol), (one_ref, stride),
        lambda x: one_ref[rows_of(x, stride, nz), :], (cur_ref, nz),
        (rcol, halo_ref.at[0], halo_ref.at[1], 2.0), 2.0, (two_ref, 0, nx), bridge_ref,
    )
    first_ref[...] = two_ref[pl.ds(0, nx, stride=stride), :]
    for ref, rows_ref in ((one_ref, rows1_ref), (two_ref, rows2_ref)):
        for q in range(chip):
            rows_ref[q * nz : (q + 1) * nz, :] = ref[rows_of(scal[0] + q, stride, nz), :]


def third_body(nx, nz, width, cur_ref, prev_ref, pot_ref, kz, kx, wy, rcol, out_ref, first_ref, bridge_ref):
    stride = nz + PAD
    apply_local(
        nx, nz, width, (pot_ref, kz, kx, wy, rcol), (cur_ref, stride),
        lambda x: cur_ref[rows_of(x, stride, nz), :], (prev_ref, stride), None, 2.0,
        (out_ref, 0, nx), bridge_ref,
    )
    first_ref[...] = out_ref[pl.ds(0, nx, stride=stride), :]


def fourth_body(nx, nz, width, chip, scal, cur_ref, pin_ref, bin_ref, prev_ref, pot_ref, *refs):
    kz, kx, wy, rcol, out_ref, rows_ref, col_ref = refs
    stride = nz + PAD

    def complete(x):
        u = with_halo(cur_ref[rows_of(x, stride, nz), :], (rcol, pin_ref, bin_ref, 2.0), x)
        col_ref[rows_of(x, stride, nz), :] = u

    repeat(nx, 16, only(complete), 0)
    for q in range(chip):
        rows_ref[q * nz : (q + 1) * nz, :] = col_ref[rows_of(scal[0] + q, stride, nz), :]
    apply_local(
        nx, nz, width, (pot_ref, kz, kx, wy, rcol), (col_ref, stride),
        lambda x: col_ref[rows_of(x, stride, nz), :], (prev_ref, stride), None, 2.0,
        (out_ref, scal[0], chip), None,
    )


def vm():
    return pl.BlockSpec(memory_space=pltpu.VMEM)


def in_vmem(*shape):
    return pltpu.VMEM(shape, F32)


def call(name, body, outs, *ins, scal=None, scratch=(), cost=4, away=()):
    specs = [pl.BlockSpec(memory_space=pltpu.HBM) if i in away else vm() for i in range(len(ins))]
    ins = tuple(
        pltpu.with_memory_space_constraint(x, pltpu.HBM) if i in away else x for i, x in enumerate(ins)
    )
    if scal is not None:
        specs = [pl.BlockSpec(memory_space=pltpu.SMEM)] + specs
        ins = (scal,) + ins
    return pl.pallas_call(
        body,
        out_shape=outs,
        in_specs=specs,
        out_specs=[vm()] * len(outs),
        scratch_shapes=list(scratch),
        compiler_params=pltpu.CompilerParams(vmem_limit_bytes=LIMIT),
        cost_estimate=pl.CostEstimate(
            flops=cost * 10**9, bytes_accessed=2 * cost * 10**6, transcendentals=0
        ),
        name=name,
    )(*ins)


def finish_body(nz, rows, scal, last_ref, pin_ref, bin_ref, rcol_ref, *refs):
    cols = refs[: POWERS - 1]
    keep_ref, send_ref = refs[POWERS - 1 :]
    core = scal[1]
    size = rows * nz
    halo = (rcol_ref, pin_ref, bin_ref, 2.0)
    for ref, where in ((keep_ref, core), (send_ref, 1 - core)):
        at = pl.ds(pl.multiple_of(where * size, size), size)
        for k in range(POWERS - 1):
            ref[k] = cols[k][at, :]
        for r in range(rows):
            x = where * rows + r
            u = with_halo(last_ref[rows_of(x, nz + PAD, nz), :], halo, scal[0] + x)
            ref[POWERS - 1, r * nz : (r + 1) * nz, :] = u


def product_sums(load, chunks, pairs, unroll, sums):
    used = sorted({c for pair in pairs for c in pair})
    turned = sorted({b for a, b in pairs if a != b})

    def chunk(i, sums):
        sums = list(sums)
        for q in range(unroll):
            v = {c: load(c, (i * unroll + q) * 8) for c in used}
            t = {c: pltpu.roll(v[c], v[c].shape[-1] // 2, 1) for c in turned}
            n = 0
            for a, b in pairs:
                sums[n] = sums[n] + v[a] * v[b]
                n += 1
                if a != b:
                    sums[n] = sums[n] + v[a] * t[b]
                    n += 1
        return tuple(sums)

    if sums is None:
        count = sum(1 if a == b else 2 for a, b in pairs)
        width = load(used[0], 0).shape[-1]
        sums = tuple(jnp.zeros((8, width), F32) for _ in range(count))
    return lax.fori_loop(0, chunks // unroll, chunk, sums)


def store_sums(acc_ref, pairs, sums, base):
    ncol = 2 * (POWERS + 1)
    width = acc_ref.shape[1]
    sign = jnp.where(lax.broadcasted_iota(jnp.int32, (8, width), 1) < width // 2, 1.0, -1.0)
    n = 0
    for a, b in pairs:
        acc_ref[pl.ds(base + a * ncol + b, 1), :] = jnp.sum(sums[n], axis=0, keepdims=True)
        n += 1
        if a != b:
            acc_ref[pl.ds(base + b * ncol + a, 1), :] = jnp.sum(sums[n] * sign, axis=0, keepdims=True)
            n += 1


def inside_body(nz, scal, first_ref, keep_ref, send_ref, acc_ref):
    npow = keep_ref.shape[0] + 1
    size = keep_ref.shape[1]
    pairs = [(a, b) for a in range(npow) for b in range(npow) if a <= b]
    sums = None
    for ref, where in ((keep_ref, scal[1]), (send_ref, 1 - scal[1])):

        def load(c, at, ref=ref, where=where):
            if c == 0:
                return first_ref[pl.ds(pl.multiple_of(scal[0] * nz + where * size + at, 8), 8), :]
            return ref[c - 1, pl.ds(pl.multiple_of(at, 8), 8), :]

        sums = product_sums(load, size // 8, pairs, 32, sums)
    acc_ref[...] = jnp.zeros_like(acc_ref)
    store_sums(acc_ref, pairs, sums, scal[1] * (npow * (2 * npow + 1)))


def gram_body(scal, packets_ref, keep_ref, recv_ref, part_ref, cols_ref, gram_ref, acc_ref):
    core = scal[1]
    ncol, size, width = cols_ref.shape
    npow = ncol // 2
    cols_ref[0] = packets_ref[0]
    cols_ref[npow] = packets_ref[1]
    for k in range(npow - 1):
        cols_ref[core * npow + 1 + k] = keep_ref[k]
        cols_ref[(1 - core) * npow + 1 + k] = recv_ref[k]
    acc_ref[...] = part_ref[...]
    first, second = list(range(npow)), list(range(npow, ncol))
    for some in (second[:3], second[3:]):
        pairs = [(a, b) for a in first for b in some]
        sums = product_sums(
            lambda c, at: cols_ref[c, pl.ds(pl.multiple_of(at, 8), 8), :], size // 8, pairs, 32, None
        )
        store_sums(acc_ref, pairs, sums, 0)
    row = jnp.sum(acc_ref[...].T, axis=0, keepdims=True)
    gram_ref[...] = jnp.broadcast_to(row[None], gram_ref.shape)


def basis_body(cells, rows, gram_ref, cols_ref, basis_ref, factor_ref, coef_ref, out_ref, sems):
    ncol, size, width = cols_ref.shape
    half = width // 2
    row = jnp.sum(gram_ref[...], axis=0) * (1.0 / cells)
    r = lax.broadcasted_iota(jnp.int32, (16, width), 0)
    c = lax.broadcasted_iota(jnp.int32, (16, width), 1)
    packed = jnp.zeros((16, width), F32)
    for j in range(ncol):
        moved = row if j == 0 else pltpu.roll(row, width - ncol * j, 1)
        packed = jnp.where(r == j, moved, packed)
    turned = jnp.concatenate([packed, jnp.zeros((width - 16, width), F32)], axis=0).T[:16]
    inside = (r < ncol) & (c < ncol)
    re = jnp.where(inside, jnp.where(r <= c, packed, turned), 0.0)
    im = jnp.where(inside & (r != c), jnp.where(r < c, turned, -packed), 0.0)
    re = jnp.where(c == r + 16, 1.0, re)
    up_re = jnp.zeros((16, width), F32)
    up_im = jnp.zeros((16, width), F32)
    for j in range(ncol):
        pivot = jnp.sqrt(re[j : j + 1, j : j + 1])
        inverse = 1.0 / pivot
        row_re = re[j : j + 1, :] * inverse
        row_im = im[j : j + 1, :] * inverse
        col_re = re[:, j : j + 1] * inverse
        col_im = im[:, j : j + 1] * inverse
        up_re = jnp.where(r == j, row_re, up_re)
        up_im = jnp.where(r == j, row_im, up_im)
        below = r > j
        re = re - jnp.where(below, col_re * row_re - col_im * row_im, 0.0)
        im = im - jnp.where(below, col_re * row_im + col_im * row_re, 0.0)
    for q, up in ((0, jnp.where(c >= r, up_re, 0.0)), (1, jnp.where(c > r, up_im, 0.0))):
        for k in range(ncol):
            factor_ref[k, q : q + 1, :] = up[k : k + 1, :ncol]
    sign = jnp.where(lax.broadcasted_iota(jnp.int32, (8, width), 1) < half, 1.0, -1.0)
    for k in range(ncol):
        for i in range(k + 1):
            coef_ref[0, k * ncol + i] = jnp.broadcast_to(up_re[k : k + 1, 16 + i : 17 + i], (8, width))
            coef_ref[1, k * ncol + i] = (
                jnp.broadcast_to(up_im[k : k + 1, 16 + i : 17 + i], (8, width)) * sign
            )
    group = 4
    each = size // rows

    def row(r, carry):
        for start in range(0, each, 8 * group):
            slots = [pl.ds(pl.multiple_of(r * each + start + 8 * g, 8), 8) for g in range(group)]
            v = [[cols_ref[i, s, :] for s in slots] for i in range(ncol)]
            t = [[pltpu.roll(x, half, 1) for x in xs] for xs in v]
            for k in range(ncol):
                total = [None] * group
                for i in range(k + 1):
                    re = coef_ref[0, k * ncol + i]
                    im = coef_ref[1, k * ncol + i]
                    for g in range(group):
                        term = re * v[i][g]
                        if i < k:
                            term = term + im * t[i][g]
                        total[g] = term if total[g] is None else total[g] + term
                for g in range(group):
                    out_ref[k, slots[g], :] = total[g]
        copy(r).start()
        return carry

    def copy(r):
        part = pl.ds(pl.multiple_of(r * each, 8), each)
        return pltpu.make_async_copy(out_ref.at[:, part, :], basis_ref.at[:, part, :], sems.at[r])

    lax.fori_loop(0, rows, row, 0)
    for r in range(rows):
        copy(r).wait()


def shards(packets, kinetic_x, kinetic_y, element_kinetic, potential):
    npack, rows, nz, width = packets.shape
    trans = lax.axis_size("trans")
    nx = rows * trans
    ncol = npack * (POWERS + 1)
    me = lax.axis_index("trans")
    core = me % 2
    chip = 2 * rows
    scal = jnp.stack([(me // 2) * chip, core, lax.axis_index("beam")]).astype(jnp.int32)

    size = rows * nz
    flat = packets.reshape(npack, size, width)
    mine = potential.reshape(size, width)
    pot = lax.all_gather(mine, "trans", axis=0, tiled=True)
    sent = pl.pallas_call(
        copies_body,
        out_shape=jax.ShapeDtypeStruct((trans, size, width), F32),
        in_specs=[vm()],
        out_specs=pl.BlockSpec(memory_space=pl.ANY),
        scratch_shapes=[pltpu.SemaphoreType.DMA((trans // npack,))],
        compiler_params=pltpu.CompilerParams(vmem_limit_bytes=LIMIT),
        name="copies",
    )(flat)
    cur = lax.all_to_all(sent, "trans", 0, 0, tiled=True).reshape(nx * nz, width)
    sent, flat_late, mine_late, ek_late = lax.optimization_barrier(
        (sent, flat, mine, element_kinetic)
    )

    def half_wide(*shape):
        return pltpu.VMEM(shape, BF16)

    square, column = half_wide(4 * nz, 4 * nz), in_vmem(nz, width)
    across = half_wide(4 * nx, 4 * nx)
    wide = half_wide(2 * width, 2 * width)
    rcol, kvec, mvec, coef = call(
        "vectors", vectors_body, [column, column, column, in_vmem(8, width)], ek_late, scal=scal, cost=1
    )

    plane = in_vmem(npack * rows, width)
    first, bridge, zrest, brest = call(
        "planes", functools.partial(planes_body, nz), [plane] * 4,
        flat_late, mine_late, rcol, kvec, mvec, cost=1,
    )
    pin, bin_ = passed(first, -1), passed(bridge, 1)
    pnext, bnext = call(
        "edges", functools.partial(edges_body, 1.0), [plane] * 2, zrest, brest, pin, bin_, coef, cost=1
    )
    planes = jnp.stack([pin, bin_, passed(pnext, -1), passed(bnext, 1)])
    planes = lax.all_gather(planes, "trans")

    full, edge = in_vmem(nx * (nz + PAD), width), in_vmem(nx, width)
    here = in_vmem(chip * nz, width)
    col1, col2, first, bridge, rows1, rows2, pot, kz2, kx2, wy2, kx4, rcol, coef = call(
        "pair", functools.partial(pair_body, nx, nz, width, chip),
        [full, full, edge, edge, here, here, in_vmem(nx * nz, width),
         square, across, wide, half_wide(4 * chip, 4 * nx), column, in_vmem(8, width)],
        cur, planes, pot, kinetic_x, kinetic_y, element_kinetic,
        scal=scal, cost=8, away=(2, 3, 4, 5),
        scratch=[full, in_vmem(4, nx, width), in_vmem(2, nx, width), pltpu.SemaphoreType.DMA((5,)),
                 in_vmem(*kinetic_x.shape), in_vmem(*kinetic_y.shape), in_vmem(*element_kinetic.shape),
                 square, across, wide, in_vmem(width, width)],
    )
    pin, bin_ = passed(first, -1), passed(bridge, 1)
    col3, first, bridge = call(
        "third", functools.partial(third_body, nx, nz, width), [full, edge, edge],
        col2, col1, pot, kz2, kx2, wy2, rcol,
    )
    first, bridge = call(
        "edges", functools.partial(edges_body, 2.0), [edge] * 2, first, bridge, pin, bin_, coef, cost=1
    )
    plast, blast = passed(first, -1), passed(bridge, 1)
    local, rows3 = call(
        "fourth", functools.partial(fourth_body, nx, nz, width, chip),
        [in_vmem(chip * (nz + PAD), width), here],
        col3, pin, bin_, col2, pot, kz2, kx4, wy2, rcol,
        scal=scal, scratch=[full], cost=2,
    )
    columns = [rows1, rows2, rows3]
    keep, send = pl.pallas_call(
        functools.partial(finish_body, nz, rows),
        out_shape=[in_vmem(POWERS, size, width)] * 2,
        in_specs=[pl.BlockSpec(memory_space=pltpu.SMEM)] + [vm()] * (4 + POWERS - 1),
        out_specs=[vm()] * 2,
        compiler_params=pltpu.CompilerParams(vmem_limit_bytes=LIMIT),
        name="finish",
    )(scal, local, plast, blast, rcol, *columns)
    recv = lax.ppermute(send, "trans", [(i, i ^ 1) for i in range(trans)])
    (part,) = call(
        "inside", functools.partial(inside_body, nz), [in_vmem(128, width)], cur, keep, send,
        scal=scal, cost=1,
    )
    cols, gram = call(
        "gram", gram_body, [in_vmem(ncol, size, width), in_vmem(trans, 1, width)],
        flat, keep, recv, part, scal=scal, scratch=[in_vmem(128, width)], cost=1,
    )
    beam = lax.axis_size("beam")
    gram = jnp.sum(lax.all_to_all(gram, "trans", 0, 0, tiled=True), axis=0, keepdims=True)
    gram = lax.all_to_all(jnp.broadcast_to(gram, (beam, 1, width)), "beam", 0, 0, tiled=True)
    cells = float(nx * (width // 2) * nz * beam)
    basis, factor = pl.pallas_call(
        functools.partial(basis_body, cells, rows),
        out_shape=[
            jax.ShapeDtypeStruct((ncol, size, width), F32),
            jax.ShapeDtypeStruct((ncol, 2, ncol), F32),
        ],
        in_specs=[vm(), vm()],
        out_specs=[pl.BlockSpec(memory_space=pl.ANY), vm()],
        scratch_shapes=[
            pltpu.VMEM((2, ncol * ncol, 8, width), F32),
            pltpu.VMEM((ncol, size, width), F32),
            pltpu.SemaphoreType.DMA((rows,)),
        ],
        compiler_params=pltpu.CompilerParams(vmem_limit_bytes=LIMIT),
        name="basis",
    )(gram, cols)
    return basis.reshape(ncol, rows, nz, width), factor.transpose(1, 0, 2)


def solution(mesh):
    in_specs = (P(None, "trans", "beam", None), P(), P(), P(), P("trans", "beam", None))
    out_specs = (P(None, "trans", "beam", None), P())
    return jax.shard_map(shards, mesh=mesh, in_specs=in_specs, out_specs=out_specs, check_vma=False)
```

```python
import functools

import jax
import jax.numpy as jnp
from jax import lax
from jax.experimental import pallas as pl
from jax.experimental.pallas import tpu as pltpu
from jax.sharding import PartitionSpec as P

POWERS = 4
F32 = jnp.float32
BF16 = jnp.bfloat16
LIMIT = 16 * 1024 * 1024


def split(v):
    high = v.astype(BF16)
    return high, (v - high.astype(F32)).astype(BF16)


def passed(x, by):
    peers = lax.axis_size("beam")
    return lax.ppermute(x, "beam", [(i, i + by) for i in range(peers) if 0 <= i + by < peers])


PAD = 8


def apply_local(nx, nz, width, refs, col, load, prev, halo, scale, out, bridge_ref, ready=None):
    pot_ref, kz_ref, kx_ref, wy_ref, wvec_ref = refs
    col_ref, stride = col
    out_ref, x_start, out_x = out
    out_stride = nz + PAD
    half = width // 2
    left = lax.broadcasted_iota(jnp.int32, (nz, width), 1) < half

    def product(k_ref, us):
        parts = [split(u) for u in us]
        rows = []
        for p, q in (parts[0:2], parts[2:4]):
            rows += [jnp.concatenate([p[0], q[0]], axis=1), jnp.concatenate([p[1], q[1]], axis=1)]
        got = jnp.dot(k_ref[...], jnp.concatenate(rows, axis=0), preferred_element_type=F32)
        m = got.shape[0] // 4
        outs = []
        for i in range(2):
            both = got[2 * i * m : (2 * i + 1) * m] + got[(2 * i + 1) * m : (2 * i + 2) * m]
            outs += [both[:, :width], both[:, width:]]
        return outs, parts

    def local_four(x0):
        us = [load(x_start + x0 + q) for q in range(4)]
        along_z, parts = product(kz_ref, us)
        along_y = jnp.dot(
            jnp.concatenate([jnp.concatenate(p, axis=1) for p in parts], axis=0),
            wy_ref[...],
            preferred_element_type=F32,
        )
        for q in range(4):
            x = x_start + x0 + q
            ay = along_y[q * nz : (q + 1) * nz]
            new = along_z[q] + ay[:, :width] + ay[:, width:]
            new = new + scale * optical(us[q], pot_ref[rows_of(x, nz, nz), :], left)
            if prev is not None:
                new = new - prev[0][rows_of(x, prev[1], nz), :]
            if halo is not None:
                new = with_halo(new, halo, x)
            out_ref[rows_of(x0 + q, out_stride, nz), :] = new

    if ready is None:
        repeat(out_x // 4, 8, only(lambda i: local_four(i * 4)), 0)
    else:
        for h in range(2):
            ready(h)
            repeat(out_x // 8, 8, only(lambda i, h=h: local_four((h * out_x // 8 + i) * 4)), 0)

    def across_four(i, bridge):
        z0 = i * 4
        us = [col_ref[pl.ds(z0 + q, nx, stride=stride), :] for q in range(4)]
        along_x, _ = product(kx_ref, us)
        for q in range(4):
            at = pl.ds(z0 + q, out_x, stride=out_stride)
            new = out_ref[at, :] + along_x[q]
            out_ref[at, :] = new
            if bridge_ref is not None:
                bridge = bridge + wvec_ref[pl.ds(z0 + q, 1), :] * new
        return bridge

    bridge = repeat(nz // 4, 8, across_four, jnp.zeros((out_x, width), F32))
    if bridge_ref is not None:
        bridge_ref[...] = bridge


def rows_of(x, stride, nz):
    return pl.ds(pl.multiple_of(x * stride, 8), nz)


def optical(u, pot, left):
    half = u.shape[-1] // 2
    turned = pltpu.roll(pot, half, 1)
    return jnp.where(left, pot, turned) * u + jnp.where(left, turned, -pot) * pltpu.roll(u, half, 1)


def with_halo(u, halo, x):
    column_ref, plane_ref, sum_ref, scale = halo
    top = lax.broadcasted_iota(jnp.int32, (8, u.shape[-1]), 0) == 0
    u = u + column_ref[...] * (scale * plane_ref[pl.ds(x, 1), :])
    head = u[0:8] + jnp.where(top, scale * sum_ref[pl.ds(x, 1), :], 0.0)
    return jnp.concatenate([head, u[8:]], axis=0)


def repeat(count, unroll, body, carry):
    unroll = min(unroll, count)

    def some(i, carry):
        for q in range(unroll):
            carry = body(i * unroll + q, carry)
        return carry

    return lax.fori_loop(0, count // unroll, some, carry)


def only(body):
    def with_carry(i, carry):
        body(i)
        return carry

    return with_carry


def copies_body(packets_ref, sent_ref, sems):
    npack = packets_ref.shape[0]
    copies = [
        pltpu.make_async_copy(packets_ref, sent_ref.at[pl.ds(i * npack, npack)], sems.at[i])
        for i in range(sent_ref.shape[0] // npack)
    ]
    for copy in copies:
        copy.start()
    for copy in copies:
        copy.wait()


def planes_body(nz, packets_ref, pot_ref, wvec_ref, kvec_ref, mvec_ref, first_ref, bridge_ref, zrest_ref, brest_ref):
    npack, size, width = packets_ref.shape
    rows = size // nz
    left = lax.broadcasted_iota(jnp.int32, (nz, width), 1) < width // 2
    for p in range(npack):
        for x in range(rows):
            u = packets_ref[p, x * nz : (x + 1) * nz, :]
            v = optical(u, pot_ref[x * nz : (x + 1) * nz, :], left)
            at = slice(p * rows + x, p * rows + x + 1)
            first_ref[at, :] = u[0:1]
            bridge_ref[at, :] = jnp.sum(wvec_ref[...] * u, axis=0, keepdims=True)
            zrest_ref[at, :] = v[0:1] + jnp.sum(kvec_ref[...] * u, axis=0, keepdims=True)
            brest_ref[at, :] = jnp.sum(wvec_ref[...] * v + mvec_ref[...] * u, axis=0, keepdims=True)


def element_matrix(scal, ek):
    nz = ek.shape[0] - 1
    r = lax.broadcasted_iota(jnp.int32, (nz, nz), 0)
    c = lax.broadcasted_iota(jnp.int32, (nz, nz), 1)
    corner = (r == 0) & (c == 0) & (scal[2] > 0)
    return ek[0:nz, 0:nz] + jnp.where(corner, ek[nz : nz + 1, nz : nz + 1], 0.0)


def vectors_body(scal, ek_ref, rcol, kvec, mvec, coef):
    nz, width = rcol.shape
    kz = element_matrix(scal, ek_ref)
    edge_vectors(ek_ref, rcol, coef)
    kvec[...] = jnp.broadcast_to(kz[:, 0:1], (nz, width))
    bridge = ek_ref[nz : nz + 1, 0:nz]
    mvec[...] = jnp.broadcast_to(jnp.sum(kz * bridge, axis=1, keepdims=True), (nz, width))


def edge_vectors(ek_ref, rcol, coef):
    nz, width = rcol.shape
    rcol[...] = jnp.broadcast_to(ek_ref[0:nz, nz : nz + 1], (nz, width))
    coef[...] = jnp.zeros_like(coef)
    coef[0:1, :] = rcol[0:1, :]
    coef[1:2, :] = jnp.sum(rcol[...] * rcol[...], axis=0, keepdims=True)


def matrices(scal, kx_ref, ky_ref, ek_ref, kz1, kx1, wy1, kz2, kx2, wy2, kx4, kyd):
    chip = kx4.shape[0] // 4

    def split_wide(k):
        high = k.astype(BF16).astype(F32)
        return high, k - high

    def left_weights(k):
        high, low = split_wide(k)
        none = jnp.zeros_like(high)
        block = jnp.concatenate(
            [jnp.concatenate([high, high], axis=1), jnp.concatenate([low, none], axis=1)], axis=0
        )
        none = jnp.zeros_like(block)
        return jnp.concatenate(
            [jnp.concatenate([block, none], axis=1), jnp.concatenate([none, block], axis=1)], axis=0
        )

    for one, two, k in ((kz1, kz2, element_matrix(scal, ek_ref)), (kx1, kx2, kx_ref[...])):
        block = left_weights(k)
        one[...] = block.astype(BF16)
        two[...] = (2.0 * block).astype(BF16)
    kx4[...] = left_weights(2.0 * kx_ref[pl.ds(pl.multiple_of(scal[0], 8), chip), :]).astype(BF16)
    ky = ky_ref[...]
    none = jnp.zeros_like(ky)
    ky = jnp.concatenate(
        [jnp.concatenate([ky, none], axis=1), jnp.concatenate([none, ky], axis=1)], axis=0
    )
    kyd[...] = ky
    high, low = split_wide(ky)
    block = jnp.concatenate(
        [jnp.concatenate([high, low], axis=1), jnp.concatenate([high, jnp.zeros_like(low)], axis=1)],
        axis=0,
    )
    wy1[...] = block.astype(BF16)
    wy2[...] = (2.0 * block).astype(BF16)


def edges_body(scale, first_ref, bridge_ref, pin_ref, bin_ref, coef_ref, out_first, out_bridge):
    head, square = coef_ref[0:1, :], coef_ref[1:2, :]
    pin, bin_ = scale * pin_ref[...], scale * bin_ref[...]
    out_first[...] = first_ref[...] + head * pin + bin_
    out_bridge[...] = bridge_ref[...] + square * pin + head * bin_


def pair_body(nx, nz, width, chip, scal, cur_ref, gathered_ref, pot_hbm, kx_hbm, ky_hbm, ek_hbm, *refs):
    one_ref, two_ref, first_ref, bridge_ref, rows1_ref, rows2_ref, pot_ref = refs[:7]
    kz2, kx2, wy2, kx4, rcol, coef = refs[7:13]
    col_ref, planes_ref, halo_ref, sems, kx_ref, ky_raw, ek_ref, kz1, kx1, wy1, ky_ref = refs[13:]
    stride = nz + PAD
    small = [
        pltpu.make_async_copy(src, dst, sems.at[2 + i])
        for i, (src, dst) in enumerate(((kx_hbm, kx_ref), (ky_hbm, ky_raw), (ek_hbm, ek_ref)))
    ]
    for copy in small:
        copy.start()
    part = nx * nz // 2
    copies = [
        pltpu.make_async_copy(
            pot_hbm.at[pl.ds(h * part, part), :], pot_ref.at[pl.ds(h * part, part), :], sems.at[h]
        )
        for h in range(2)
    ]
    for copy in copies:
        copy.start()

    trans, planes, each, _ = gathered_ref.shape
    each = each // 2
    for t in range(trans):
        for q in range(planes):
            planes_ref[q, t * each : (t + 1) * each, :] = gathered_ref[
                t, q, pl.ds(pl.multiple_of(scal[1] * each, 8), each), :
            ]
    for copy in small:
        copy.wait()
    matrices(scal, kx_ref, ky_raw, ek_ref, kz1, kx1, wy1, kz2, kx2, wy2, kx4, ky_ref)
    edge_vectors(ek_ref, rcol, coef)
    precise = lax.Precision.HIGHEST
    for q in range(2):
        plane = planes_ref[q]
        moved = jnp.dot(kx_ref[...], plane, precision=precise, preferred_element_type=F32)
        moved = moved + jnp.dot(plane, ky_ref[...], precision=precise, preferred_element_type=F32)
        halo_ref[q] = moved + planes_ref[2 + q]

    def packed(x):
        u = cur_ref[rows_of(x, nz, nz), :]
        col_ref[rows_of(x, stride, nz), :] = u
        return u

    apply_local(
        nx, nz, width, (pot_ref, kz1, kx1, wy1, rcol), (col_ref, stride), packed, None,
        (rcol, planes_ref.at[0], planes_ref.at[1], 1.0), 1.0, (one_ref, 0, nx), None,
        ready=lambda h: copies[h].wait(),
    )
    apply_local(
        nx, nz, width, (pot_ref, kz2, kx2, wy2, rcol), (one_ref, stride),
        lambda x: one_ref[rows_of(x, stride, nz), :], (cur_ref, nz),
        (rcol, halo_ref.at[0], halo_ref.at[1], 2.0), 2.0, (two_ref, 0, nx), bridge_ref,
    )
    first_ref[...] = two_ref[pl.ds(0, nx, stride=stride), :]
    for ref, rows_ref in ((one_ref, rows1_ref), (two_ref, rows2_ref)):
        for q in range(chip):
            rows_ref[q * nz : (q + 1) * nz, :] = ref[rows_of(scal[0] + q, stride, nz), :]


def third_body(nx, nz, width, cur_ref, prev_ref, pot_ref, kz, kx, wy, rcol, out_ref, first_ref, bridge_ref):
    stride = nz + PAD
    apply_local(
        nx, nz, width, (pot_ref, kz, kx, wy, rcol), (cur_ref, stride),
        lambda x: cur_ref[rows_of(x, stride, nz), :], (prev_ref, stride), None, 2.0,
        (out_ref, 0, nx), bridge_ref,
    )
    first_ref[...] = out_ref[pl.ds(0, nx, stride=stride), :]


def fourth_body(nx, nz, width, chip, scal, cur_ref, pin_ref, bin_ref, prev_ref, pot_ref, *refs):
    kz, kx, wy, rcol, out_ref, rows_ref, col_ref = refs
    stride = nz + PAD

    def complete(x):
        u = with_halo(cur_ref[rows_of(x, stride, nz), :], (rcol, pin_ref, bin_ref, 2.0), x)
        col_ref[rows_of(x, stride, nz), :] = u

    repeat(nx, 16, only(complete), 0)
    for q in range(chip):
        rows_ref[q * nz : (q + 1) * nz, :] = col_ref[rows_of(scal[0] + q, stride, nz), :]
    apply_local(
        nx, nz, width, (pot_ref, kz, kx, wy, rcol), (col_ref, stride),
        lambda x: col_ref[rows_of(x, stride, nz), :], (prev_ref, stride), None, 2.0,
        (out_ref, scal[0], chip), None,
    )


def vm():
    return pl.BlockSpec(memory_space=pltpu.VMEM)


def in_vmem(*shape):
    return pltpu.VMEM(shape, F32)


def call(name, body, outs, *ins, scal=None, scratch=(), cost=4, away=()):
    specs = [pl.BlockSpec(memory_space=pltpu.HBM) if i in away else vm() for i in range(len(ins))]
    ins = tuple(
        pltpu.with_memory_space_constraint(x, pltpu.HBM) if i in away else x for i, x in enumerate(ins)
    )
    if scal is not None:
        specs = [pl.BlockSpec(memory_space=pltpu.SMEM)] + specs
        ins = (scal,) + ins
    return pl.pallas_call(
        body,
        out_shape=outs,
        in_specs=specs,
        out_specs=[vm()] * len(outs),
        scratch_shapes=list(scratch),
        compiler_params=pltpu.CompilerParams(vmem_limit_bytes=LIMIT),
        cost_estimate=pl.CostEstimate(
            flops=cost * 10**9, bytes_accessed=2 * cost * 10**6, transcendentals=0
        ),
        name=name,
    )(*ins)


def finish_body(nz, rows, scal, last_ref, pin_ref, bin_ref, rcol_ref, *refs):
    cols = refs[: POWERS - 1]
    keep_ref, send_ref = refs[POWERS - 1 :]
    core = scal[1]
    size = rows * nz
    halo = (rcol_ref, pin_ref, bin_ref, 2.0)
    for ref, where in ((keep_ref, core), (send_ref, 1 - core)):
        at = pl.ds(pl.multiple_of(where * size, size), size)
        for k in range(POWERS - 1):
            ref[k] = cols[k][at, :]
        for r in range(rows):
            x = where * rows + r
            u = with_halo(last_ref[rows_of(x, nz + PAD, nz), :], halo, scal[0] + x)
            ref[POWERS - 1, r * nz : (r + 1) * nz, :] = u


def product_sums(load, chunks, pairs, unroll, sums):
    used = sorted({c for pair in pairs for c in pair})
    turned = sorted({b for a, b in pairs if a != b})

    def chunk(i, sums):
        sums = list(sums)
        for q in range(unroll):
            v = {c: load(c, (i * unroll + q) * 8) for c in used}
            t = {c: pltpu.roll(v[c], v[c].shape[-1] // 2, 1) for c in turned}
            n = 0
            for a, b in pairs:
                sums[n] = sums[n] + v[a] * v[b]
                n += 1
                if a != b:
                    sums[n] = sums[n] + v[a] * t[b]
                    n += 1
        return tuple(sums)

    if sums is None:
        count = sum(1 if a == b else 2 for a, b in pairs)
        width = load(used[0], 0).shape[-1]
        sums = tuple(jnp.zeros((8, width), F32) for _ in range(count))
    return lax.fori_loop(0, chunks // unroll, chunk, sums)


def store_sums(acc_ref, pairs, sums, base):
    ncol = 2 * (POWERS + 1)
    width = acc_ref.shape[1]
    sign = jnp.where(lax.broadcasted_iota(jnp.int32, (8, width), 1) < width // 2, 1.0, -1.0)
    n = 0
    for a, b in pairs:
        acc_ref[pl.ds(base + a * ncol + b, 1), :] = jnp.sum(sums[n], axis=0, keepdims=True)
        n += 1
        if a != b:
            acc_ref[pl.ds(base + b * ncol + a, 1), :] = jnp.sum(sums[n] * sign, axis=0, keepdims=True)
            n += 1


def inside_body(nz, scal, first_ref, keep_ref, send_ref, acc_ref):
    npow = keep_ref.shape[0] + 1
    size = keep_ref.shape[1]
    pairs = [(a, b) for a in range(npow) for b in range(npow) if a <= b]
    sums = None
    for ref, where in ((keep_ref, scal[1]), (send_ref, 1 - scal[1])):

        def load(c, at, ref=ref, where=where):
            if c == 0:
                return first_ref[pl.ds(pl.multiple_of(scal[0] * nz + where * size + at, 8), 8), :]
            return ref[c - 1, pl.ds(pl.multiple_of(at, 8), 8), :]

        sums = product_sums(load, size // 8, pairs, 32, sums)
    acc_ref[...] = jnp.zeros_like(acc_ref)
    store_sums(acc_ref, pairs, sums, scal[1] * (npow * (2 * npow + 1)))


def gram_body(scal, packets_ref, keep_ref, recv_ref, part_ref, cols_ref, gram_ref, acc_ref):
    core = scal[1]
    ncol, size, width = cols_ref.shape
    npow = ncol // 2
    cols_ref[0] = packets_ref[0]
    cols_ref[npow] = packets_ref[1]
    for k in range(npow - 1):
        cols_ref[core * npow + 1 + k] = keep_ref[k]
        cols_ref[(1 - core) * npow + 1 + k] = recv_ref[k]
    acc_ref[...] = part_ref[...]
    first, second = list(range(npow)), list(range(npow, ncol))
    for some in (second[:3], second[3:]):
        pairs = [(a, b) for a in first for b in some]
        sums = product_sums(
            lambda c, at: cols_ref[c, pl.ds(pl.multiple_of(at, 8), 8), :], size // 8, pairs, 32, None
        )
        store_sums(acc_ref, pairs, sums, 0)
    row = jnp.sum(acc_ref[...].T, axis=0, keepdims=True)
    gram_ref[...] = jnp.broadcast_to(row[None], gram_ref.shape)


def basis_body(cells, rows, gram_ref, cols_ref, basis_ref, factor_ref, coef_ref, out_ref, sems):
    ncol, size, width = cols_ref.shape
    half = width // 2
    row = jnp.sum(gram_ref[...], axis=0) * (1.0 / cells)
    r = lax.broadcasted_iota(jnp.int32, (16, width), 0)
    c = lax.broadcasted_iota(jnp.int32, (16, width), 1)
    packed = jnp.zeros((16, width), F32)
    for j in range(ncol):
        moved = row if j == 0 else pltpu.roll(row, width - ncol * j, 1)
        packed = jnp.where(r == j, moved, packed)
    turned = jnp.concatenate([packed, jnp.zeros((width - 16, width), F32)], axis=0).T[:16]
    inside = (r < ncol) & (c < ncol)
    re = jnp.where(inside, jnp.where(r <= c, packed, turned), 0.0)
    im = jnp.where(inside & (r != c), jnp.where(r < c, turned, -packed), 0.0)
    re = jnp.where(c == r + 16, 1.0, re)
    up_re = jnp.zeros((16, width), F32)
    up_im = jnp.zeros((16, width), F32)
    for j in range(ncol):
        pivot = jnp.sqrt(re[j : j + 1, j : j + 1])
        inverse = 1.0 / pivot
        row_re = re[j : j + 1, :] * inverse
        row_im = im[j : j + 1, :] * inverse
        col_re = re[:, j : j + 1] * inverse
        col_im = im[:, j : j + 1] * inverse
        up_re = jnp.where(r == j, row_re, up_re)
        up_im = jnp.where(r == j, row_im, up_im)
        below = r > j
        re = re - jnp.where(below, col_re * row_re - col_im * row_im, 0.0)
        im = im - jnp.where(below, col_re * row_im + col_im * row_re, 0.0)
    for q, up in ((0, jnp.where(c >= r, up_re, 0.0)), (1, jnp.where(c > r, up_im, 0.0))):
        for k in range(ncol):
            factor_ref[k, q : q + 1, :] = up[k : k + 1, :ncol]
    sign = jnp.where(lax.broadcasted_iota(jnp.int32, (8, width), 1) < half, 1.0, -1.0)
    for k in range(ncol):
        for i in range(k + 1):
            coef_ref[0, k * ncol + i] = jnp.broadcast_to(up_re[k : k + 1, 16 + i : 17 + i], (8, width))
            coef_ref[1, k * ncol + i] = (
                jnp.broadcast_to(up_im[k : k + 1, 16 + i : 17 + i], (8, width)) * sign
            )
    group = 4
    each = size // rows

    def row(r, carry):
        for start in range(0, each, 8 * group):
            slots = [pl.ds(pl.multiple_of(r * each + start + 8 * g, 8), 8) for g in range(group)]
            v = [[cols_ref[i, s, :] for s in slots] for i in range(ncol)]
            t = [[pltpu.roll(x, half, 1) for x in xs] for xs in v]
            for k in range(ncol):
                total = [None] * group
                for i in range(k + 1):
                    re = coef_ref[0, k * ncol + i]
                    im = coef_ref[1, k * ncol + i]
                    for g in range(group):
                        term = re * v[i][g]
                        if i < k:
                            term = term + im * t[i][g]
                        total[g] = term if total[g] is None else total[g] + term
                for g in range(group):
                    out_ref[k, slots[g], :] = total[g]
        copy(r).start()
        return carry

    def copy(r):
        part = pl.ds(pl.multiple_of(r * each, 8), each)
        return pltpu.make_async_copy(out_ref.at[:, part, :], basis_ref.at[:, part, :], sems.at[r])

    lax.fori_loop(0, rows, row, 0)
    for r in range(rows):
        copy(r).wait()


def shards(packets, kinetic_x, kinetic_y, element_kinetic, potential):
    npack, rows, nz, width = packets.shape
    trans = lax.axis_size("trans")
    nx = rows * trans
    ncol = npack * (POWERS + 1)
    me = lax.axis_index("trans")
    core = me % 2
    chip = 2 * rows
    scal = jnp.stack([(me // 2) * chip, core, lax.axis_index("beam")]).astype(jnp.int32)

    size = rows * nz
    flat = packets.reshape(npack, size, width)
    mine = potential.reshape(size, width)
    pot = lax.all_gather(mine, "trans", axis=0, tiled=True)
    sent = pl.pallas_call(
        copies_body,
        out_shape=jax.ShapeDtypeStruct((trans, size, width), F32),
        in_specs=[vm()],
        out_specs=pl.BlockSpec(memory_space=pl.ANY),
        scratch_shapes=[pltpu.SemaphoreType.DMA((trans // npack,))],
        compiler_params=pltpu.CompilerParams(vmem_limit_bytes=LIMIT),
        name="copies",
    )(flat)
    cur = lax.all_to_all(sent, "trans", 0, 0, tiled=True).reshape(nx * nz, width)
    sent, flat_late, mine_late, ek_late = lax.optimization_barrier(
        (sent, flat, mine, element_kinetic)
    )

    def half_wide(*shape):
        return pltpu.VMEM(shape, BF16)

    square, column = half_wide(4 * nz, 4 * nz), in_vmem(nz, width)
    across = half_wide(4 * nx, 4 * nx)
    wide = half_wide(2 * width, 2 * width)
    rcol, kvec, mvec, coef = call(
        "vectors", vectors_body, [column, column, column, in_vmem(8, width)], ek_late, scal=scal, cost=1
    )

    plane = in_vmem(npack * rows, width)
    first, bridge, zrest, brest = call(
        "planes", functools.partial(planes_body, nz), [plane] * 4,
        flat_late, mine_late, rcol, kvec, mvec, cost=1,
    )
    pin, bin_ = passed(first, -1), passed(bridge, 1)
    pnext, bnext = call(
        "edges", functools.partial(edges_body, 1.0), [plane] * 2, zrest, brest, pin, bin_, coef, cost=1
    )
    planes = jnp.stack([pin, bin_, passed(pnext, -1), passed(bnext, 1)])
    planes = lax.all_gather(planes, "trans")

    full, edge = in_vmem(nx * (nz + PAD), width), in_vmem(nx, width)
    here = in_vmem(chip * nz, width)
    col1, col2, first, bridge, rows1, rows2, pot, kz2, kx2, wy2, kx4, rcol, coef = call(
        "pair", functools.partial(pair_body, nx, nz, width, chip),
        [full, full, edge, edge, here, here, in_vmem(nx * nz, width),
         square, across, wide, half_wide(4 * chip, 4 * nx), column, in_vmem(8, width)],
        cur, planes, pot, kinetic_x, kinetic_y, element_kinetic,
        scal=scal, cost=8, away=(2, 3, 4, 5),
        scratch=[full, in_vmem(4, nx, width), in_vmem(2, nx, width), pltpu.SemaphoreType.DMA((5,)),
                 in_vmem(*kinetic_x.shape), in_vmem(*kinetic_y.shape), in_vmem(*element_kinetic.shape),
                 square, across, wide, in_vmem(width, width)],
    )
    pin, bin_ = passed(first, -1), passed(bridge, 1)
    col3, first, bridge = call(
        "third", functools.partial(third_body, nx, nz, width), [full, edge, edge],
        col2, col1, pot, kz2, kx2, wy2, rcol,
    )
    first, bridge = call(
        "edges", functools.partial(edges_body, 2.0), [edge] * 2, first, bridge, pin, bin_, coef, cost=1
    )
    plast, blast = passed(first, -1), passed(bridge, 1)
    local, rows3 = call(
        "fourth", functools.partial(fourth_body, nx, nz, width, chip),
        [in_vmem(chip * (nz + PAD), width), here],
        col3, pin, bin_, col2, pot, kz2, kx4, wy2, rcol,
        scal=scal, scratch=[full], cost=2,
    )
    columns = [rows1, rows2, rows3]
    keep, send = pl.pallas_call(
        functools.partial(finish_body, nz, rows),
        out_shape=[in_vmem(POWERS, size, width)] * 2,
        in_specs=[pl.BlockSpec(memory_space=pltpu.SMEM)] + [vm()] * (4 + POWERS - 1),
        out_specs=[vm()] * 2,
        compiler_params=pltpu.CompilerParams(vmem_limit_bytes=LIMIT),
        name="finish",
    )(scal, local, plast, blast, rcol, *columns)
    recv = lax.ppermute(send, "trans", [(i, i ^ 1) for i in range(trans)])
    (part,) = call(
        "inside", functools.partial(inside_body, nz), [in_vmem(128, width)], cur, keep, send,
        scal=scal, cost=1,
    )
    cols, gram = call(
        "gram", gram_body, [in_vmem(ncol, size, width), in_vmem(lax.axis_size("beam"), 1, width)],
        flat, keep, recv, part, scal=scal, scratch=[in_vmem(128, width)], cost=1,
    )
    beam = lax.axis_size("beam")
    gram = jnp.sum(lax.all_to_all(gram, "beam", 0, 0, tiled=True), axis=0, keepdims=True)
    gram = lax.all_to_all(jnp.broadcast_to(gram, (trans, 1, width)), "trans", 0, 0, tiled=True)
    cells = float(nx * (width // 2) * nz * beam)
    basis, factor = pl.pallas_call(
        functools.partial(basis_body, cells, rows),
        out_shape=[
            jax.ShapeDtypeStruct((ncol, size, width), F32),
            jax.ShapeDtypeStruct((ncol, 2, ncol), F32),
        ],
        in_specs=[vm(), vm()],
        out_specs=[pl.BlockSpec(memory_space=pl.ANY), vm()],
        scratch_shapes=[
            pltpu.VMEM((2, ncol * ncol, 8, width), F32),
            pltpu.VMEM((ncol, size, width), F32),
            pltpu.SemaphoreType.DMA((rows,)),
        ],
        compiler_params=pltpu.CompilerParams(vmem_limit_bytes=LIMIT),
        name="basis",
    )(gram, cols)
    return basis.reshape(ncol, rows, nz, width), factor.transpose(1, 0, 2)


def solution(mesh):
    in_specs = (P(None, "trans", "beam", None), P(), P(), P(), P("trans", "beam", None))
    out_specs = (P(None, "trans", "beam", None), P())
    return jax.shard_map(shards, mesh=mesh, in_specs=in_specs, out_specs=out_specs, check_vma=False)
```
